256 devices in a mesh: ctx: 16 (over x, y), tp: 8 (over z), dp: 2 (over core).
Axes of the slice: x: 4, y: 4, z: 8, core: 2. Of those that a mesh axis runs over, the one named last changes fastest.
Arguments:
- projected: bfloat16 [3, 8192, 4096], P(None, ('dp', 'ctx'), 'tp'), parts along dimension 1, may hold values from -6 to 6
- short_taps: float32 [3, 7, 4096], P(None, None, 'tp'), may hold values from -2 to 2
- long_filter: float32 [4096, 4096], P('ctx', 'tp'), may hold values from -2 to 2, as said below
- skip_gain: float32 [4096], P('tp'), may hold values from -1 to 1
- w_out: bfloat16 [4096, 4096], P('tp'), may hold values from -0.125 to 0.125
Outputs:
- hyena_out: bfloat16 [8192, 4096], P(('dp', 'ctx'), 'tp'), parts along dimension 0
The draws below stay inside these ranges and needn't reach their ends.
There are 2 independent parts, one for each index of `dp`. The reference program is written for one: setup_inputs(seed, part) draws one part's arguments, and reference() takes and returns one part's arrays. A program takes and returns all parts, laid end to end along the dimension named above; an argument that names none is the same for every part. Nothing has to cross between parts.
Inputs may be any that keep to these rules, and one draw needn't show every extreme that they name: `long_filter`: taps of each channel's causal filter.
All inputs are finite; a program needn't handle non-finite values.
Results may differ from the reference program's by a relative error of at most 0.014.
Values may be sent and summed in bfloat16 or wider, within the bound.
No kernel may reach another device: no remote copies, remote signals or barrier semaphores. Data moves between devices by JAX's collectives and lax.ppermute only.
A program may use at most 64 MiB of HBM per device.

```python
import math
import jax
import jax.numpy as jnp
from jax import lax

D = 4096
TAPS = 7
SEQ = 4096


def draw_long_filter(key, part):
    key_noise = jax.random.fold_in(key, 11)
    key_rate = jax.random.fold_in(key, 12)
    key_kind = jax.random.fold_in(key, 13)
    fast_share = 0.5
    noise = jnp.clip(jax.random.normal(key_noise, (SEQ, D), jnp.float32), -5.0, 5.0)
    fast_mask = jax.random.bernoulli(key_kind, fast_share, (D,))
    unit_draw = jax.random.uniform(key_rate, (D,), jnp.float32)
    fast_rate = 1.0 / 50.0 * jnp.power(50.0 / 30.0, unit_draw)
    slow_rate = 0.1 / SEQ * jnp.power(20.0, unit_draw)
    rate_all = jnp.where(fast_mask, fast_rate, slow_rate)
    amplitude = jnp.sqrt(2.0 * rate_all + 1.0 / SEQ)
    positions = jnp.arange(SEQ, dtype=jnp.float32)[:, None]
    return (noise * amplitude[None, :] * jnp.exp(-rate_all[None, :] * positions)).astype(jnp.float32)


def strengthened(drawn, stream_key, source, target, shards_of, factor):
    def block_of(axis_at):
        return (jnp.arange(drawn.shape[axis_at]) // (drawn.shape[axis_at] // shards_of)).reshape((-1,) + (1,) * (drawn.ndim - 1 - axis_at))

    one_side = jax.random.permutation(stream_key, shards_of)[block_of(target)]
    far = (block_of(target) + shards_of // 2) % shards_of
    return jnp.where((block_of(source) == one_side) | (block_of(source) == far), factor * drawn, drawn)


def levels(own_key, shape, cuts, low, high):
    level = 1.0
    for axis_at, parts in cuts:
        steps = jax.random.uniform(jax.random.fold_in(jax.random.fold_in(own_key, 6), axis_at), (parts,), jnp.float32, low / len(cuts), high / len(cuts))
        level = level * jnp.repeat(jnp.exp(steps), shape[axis_at] // parts).reshape((-1,) + (1,) * (len(shape) - 1 - axis_at))
    return level


def centred(own_key, extent, scale, reach, pieces=(), kind=jnp.bfloat16):
    values = jax.random.normal(own_key, extent, jnp.float32) * scale
    if len(pieces) > 0:
        values = levels(own_key, extent, pieces, -0.22, 0.18) * values
    return jnp.clip(values, min=-reach, max=reach).astype(kind)


def gaussian_with(rng, dims, deviation, limit, cuts, heavy, kind=jnp.bfloat16):
    drawn = deviation * jax.random.normal(rng, dims, jnp.float32)
    if cuts:
        drawn = drawn * levels(rng, dims, cuts, -0.22, 0.18)
    return jnp.clip(strengthened(drawn, jax.random.fold_in(rng, 3), *heavy), -limit, limit).astype(kind)


def setup_inputs(seed: int = 0, part: int = 0) -> dict:
    arg_keys = jax.random.split(jax.random.key(seed), 6)
    part_splits = jax.random.split(jax.random.fold_in(arg_keys[5], part), 6)
    return {
        "projected": centred(part_splits[0], (3, SEQ, D), 1.0, 6.0, ((1, 16), (2, 8))),
        "short_taps": centred(arg_keys[1], (3, TAPS, D), TAPS ** -0.5, 2.0, ((2, 8),), jnp.float32),
        "long_filter": draw_long_filter(jax.random.fold_in(arg_keys[5], 71), part),
        "skip_gain": jnp.clip(jax.random.uniform(arg_keys[3], (D,), jnp.float32, -1.0, 1.0) * levels(arg_keys[3], (D,), ((0, 8),), -0.4, 0.0), -1.0, 1.0),
        "w_out": gaussian_with(arg_keys[4], (D, D), D ** -0.5, 0.125, ((0, 8),), (0, 1, 8, 2.0)),
    }


def featurize(inputs, taps):
    values = inputs.astype(jnp.float32)
    padded = jnp.pad(values, ((TAPS - 1, 0), (0, 0)))
    result = taps[0][None, :] * padded[TAPS - 1:TAPS - 1 + SEQ]
    for tap_index in range(1, TAPS):
        result = result + taps[tap_index][None, :] * padded[TAPS - 1 - tap_index:TAPS - 1 - tap_index + SEQ]
    return result


def reference(projected, short_taps, long_filter, skip_gain, w_out):
    query = featurize(projected[0], short_taps[0])
    keyed = featurize(projected[1], short_taps[1])
    valued = featurize(projected[2], short_taps[2])
    gated = keyed * valued
    block_width = math.gcd(D, 512)
    blocks = D // block_width
    span_len = 2 * SEQ

    def convolve(pair):
        gated_block, filter_block = pair
        spectrum = jnp.fft.rfft(gated_block, n=span_len, axis=0) * jnp.fft.rfft(filter_block, n=span_len, axis=0)
        return jnp.fft.irfft(spectrum, n=span_len, axis=0)[:SEQ].astype(gated_block.dtype)

    gated_blocks = gated.reshape(SEQ, blocks, block_width).transpose(1, 0, 2)
    filter_blocks = long_filter.reshape(SEQ, blocks, block_width).transpose(1, 0, 2)
    long_conv = lax.map(convolve, (gated_blocks, filter_blocks)).transpose(1, 0, 2).reshape(SEQ, D)
    mixed = (query * (long_conv + skip_gain[None, :] * gated)).astype(jnp.bfloat16)
    return jnp.dot(mixed, w_out, preferred_element_type=jnp.float32).astype(jnp.bfloat16)
```

```python
import math

import jax
import jax.numpy as jnp
import numpy as np
from jax import lax
from jax.experimental import pallas as pl
from jax.experimental.pallas import tpu as pltpu
from jax.sharding import PartitionSpec as P

TAPS = 7
BF16 = jnp.bfloat16
F32 = jnp.float32
VMEM_LIMIT = 50 * 1024 * 1024


def split_bf16(values):
    high = values.astype(BF16)
    return high, (values - high.astype(F32)).astype(BF16)


def lane_dft(width):
    turns = np.outer(np.arange(width), np.arange(width)) % width
    angle = 2.0 * np.pi * turns / width
    cos, sin = np.cos(angle), np.sin(angle)
    forward = np.block([[cos, -sin], [sin, cos]]).astype(np.float32)
    high = forward.astype(jnp.bfloat16)
    low = (forward - high.astype(np.float32)).astype(jnp.bfloat16)
    return np.stack([high, low]), np.stack([high.T.copy(), low.T.copy()])


def twiddles(blocks, width):
    angle = 2.0 * np.pi * np.outer(np.arange(blocks) + 0.5, np.arange(width)) / (2 * blocks * width)
    return np.stack([np.cos(angle), -np.sin(angle)]).astype(np.float32)[:, :, None, :]


def block_angle(s, k, blocks):
    return math.pi * ((s * (2 * k + 1)) % (4 * blocks)) / (2 * blocks)


def prep_kernel(projected_ref, filter_ref, out_ref):
    blocks, _, rows = out_ref.shape
    group = filter_ref.shape[1] // blocks
    for part in range(4):
        source = projected_ref[part] if part < 3 else filter_ref[...].astype(BF16)
        turned = source.T
        out_ref[:, part * group : (part + 1) * group, :] = turned.reshape(blocks, group, rows)


def over_blocks(values, k, blocks):
    even_c = even_s = odd_c = odd_s = None
    for s, value in enumerate(values):
        c, t = math.cos(block_angle(s, k, blocks)), math.sin(block_angle(s, k, blocks))
        if s == 0:
            even_c = value
            continue
        term_c, term_s = value * c, value * t
        if s % 2 == 0:
            even_c = even_c + term_c
            even_s = term_s if even_s is None else even_s + term_s
        else:
            odd_c = term_c if odd_c is None else odd_c + term_c
            odd_s = term_s if odd_s is None else odd_s + term_s
    return (even_c + odd_c, -(even_s + odd_s)), (even_c - odd_c, even_s - odd_s)


def store_split(ref_high, ref_low, rows, cols, value):
    high, low = split_bf16(value)
    ref_high[rows, cols] = high
    ref_low[rows, cols] = low


def dot3(high, low, table_ref):
    def dot(a, b):
        return jnp.dot(a, b, preferred_element_type=F32)

    return dot(high, table_ref[0]) + dot(low, table_ref[0]) + dot(high, table_ref[1])


def conv_kernel(recv_ref, taps_ref, fwd_ref, inv_ref, tw_ref, out_ref, query, gated, high, low, spec_h, spec_u):
    blocks, quad, width = recv_ref.shape
    group = quad // 4
    lane = lax.broadcasted_iota(jnp.int32, (group, width), 1)

    def tap(part, j):
        column = part * TAPS + j
        return taps_ref[:, column : column + 1]

    def shifted(now, before, amount):
        return jnp.where(lane < amount, pltpu.roll(before, amount, 1), pltpu.roll(now, amount, 1))

    zeros = jnp.zeros((group, width), F32)
    state = [[zeros] * 4 for _ in range(3)]
    for s in range(blocks):
        results = []
        for part in range(3):
            now = recv_ref[s, part * group : (part + 1) * group, :].astype(F32)
            one = shifted(now, state[part][0], 1)
            pair6 = tap(part, 6) * now
            pair4 = tap(part, 4) * now + tap(part, 5) * one + shifted(pair6, state[part][1], 2)
            pair2 = tap(part, 2) * now + tap(part, 3) * one + shifted(pair4, state[part][2], 2)
            pair0 = tap(part, 0) * now + tap(part, 1) * one + shifted(pair2, state[part][3], 2)
            state[part] = [now, pair6, pair4, pair2]
            results.append(pair0)
        query[s] = results[0]
        gated[s] = results[1] * results[2]

    def forward(load, spec):
        for c0 in range(0, group, 16):
            for l0 in range(0, width, 128):
                values = [load(s, slice(c0, c0 + 16), slice(l0, l0 + 128)) for s in range(blocks)]
                for k in range(blocks // 2):
                    for kk, (re, im) in zip((k, blocks - 1 - k), over_blocks(values, k, blocks)):
                        tr = tw_ref[0, kk, :, l0 : l0 + 128]
                        ti = tw_ref[1, kk, :, l0 : l0 + 128]
                        rows = slice(kk * group + c0, kk * group + c0 + 16)
                        store_split(high, low, rows, slice(l0, l0 + 128), re * tr - im * ti)
                        store_split(high, low, rows, slice(width + l0, width + l0 + 128), re * ti + im * tr)
        spec[...] = dot3(high[...], low[...], fwd_ref)

    forward(lambda s, c, p: recv_ref[s, 3 * group + c.start : 3 * group + c.stop, p].astype(F32), spec_h)
    forward(lambda s, c, p: gated[s, c, p], spec_u)

    hr, hi = spec_h[:, :width], spec_h[:, width:]
    ur, ui = spec_u[:, :width], spec_u[:, width:]
    store_split(high, low, slice(None), slice(0, width), hr * ur - hi * ui)
    store_split(high, low, slice(None), slice(width, 2 * width), hr * ui + hi * ur)
    spec_h[...] = dot3(high[...], low[...], inv_ref)

    scale = 1.0 / (blocks * width)
    for c0 in range(0, group, 16):
        for l0 in range(0, width, 128):
            reals, imags = [], []
            for k in range(blocks):
                rows = slice(k * group + c0, k * group + c0 + 16)
                tr = tw_ref[0, k, :, l0 : l0 + 128] * scale
                ti = tw_ref[1, k, :, l0 : l0 + 128] * scale
                re = spec_h[rows, l0 : l0 + 128]
                im = spec_h[rows, width + l0 : width + l0 + 128]
                reals.append(re * tr + im * ti)
                imags.append(im * tr - re * ti)
            half = blocks // 2
            sum_re = [reals[k] + reals[blocks - 1 - k] for k in range(half)]
            dif_re = [reals[k] - reals[blocks - 1 - k] for k in range(half)]
            sum_im = [imags[k] + imags[blocks - 1 - k] for k in range(half)]
            dif_im = [imags[k] - imags[blocks - 1 - k] for k in range(half)]
            skip = taps_ref[c0 : c0 + 16, 3 * TAPS : 3 * TAPS + 1]
            for s in range(blocks):
                res, ims = (sum_re, dif_im) if s % 2 == 0 else (dif_re, sum_im)
                total = None
                for k in range(half):
                    angle = block_angle(s, k, blocks)
                    if s == 0:
                        term = res[k]
                    else:
                        term = res[k] * math.cos(angle) - ims[k] * math.sin(angle)
                    total = term if total is None else total + term
                at = (s, slice(c0, c0 + 16), slice(l0, l0 + 128))
                mixed = (query[at] * (total + skip * gated[at])).astype(BF16)
                out_ref[(0, *at)] = mixed
                out_ref[(1, *at)] = mixed


def project_kernel(place_ref, mixed_ref, own_ref, other_ref, out_ref):
    mine = place_ref[0]
    depth = own_ref.shape[0]
    rows = mixed_ref.shape[-1]

    def dot(part, table):
        return lax.dot_general(part, table, (((0,), (0,)), ((), ())), preferred_element_type=F32)

    first = mixed_ref[mine].reshape(depth, rows)
    second = mixed_ref[1 - mine].reshape(depth, rows)
    total = dot(first, own_ref[...]) + dot(second, other_ref[...])
    out_ref[0] = total.astype(BF16)


def local(projected, short_taps, long_filter, skip_gain, w_out):
    ctx, tp, dp = lax.axis_size("ctx"), lax.axis_size("tp"), lax.axis_size("dp")
    rows, width = projected.shape[1:]
    group = width // ctx
    me_ctx, me_tp, me_dp = lax.axis_index("ctx"), lax.axis_index("tp"), lax.axis_index("dp")

    def partner(z, d):
        first = d + (z - d) % tp // 2 * 2
        return (first + (1 - (z - d) % tp % 2)) % tp

    pair_route = [(z * dp + d, partner(z, d) * dp + d) for z in range(tp) for d in range(dp)]
    pair_groups = [
        [(c * tp + (first + d + b) % tp) * dp + d for b in range(2) for c in range(ctx)]
        for d in range(dp)
        for first in range(0, tp, 2)
    ]
    parity_groups = [list(range(odd, tp, 2)) for odd in range(2)]
    chunks = tp // 2
    parity = me_tp % 2
    place = (me_tp - me_dp) % tp % 2

    w_view = w_out.reshape(width, chunks, 2, width)
    w_send = lax.dynamic_index_in_dim(w_view, 1 - parity, 2, keepdims=False).reshape(width, chunks * width)
    w_other = lax.ppermute(w_send, ("tp", "dp"), pair_route)

    send = pl.pallas_call(
        prep_kernel,
        out_shape=jax.ShapeDtypeStruct((ctx, 4 * group, rows), BF16),
        compiler_params=pltpu.CompilerParams(vmem_limit_bytes=VMEM_LIMIT),
        name="prep",
    )(projected, long_filter)
    recv = lax.all_to_all(send, "ctx", 0, 0, tiled=True)

    table = jnp.concatenate([short_taps.reshape(3 * TAPS, width), skip_gain[None, :]], axis=0)
    table = lax.dynamic_slice_in_dim(table, me_ctx * group, group, axis=1).T
    fwd, inv = lane_dft(rows)
    mixed = pl.pallas_call(
        conv_kernel,
        out_shape=jax.ShapeDtypeStruct((2, ctx, group, rows), BF16),
        scratch_shapes=[
            pltpu.VMEM((ctx, group, rows), F32),
            pltpu.VMEM((ctx, group, rows), F32),
            pltpu.VMEM((ctx * group, 2 * rows), BF16),
            pltpu.VMEM((ctx * group, 2 * rows), BF16),
            pltpu.VMEM((ctx * group, 2 * rows), F32),
            pltpu.VMEM((ctx * group, 2 * rows), F32),
        ],
        compiler_params=pltpu.CompilerParams(vmem_limit_bytes=VMEM_LIMIT),
        name="conv",
    )(recv, table, jnp.asarray(fwd), jnp.asarray(inv), jnp.asarray(twiddles(ctx, rows)))
    mixed = lax.all_to_all(
        mixed.reshape(2 * ctx, group, rows), ("ctx", "tp", "dp"), 0, 0, tiled=True, axis_index_groups=pair_groups
    ).reshape(2, ctx, group, rows)

    partial = pl.pallas_call(
        project_kernel,
        grid_spec=pltpu.PrefetchScalarGridSpec(
            num_scalar_prefetch=1,
            grid=(chunks,),
            in_specs=[
                pl.BlockSpec((2, ctx, group, rows), lambda i, p: (0, 0, 0, 0)),
                pl.BlockSpec((width, width), lambda i, p: (0, 2 * i + p[1])),
                pl.BlockSpec((width, width), lambda i, p: (0, i)),
            ],
            out_specs=pl.BlockSpec((1, rows, width), lambda i, p: (i, 0, 0)),
        ),
        out_shape=jax.ShapeDtypeStruct((chunks, rows, width), BF16),
        compiler_params=pltpu.CompilerParams(vmem_limit_bytes=VMEM_LIMIT),
        name="project",
    )(jnp.stack([place, parity]).astype(jnp.int32), mixed, w_out, w_other)
    gathered = lax.all_to_all(partial, "tp", 0, 0, tiled=True, axis_index_groups=parity_groups)
    return jnp.sum(gathered.astype(F32), axis=0).astype(BF16)


def solution(mesh):
    in_specs = (
        P(None, ("dp", "ctx"), "tp"),
        P(None, None, "tp"),
        P("ctx", "tp"),
        P("tp"),
        P("tp", None),
    )
    out_specs = P(("dp", "ctx"), "tp")
    return jax.shard_map(local, mesh=mesh, in_specs=in_specs, out_specs=out_specs, check_vma=False)
```

```python
import math

import jax
import jax.numpy as jnp
import numpy as np
from jax import lax
from jax.experimental import pallas as pl
from jax.experimental.pallas import tpu as pltpu
from jax.sharding import PartitionSpec as P

TAPS = 7
BF16 = jnp.bfloat16
F32 = jnp.float32
VMEM_LIMIT = 50 * 1024 * 1024


def split_bf16(values):
    high = values.astype(BF16)
    return high, (values - high.astype(F32)).astype(BF16)


def lane_dft(width):
    turns = np.outer(np.arange(width), np.arange(width)) % width
    angle = 2.0 * np.pi * turns / width
    cos, sin = np.cos(angle), np.sin(angle)
    forward = np.block([[cos, -sin], [sin, cos]]).astype(np.float32)
    high = forward.astype(jnp.bfloat16)
    low = (forward - high.astype(np.float32)).astype(jnp.bfloat16)
    return np.stack([high, low]), np.stack([high.T.copy(), low.T.copy()])


def twiddles(blocks, width):
    angle = 2.0 * np.pi * np.outer(np.arange(blocks) + 0.5, np.arange(width)) / (2 * blocks * width)
    return np.stack([np.cos(angle), -np.sin(angle)]).astype(np.float32)[:, :, None, :]


def block_angle(s, k, blocks):
    return math.pi * ((s * (2 * k + 1)) % (4 * blocks)) / (2 * blocks)


def prep_kernel(parity_ref, projected_ref, filter_ref, w_ref, out_ref, w_send_ref, sems):
    blocks, _, rows = out_ref.shape
    width = filter_ref.shape[1]
    group = width // blocks
    copies = []
    for i in range(w_send_ref.shape[1] // width):
        start = pl.multiple_of((2 * i + 1 - parity_ref[0]) * width, width)
        copies.append(
            pltpu.make_async_copy(
                w_ref.at[:, pl.ds(start, width)], w_send_ref.at[:, i * width : (i + 1) * width], sems.at[i]
            )
        )
        copies[-1].start()
    for part in range(4):
        source = projected_ref[part] if part < 3 else filter_ref[...].astype(BF16)
        turned = source.T
        out_ref[:, part * group : (part + 1) * group, :] = turned.reshape(blocks, group, rows)
    for copy in copies:
        copy.wait()


def over_blocks(values, k, blocks):
    even_c = even_s = odd_c = odd_s = None
    for s, value in enumerate(values):
        c, t = math.cos(block_angle(s, k, blocks)), math.sin(block_angle(s, k, blocks))
        if s == 0:
            even_c = value
            continue
        term_c, term_s = value * c, value * t
        if s % 2 == 0:
            even_c = even_c + term_c
            even_s = term_s if even_s is None else even_s + term_s
        else:
            odd_c = term_c if odd_c is None else odd_c + term_c
            odd_s = term_s if odd_s is None else odd_s + term_s
    return (even_c + odd_c, -(even_s + odd_s)), (even_c - odd_c, even_s - odd_s)


def store_split(ref_high, ref_low, rows, cols, value):
    high, low = split_bf16(value)
    ref_high[rows, cols] = high
    ref_low[rows, cols] = low


def dot3(high, low, table_ref):
    def dot(a, b):
        return jnp.dot(a, b, preferred_element_type=F32)

    return dot(high, table_ref[0]) + dot(low, table_ref[0]) + dot(high, table_ref[1])


def conv_kernel(
    recv_ref, taps_ref, fwd_hbm, inv_hbm, tw_ref, out_ref, query, gated, high, low, spec_h, spec_u, fwd_ref, inv_ref, sems
):
    blocks, quad, width = recv_ref.shape
    fwd_copy = pltpu.make_async_copy(fwd_hbm, fwd_ref, sems.at[0])
    inv_copy = pltpu.make_async_copy(inv_hbm, inv_ref, sems.at[1])
    fwd_copy.start()
    inv_copy.start()
    group = quad // 4
    lane = lax.broadcasted_iota(jnp.int32, (group, width), 1)

    def tap(part, j):
        column = part * TAPS + j
        return taps_ref[:, column : column + 1]

    def shifted(now, before, amount):
        return jnp.where(lane < amount, pltpu.roll(before, amount, 1), pltpu.roll(now, amount, 1))

    zeros = jnp.zeros((group, width), F32)
    state = [[zeros] * 4 for _ in range(3)]
    for s in range(blocks):
        results = []
        for part in range(3):
            now = recv_ref[s, part * group : (part + 1) * group, :].astype(F32)
            one = shifted(now, state[part][0], 1)
            pair6 = tap(part, 6) * now
            pair4 = tap(part, 4) * now + tap(part, 5) * one + shifted(pair6, state[part][1], 2)
            pair2 = tap(part, 2) * now + tap(part, 3) * one + shifted(pair4, state[part][2], 2)
            pair0 = tap(part, 0) * now + tap(part, 1) * one + shifted(pair2, state[part][3], 2)
            state[part] = [now, pair6, pair4, pair2]
            results.append(pair0)
        query[s] = results[0]
        gated[s] = results[1] * results[2]

    def forward(load, _):
        for c0 in range(0, group, 16):
            for l0 in range(0, width, 128):
                values = [load(s, slice(c0, c0 + 16), slice(l0, l0 + 128)) for s in range(blocks)]
                for k in range(blocks // 2):
                    for kk, (re, im) in zip((k, blocks - 1 - k), over_blocks(values, k, blocks)):
                        tr = tw_ref[0, kk, :, l0 : l0 + 128]
                        ti = tw_ref[1, kk, :, l0 : l0 + 128]
                        rows = slice(kk * group + c0, kk * group + c0 + 16)
                        store_split(high, low, rows, slice(l0, l0 + 128), re * tr - im * ti)
                        store_split(high, low, rows, slice(width + l0, width + l0 + 128), re * ti + im * tr)

    forward(lambda s, c, p: recv_ref[s, 3 * group + c.start : 3 * group + c.stop, p].astype(F32), spec_h)
    fwd_copy.wait()
    spec_h[...] = dot3(high[...], low[...], fwd_ref)
    forward(lambda s, c, p: gated[s, c, p], spec_u)
    spec_u[...] = dot3(high[...], low[...], fwd_ref)

    hr, hi = spec_h[:, :width], spec_h[:, width:]
    ur, ui = spec_u[:, :width], spec_u[:, width:]
    store_split(high, low, slice(None), slice(0, width), hr * ur - hi * ui)
    store_split(high, low, slice(None), slice(width, 2 * width), hr * ui + hi * ur)
    inv_copy.wait()
    spec_h[...] = dot3(high[...], low[...], inv_ref)

    scale = 1.0 / (blocks * width)
    for c0 in range(0, group, 16):
        for l0 in range(0, width, 128):
            reals, imags = [], []
            for k in range(blocks):
                rows = slice(k * group + c0, k * group + c0 + 16)
                tr = tw_ref[0, k, :, l0 : l0 + 128] * scale
                ti = tw_ref[1, k, :, l0 : l0 + 128] * scale
                re = spec_h[rows, l0 : l0 + 128]
                im = spec_h[rows, width + l0 : width + l0 + 128]
                reals.append(re * tr + im * ti)
                imags.append(im * tr - re * ti)
            half = blocks // 2
            sum_re = [reals[k] + reals[blocks - 1 - k] for k in range(half)]
            dif_re = [reals[k] - reals[blocks - 1 - k] for k in range(half)]
            sum_im = [imags[k] + imags[blocks - 1 - k] for k in range(half)]
            dif_im = [imags[k] - imags[blocks - 1 - k] for k in range(half)]
            skip = taps_ref[c0 : c0 + 16, 3 * TAPS : 3 * TAPS + 1]
            for s in range(blocks):
                res, ims = (sum_re, dif_im) if s % 2 == 0 else (dif_re, sum_im)
                total = None
                for k in range(half):
                    angle = block_angle(s, k, blocks)
                    if s == 0:
                        term = res[k]
                    else:
                        term = res[k] * math.cos(angle) - ims[k] * math.sin(angle)
                    total = term if total is None else total + term
                at = (s, slice(c0, c0 + 16), slice(l0, l0 + 128))
                mixed = (query[at] * (total + skip * gated[at])).astype(BF16)
                out_ref[(0, *at)] = mixed
                out_ref[(1, *at)] = mixed


def project_kernel(place_ref, mixed_ref, own_ref, other_ref, out_ref, turned):
    mine = place_ref[0]
    depth = own_ref.shape[0]
    rows = mixed_ref.shape[-1]

    @pl.when(pl.program_id(0) == 0)
    def _():
        turned[0] = mixed_ref[mine].reshape(depth, rows).T
        turned[1] = mixed_ref[1 - mine].reshape(depth, rows).T

    total = jnp.dot(turned[0], own_ref[...], preferred_element_type=F32)
    total += jnp.dot(turned[1], other_ref[...], preferred_element_type=F32)
    out_ref[0] = total.astype(BF16)


def local(projected, short_taps, long_filter, skip_gain, w_out):
    ctx, tp, dp = lax.axis_size("ctx"), lax.axis_size("tp"), lax.axis_size("dp")
    rows, width = projected.shape[1:]
    group = width // ctx
    me_ctx, me_tp, me_dp = lax.axis_index("ctx"), lax.axis_index("tp"), lax.axis_index("dp")

    def partner(z, d):
        first = d + (z - d) % tp // 2 * 2
        return (first + (1 - (z - d) % tp % 2)) % tp

    pair_route = [(z * dp + d, partner(z, d) * dp + d) for z in range(tp) for d in range(dp)]
    pair_groups = [
        [(c * tp + (first + d + b) % tp) * dp + d for b in range(2) for c in range(ctx)]
        for d in range(dp)
        for first in range(0, tp, 2)
    ]
    parity_groups = [list(range(odd, tp, 2)) for odd in range(2)]
    chunks = tp // 2
    parity = me_tp % 2
    place = (me_tp - me_dp) % tp % 2

    whole = pl.BlockSpec()
    in_place = pl.BlockSpec(memory_space=pl.ANY)
    send, w_send = pl.pallas_call(
        prep_kernel,
        in_specs=[pl.BlockSpec(memory_space=pltpu.SMEM), whole, whole, in_place],
        out_specs=[whole, in_place],
        out_shape=[
            jax.ShapeDtypeStruct((ctx, 4 * group, rows), BF16),
            jax.ShapeDtypeStruct((width, chunks * width), BF16),
        ],
        scratch_shapes=[pltpu.SemaphoreType.DMA((chunks,))],
        compiler_params=pltpu.CompilerParams(vmem_limit_bytes=VMEM_LIMIT),
        name="prep",
    )(parity.astype(jnp.int32)[None], projected, long_filter, w_out)
    w_other = lax.ppermute(w_send, ("tp", "dp"), pair_route)
    recv = lax.all_to_all(send, "ctx", 0, 0, tiled=True)

    table = jnp.concatenate([short_taps.reshape(3 * TAPS, width), skip_gain[None, :]], axis=0)
    table = lax.dynamic_slice_in_dim(table, me_ctx * group, group, axis=1).T
    fwd, inv = lane_dft(rows)
    mixed = pl.pallas_call(
        conv_kernel,
        out_shape=jax.ShapeDtypeStruct((2, ctx, group, rows), BF16),
        scratch_shapes=[
            pltpu.VMEM((ctx, group, rows), F32),
            pltpu.VMEM((ctx, group, rows), F32),
            pltpu.VMEM((ctx * group, 2 * rows), BF16),
            pltpu.VMEM((ctx * group, 2 * rows), BF16),
            pltpu.VMEM((ctx * group, 2 * rows), F32),
            pltpu.VMEM((ctx * group, 2 * rows), F32),
            pltpu.VMEM((2, 2 * rows, 2 * rows), BF16),
            pltpu.VMEM((2, 2 * rows, 2 * rows), BF16),
            pltpu.SemaphoreType.DMA((2,)),
        ],
        in_specs=[whole, whole, in_place, in_place, whole],
        compiler_params=pltpu.CompilerParams(vmem_limit_bytes=VMEM_LIMIT),
        name="conv",
    )(recv, table, jnp.asarray(fwd), jnp.asarray(inv), jnp.asarray(twiddles(ctx, rows)))
    mixed = lax.all_to_all(
        mixed.reshape(2 * ctx, group, rows), ("ctx", "tp", "dp"), 0, 0, tiled=True, axis_index_groups=pair_groups
    ).reshape(2, ctx, group, rows)

    partial = pl.pallas_call(
        project_kernel,
        grid_spec=pltpu.PrefetchScalarGridSpec(
            num_scalar_prefetch=1,
            grid=(chunks,),
            in_specs=[
                pl.BlockSpec((2, ctx, group, rows), lambda i, p: (0, 0, 0, 0)),
                pl.BlockSpec((width, width), lambda i, p: (0, 2 * i + p[1])),
                pl.BlockSpec((width, width), lambda i, p: (0, i)),
            ],
            out_specs=pl.BlockSpec((1, rows, width), lambda i, p: (i, 0, 0)),
            scratch_shapes=[pltpu.VMEM((2, rows, width), BF16)],
        ),
        out_shape=jax.ShapeDtypeStruct((chunks, rows, width), BF16),
        compiler_params=pltpu.CompilerParams(vmem_limit_bytes=VMEM_LIMIT),
        name="project",
    )(jnp.stack([place, parity]).astype(jnp.int32), mixed, w_out, w_other)
    gathered = lax.all_to_all(partial, "tp", 0, 0, tiled=True, axis_index_groups=parity_groups)
    return jnp.sum(gathered.astype(F32), axis=0).astype(BF16)


def solution(mesh):
    in_specs = (
        P(None, ("dp", "ctx"), "tp"),
        P(None, None, "tp"),
        P("ctx", "tp"),
        P("tp"),
        P("tp", None),
    )
    out_specs = P(("dp", "ctx"), "tp")
    return jax.shard_map(local, mesh=mesh, in_specs=in_specs, out_specs=out_specs, check_vma=False)
```

```python
import jax
import jax.numpy as jnp
import numpy as np
from jax import lax
from jax.experimental import pallas as pl
from jax.experimental.pallas import tpu as pltpu
from jax.sharding import PartitionSpec as P

TAPS = 7
LANES = 128
BF16 = jnp.bfloat16
F32 = jnp.float32
MIB = 1024 * 1024


def split_table(table):
    high = table.astype(np.float32).astype(jnp.bfloat16)
    low = (table - high.astype(np.float64)).astype(np.float32).astype(jnp.bfloat16)
    return np.stack([high, low])


def dft_tables(blocks, width, channels):
    angle = 2.0 * np.pi * (np.outer(np.arange(width), np.arange(width)) % width) / width
    cos, sin = np.cos(angle), np.sin(angle)
    lanes = np.block([[cos, -sin], [sin, cos]])
    angle = np.pi * (np.outer(2 * np.arange(blocks) + 1, np.arange(blocks)) % (4 * blocks)) / (2 * blocks)
    cos, sin = np.kron(np.cos(angle), np.eye(channels)), np.kron(np.sin(angle), np.eye(channels))
    scale = 1.0 / (blocks * width)
    tables = (np.concatenate([cos, -sin]), lanes, lanes.T, scale * np.concatenate([cos.T, -sin.T]))
    return [split_table(table).reshape(-1, table.shape[1]) for table in tables]


def twiddles(blocks, width):
    angle = 2.0 * np.pi * np.outer(np.arange(blocks) + 0.5, np.arange(width)) / (2 * blocks * width)
    return np.stack([np.cos(angle), -np.sin(angle)]).astype(np.float32)[:, :, None, :]


def split_bf16(values):
    high = values.astype(BF16)
    return high, (values - high.astype(F32)).astype(BF16)


def dot(a, b):
    return jnp.dot(a, b, preferred_element_type=F32)


def prep_kernel(
    parity_ref, projected_hbm, filter_hbm, w_hbm, out_hbm, w_send, inputs, taps_in, turned, held, sems, w_sems
):
    blocks, quad, rows = turned.shape
    group = quad // 4
    width = w_hbm.shape[0]
    chunks = w_send.shape[1] // width
    arrive = [pltpu.make_async_copy(projected_hbm.at[part], inputs.at[part], sems.at[part]) for part in range(3)]
    arrive.append(pltpu.make_async_copy(filter_hbm, taps_in, sems.at[3]))
    for copy in arrive:
        copy.start()
    w_in, w_out = [], []
    for i in range(chunks):
        start = pl.multiple_of((2 * i + 1 - parity_ref[0]) * width, width)
        columns = slice(i * width, (i + 1) * width)
        w_in.append(pltpu.make_async_copy(w_hbm.at[:, pl.ds(start, width)], held.at[:, columns], w_sems.at[i]))
        w_out.append(pltpu.make_async_copy(held.at[:, columns], w_send.at[:, columns], w_sems.at[chunks + i]))
        w_in[i].start()
    leave = []
    for part in range(4):
        arrive[part].wait()
        source = inputs[part] if part < 3 else taps_in[...].astype(BF16)
        lines = slice(part * group, (part + 1) * group)
        turned[:, lines, :] = source.T.reshape(blocks, group, rows)
        leave.append(pltpu.make_async_copy(turned.at[:, lines], out_hbm.at[:, lines], sems.at[4 + part]))
        leave[part].start()
    for i in range(chunks):
        w_in[i].wait()
        w_out[i].start()
    for copy in leave + w_out:
        copy.wait()


def featurize(recv_ref, taps_ref, query, gated, u_high, u_low):
    blocks, quad, width = recv_ref.shape
    group = quad // 4
    tile = 16
    lane = lax.broadcasted_iota(jnp.int32, (tile, LANES), 1)
    first, second = lane < 1, lane < 2
    zeros = jnp.zeros((tile, LANES), F32)
    for part in (1, 2, 0):
        for c0 in range(0, group, tile):
            lines = slice(c0, c0 + tile)
            t = [
                jnp.broadcast_to(taps_ref[lines, part * TAPS + j : part * TAPS + j + 1], (tile, LANES))
                for j in range(TAPS)
            ]
            before = [zeros] * 4
            for s in range(blocks):
                for l0 in range(0, width, LANES):
                    cols = slice(l0, l0 + LANES)
                    now = recv_ref[s, part * group + c0 : part * group + c0 + tile, cols].astype(F32)
                    turn = [pltpu.roll(now, 1, 1)]
                    one = jnp.where(first, before[0], turn[0])
                    turn.append(pltpu.roll(t[6] * now, 2, 1))
                    level = t[4] * now + t[5] * one + jnp.where(second, before[1], turn[1])
                    turn.append(pltpu.roll(level, 2, 1))
                    level = t[2] * now + t[3] * one + jnp.where(second, before[2], turn[2])
                    turn.append(pltpu.roll(level, 2, 1))
                    level = t[0] * now + t[1] * one + jnp.where(second, before[3], turn[3])
                    before = turn
                    if part == 0:
                        query[s, lines, cols] = level
                    elif part == 1:
                        gated[s, lines, cols] = level
                    else:
                        product = gated[s, lines, cols] * level
                        gated[s, lines, cols] = product
                        at = slice(s * group + c0, s * group + c0 + tile)
                        u_high[at, cols], u_low[at, cols] = split_bf16(product)


def conv_kernel(
    recv_ref, taps_ref, tw_ref, tables_hbm, out_hbm, query, gated, u_high, u_low, b_high, b_low, mixed, tables, sems, out_sems
):
    blocks, quad, width = recv_ref.shape
    group = quad // 4
    rows = blocks * group
    step = rows // 2
    per = blocks // 2
    copies, firsts, start = [], [], 0
    for i, size in enumerate((4 * rows, 4 * width, 4 * width, 4 * rows)):
        firsts.append((start, size))
        copies.append(pltpu.make_async_copy(tables_hbm.at[start : start + size], tables.at[start : start + size], sems.at[i]))
        copies[i].start()
        start += size

    def table(which, low, at=None):
        start, size = firsts[which]
        at = slice(0, size // 2) if at is None else at
        start += low * (size // 2)
        return tables[start + at.start : start + at.stop, :]

    featurize(recv_ref, taps_ref, query, gated, u_high, u_low)
    filter_rows = recv_ref[:, 3 * group :, :].reshape(rows, width)

    def turned(re, im, k0, sign):
        tr, ti = tw_ref[0, k0 : k0 + per], sign * tw_ref[1, k0 : k0 + per]
        re, im = re.reshape(per, group, width), im.reshape(per, group, width)
        return (re * tr - im * ti).reshape(step, width), (re * ti + im * tr).reshape(step, width)

    def lanes(re, im, which):
        high, low = split_bf16(jnp.concatenate([re, im], axis=1))
        out = dot(high, table(which, 0)) + dot(low, table(which, 0)) + dot(high, table(which, 1))
        return out[:, :width], out[:, width:]

    for copy in copies:
        copy.wait()
    for k0 in range(0, blocks, per):
        spectra = []
        for high, low in ((filter_rows, None), (u_high[...], u_low[...])):
            parts = []
            for half in range(2):
                at = slice(half * rows + k0 * group, half * rows + k0 * group + step)
                part = dot(table(0, 0, at), high) + dot(table(0, 1, at), high)
                if low is not None:
                    part = part + dot(table(0, 0, at), low)
                parts.append(part)
            spectra.append(lanes(*turned(*parts, k0, 1.0), 1))
        (hr, hi), (ur, ui) = spectra
        re, im = lanes(hr * ur - hi * ui, hr * ui + hi * ur, 2)
        for half, part in enumerate(turned(re, im, k0, -1.0)):
            at = slice(half * rows + k0 * group, half * rows + k0 * group + step)
            b_high[at], b_low[at] = split_bf16(part)

    out_copies = []
    skip = taps_ref[:, 3 * TAPS : 3 * TAPS + 1][None]
    for s0 in range(0, blocks, per):
        total = None
        for half in range(2):
            at = slice(half * rows + s0 * group, half * rows + s0 * group + step)
            from_rows = slice(half * rows, (half + 1) * rows)
            for t, b in ((0, b_high), (0, b_low), (1, b_high)):
                term = dot(table(3, t, at), b[from_rows])
                total = term if total is None else total + term
        span = slice(s0, s0 + per)
        mixed[span] = (query[span] * (total.reshape(per, group, width) + skip * gated[span])).astype(BF16)
        for twin in range(2):
            i = len(out_copies)
            out_copies.append(pltpu.make_async_copy(mixed.at[span], out_hbm.at[twin, span], out_sems.at[i]))
            out_copies[i].start()
    for copy in out_copies:
        copy.wait()


def project_kernel(index_ref, mixed_ref, w_hbm, other_ref, out_ref, own, sems):
    chunks, rows, width = out_ref.shape
    copies = []
    for i in range(chunks):
        start = pl.multiple_of((2 * i + index_ref[1]) * width, width)
        copies.append(
            pltpu.make_async_copy(w_hbm.at[:, pl.ds(start, width)], own.at[:, i * width : (i + 1) * width], sems.at[i])
        )
        copies[i].start()
    mine = index_ref[0]
    first = mixed_ref[mine].reshape(width, rows).T
    second = mixed_ref[1 - mine].reshape(width, rows).T
    for i in range(chunks):
        columns = slice(i * width, (i + 1) * width)
        total = dot(second, other_ref[:, columns])
        copies[i].wait()
        out_ref[i] = (total + dot(first, own[:, columns])).astype(BF16)


def local(projected, short_taps, long_filter, skip_gain, w_out):
    ctx, tp, dp = lax.axis_size("ctx"), lax.axis_size("tp"), lax.axis_size("dp")
    rows, width = projected.shape[1:]
    group = width // ctx
    me_ctx, me_tp, me_dp = lax.axis_index("ctx"), lax.axis_index("tp"), lax.axis_index("dp")

    def partner(z, d):
        first = d + (z - d) % tp // 2 * 2
        return (first + (1 - (z - d) % tp % 2)) % tp

    pair_route = [(z * dp + d, partner(z, d) * dp + d) for z in range(tp) for d in range(dp)]
    pair_groups = [
        [(c * tp + (first + d + b) % tp) * dp + d for b in range(2) for c in range(ctx)]
        for d in range(dp)
        for first in range(0, tp, 2)
    ]
    parity_groups = [list(range(odd, tp, 2)) for odd in range(2)]
    chunks = tp // 2
    parity = (me_tp % 2).astype(jnp.int32)
    place = ((me_tp - me_dp) % tp % 2).astype(jnp.int32)

    vmem = pl.BlockSpec(memory_space=pltpu.VMEM)
    smem = pl.BlockSpec(memory_space=pltpu.SMEM)
    hbm = pl.BlockSpec(memory_space=pl.ANY)
    params = pltpu.CompilerParams(vmem_limit_bytes=60 * MIB)

    send, w_send = pl.pallas_call(
        prep_kernel,
        in_specs=[smem, hbm, hbm, hbm],
        out_specs=[hbm, hbm],
        out_shape=[
            jax.ShapeDtypeStruct((ctx, 4 * group, rows), BF16),
            jax.ShapeDtypeStruct((width, chunks * width), BF16),
        ],
        scratch_shapes=[
            pltpu.VMEM((3, rows, width), BF16),
            pltpu.VMEM((rows, width), F32),
            pltpu.VMEM((ctx, 4 * group, rows), BF16),
            pltpu.VMEM((width, chunks * width), BF16),
            pltpu.SemaphoreType.DMA((8,)),
            pltpu.SemaphoreType.DMA((2 * chunks,)),
        ],
        compiler_params=params,
        name="prep",
    )(parity[None], projected, long_filter, w_out)
    recv = lax.all_to_all(send, "ctx", 0, 0, tiled=True)
    w_other = lax.ppermute(w_send, ("tp", "dp"), pair_route)

    taps = jnp.concatenate([short_taps.reshape(3 * TAPS, width), skip_gain[None, :]], axis=0)
    taps = lax.dynamic_slice_in_dim(taps, me_ctx * group, group, axis=1).T
    tables = np.concatenate(dft_tables(ctx, rows, group))
    mixed = pl.pallas_call(
        conv_kernel,
        in_specs=[vmem, vmem, vmem, hbm],
        out_specs=hbm,
        out_shape=jax.ShapeDtypeStruct((2, ctx, group, rows), BF16),
        scratch_shapes=[
            pltpu.VMEM((ctx, group, rows), F32),
            pltpu.VMEM((ctx, group, rows), F32),
            pltpu.VMEM((ctx * group, rows), BF16),
            pltpu.VMEM((ctx * group, rows), BF16),
            pltpu.VMEM((2 * ctx * group, rows), BF16),
            pltpu.VMEM((2 * ctx * group, rows), BF16),
            pltpu.VMEM((ctx, group, rows), BF16),
            pltpu.VMEM(tables.shape, BF16),
            pltpu.SemaphoreType.DMA((4,)),
            pltpu.SemaphoreType.DMA((4,)),
        ],
        compiler_params=pltpu.CompilerParams(vmem_limit_bytes=52 * MIB),
        name="conv",
    )(recv, taps, jnp.asarray(twiddles(ctx, rows)), jnp.asarray(tables))
    mixed = lax.all_to_all(
        mixed.reshape(2 * ctx, group, rows), ("ctx", "tp", "dp"), 0, 0, tiled=True, axis_index_groups=pair_groups
    ).reshape(2, ctx, group, rows)

    partial = pl.pallas_call(
        project_kernel,
        in_specs=[smem, vmem, hbm, vmem],
        out_specs=vmem,
        out_shape=jax.ShapeDtypeStruct((chunks, rows, width), BF16),
        scratch_shapes=[
            pltpu.VMEM((width, chunks * width), BF16),
            pltpu.SemaphoreType.DMA((chunks,)),
        ],
        compiler_params=params,
        name="project",
    )(jnp.stack([place, parity]), mixed, w_out, w_other)
    gathered = lax.all_to_all(partial, "tp", 0, 0, tiled=True, axis_index_groups=parity_groups)
    return jnp.sum(gathered.astype(F32), axis=0).astype(BF16)


def solution(mesh):
    in_specs = (
        P(None, ("dp", "ctx"), "tp"),
        P(None, None, "tp"),
        P("ctx", "tp"),
        P("tp"),
        P("tp", None),
    )
    out_specs = P(("dp", "ctx"), "tp")
    return jax.shard_map(local, mesh=mesh, in_specs=in_specs, out_specs=out_specs, check_vma=False)
```

```python
import math

import jax
import jax.numpy as jnp
import numpy as np
from jax import lax
from jax.experimental import pallas as pl
from jax.experimental.pallas import tpu as pltpu
from jax.sharding import PartitionSpec as P

TAPS = 7
LANES = 128
BF16 = jnp.bfloat16
F32 = jnp.float32
MIB = 1024 * 1024


def split_table(table):
    high = table.astype(np.float32).astype(jnp.bfloat16)
    low = (table - high.astype(np.float64)).astype(np.float32).astype(jnp.bfloat16)
    return np.stack([high, low])


def lane_tables(width):
    angle = 2.0 * np.pi * (np.outer(np.arange(width), np.arange(width)) % width) / width
    cos, sin = np.cos(angle), np.sin(angle)
    forward = np.block([[cos, -sin], [sin, cos]])
    return np.concatenate([split_table(table).reshape(-1, 2 * width) for table in (forward, forward.T)])


def twiddles(blocks, width):
    angle = 2.0 * np.pi * np.outer(np.arange(blocks) + 0.5, np.arange(width)) / (2 * blocks * width)
    return np.stack([np.cos(angle), -np.sin(angle)]).astype(np.float32)[:, :, None, :]


def block_angle(s, k, blocks):
    return math.pi * ((s * (2 * k + 1)) % (4 * blocks)) / (2 * blocks)


def split_bf16(values):
    high = values.astype(BF16)
    return high, (values - high.astype(F32)).astype(BF16)


def dot(a, b):
    return jnp.dot(a, b, preferred_element_type=F32)


def prep_kernel(
    parity_ref, projected_hbm, filter_hbm, w_hbm, out_hbm, w_send, inputs, taps_in, turned, held, sems, w_sems
):
    blocks, quad, rows = turned.shape
    group = quad // 4
    width = w_hbm.shape[0]
    chunks = w_send.shape[1] // width
    arrive = [pltpu.make_async_copy(projected_hbm.at[part], inputs.at[part], sems.at[part]) for part in range(3)]
    arrive.append(pltpu.make_async_copy(filter_hbm, taps_in, sems.at[3]))
    for copy in arrive:
        copy.start()
    w_in, w_out = [], []
    for i in range(chunks):
        start = pl.multiple_of((2 * i + 1 - parity_ref[0]) * width, width)
        columns = slice(i * width, (i + 1) * width)
        w_in.append(pltpu.make_async_copy(w_hbm.at[:, pl.ds(start, width)], held.at[:, columns], w_sems.at[i]))
        w_out.append(pltpu.make_async_copy(held.at[:, columns], w_send.at[:, columns], w_sems.at[chunks + i]))
        w_in[i].start()
    leave = []
    for part in range(4):
        arrive[part].wait()
        source = inputs[part] if part < 3 else taps_in[...].astype(BF16)
        lines = slice(part * group, (part + 1) * group)
        turned[:, lines, :] = source.T.reshape(blocks, group, rows)
        leave.append(pltpu.make_async_copy(turned.at[:, lines], out_hbm.at[:, lines], sems.at[4 + part]))
        leave[part].start()
    for i in range(chunks):
        w_in[i].wait()
        w_out[i].start()
    for copy in leave + w_out:
        copy.wait()


def featurize(recv_ref, taps_ref, query, gated):
    blocks, quad, width = recv_ref.shape
    group = quad // 4
    tile = 16
    batch = blocks
    lane = lax.broadcasted_iota(jnp.int32, (tile, LANES), 1)
    for c0 in range(0, group, tile):
        lines = slice(c0, c0 + tile)
        for part in (1, 2, 0):
            t = [
                jnp.broadcast_to(taps_ref[lines, part * TAPS + j : part * TAPS + j + 1], (tile, LANES))
                for j in range(TAPS)
            ]
            last = [jnp.zeros((tile, LANES), F32)] * 4
            first_row = part * group + c0
            for s0 in range(0, blocks, batch):
                places = [(s, lines, slice(l0, l0 + LANES)) for s in range(s0, s0 + batch) for l0 in range(0, width, LANES)]
                now = [recv_ref[s, first_row : first_row + tile, cols].astype(F32) for s, _, cols in places]
                gates = [gated[at] for at in places] if part == 2 else None

                def shifted(values, amount, which):
                    turns = [pltpu.roll(value, amount, 1) for value in values]
                    moved = [jnp.where(lane < amount, b, a) for b, a in zip([last[which]] + turns[:-1], turns)]
                    last[which] = turns[-1]
                    return moved

                one = shifted(now, 1, 0)
                two = shifted([t[2] * x + t[3] * y for x, y in zip(now, one)], 2, 1)
                four = shifted([t[4] * x + t[5] * y for x, y in zip(now, one)], 4, 2)
                six = shifted([t[6] * x for x in now], 6, 3)
                totals = [t[0] * x + t[1] * y + a + b + c for x, y, a, b, c in zip(now, one, two, four, six)]
                if part == 2:
                    totals = [g * total for g, total in zip(gates, totals)]
                for at, total in zip(places, totals):
                    (query if part == 0 else gated)[at] = total


def over_blocks(values, k, blocks):
    even_c = even_s = odd_c = odd_s = None
    for s, value in enumerate(values):
        c, t = math.cos(block_angle(s, k, blocks)), math.sin(block_angle(s, k, blocks))
        if s == 0:
            even_c = value
            continue
        term_c, term_s = value * c, value * t
        if s % 2 == 0:
            even_c = even_c + term_c
            even_s = term_s if even_s is None else even_s + term_s
        else:
            odd_c = term_c if odd_c is None else odd_c + term_c
            odd_s = term_s if odd_s is None else odd_s + term_s
    return (even_c + odd_c, -(even_s + odd_s)), (even_c - odd_c, even_s - odd_s)


def conv_kernel(
    recv_ref, taps_ref, tw_ref, tables_hbm, out_hbm, query, gated, high, low, spec_h, spec_u, mixed, tables, sems, out_sems
):
    blocks, quad, width = recv_ref.shape
    group = quad // 4
    tile = 16
    load = pltpu.make_async_copy(tables_hbm, tables, sems.at[0])
    load.start()
    featurize(recv_ref, taps_ref, query, gated)

    def table(which, term):
        start = (2 * which + term) * 2 * width
        return tables[start : start + 2 * width, :]

    def store_split(rows, cols, value):
        high[rows, cols], low[rows, cols] = split_bf16(value)

    def lanes(which):
        return dot(high[...], table(which, 0)) + dot(low[...], table(which, 0)) + dot(high[...], table(which, 1))

    def to_odd(block):
        for c0 in range(0, group, tile):
            for l0 in range(0, width, LANES):
                values = [block(s, c0, slice(l0, l0 + LANES)) for s in range(blocks)]
                for k in range(blocks // 2):
                    for kk, (re, im) in zip((k, blocks - 1 - k), over_blocks(values, k, blocks)):
                        tr = tw_ref[0, kk, :, l0 : l0 + LANES]
                        ti = tw_ref[1, kk, :, l0 : l0 + LANES]
                        rows = slice(kk * group + c0, kk * group + c0 + tile)
                        store_split(rows, slice(l0, l0 + LANES), re * tr - im * ti)
                        store_split(rows, slice(width + l0, width + l0 + LANES), re * ti + im * tr)

    to_odd(lambda s, c, p: recv_ref[s, 3 * group + c : 3 * group + c + tile, p].astype(F32))
    load.wait()
    spec_h[...] = lanes(0)
    to_odd(lambda s, c, p: gated[s, c : c + tile, p])
    spec_u[...] = lanes(0)

    hr, hi = spec_h[:, :width], spec_h[:, width:]
    ur, ui = spec_u[:, :width], spec_u[:, width:]
    store_split(slice(None), slice(0, width), hr * ur - hi * ui)
    store_split(slice(None), slice(width, 2 * width), hr * ui + hi * ur)
    spec_h[...] = lanes(1)

    scale = 1.0 / (blocks * width)
    half = blocks // 2
    for c0 in range(0, group, tile):
        skip = taps_ref[c0 : c0 + tile, 3 * TAPS : 3 * TAPS + 1]
        for l0 in range(0, width, LANES):
            reals, imags = [], []
            for k in range(blocks):
                rows = slice(k * group + c0, k * group + c0 + tile)
                tr = tw_ref[0, k, :, l0 : l0 + LANES] * scale
                ti = tw_ref[1, k, :, l0 : l0 + LANES] * scale
                re = spec_h[rows, l0 : l0 + LANES]
                im = spec_h[rows, width + l0 : width + l0 + LANES]
                reals.append(re * tr + im * ti)
                imags.append(im * tr - re * ti)
            sum_re = [reals[k] + reals[blocks - 1 - k] for k in range(half)]
            dif_re = [reals[k] - reals[blocks - 1 - k] for k in range(half)]
            sum_im = [imags[k] + imags[blocks - 1 - k] for k in range(half)]
            dif_im = [imags[k] - imags[blocks - 1 - k] for k in range(half)]
            for s in range(blocks):
                res, ims = (sum_re, dif_im) if s % 2 == 0 else (dif_re, sum_im)
                total = None
                for k in range(half):
                    angle = block_angle(s, k, blocks)
                    term = res[k] if s == 0 else res[k] * math.cos(angle) - ims[k] * math.sin(angle)
                    total = term if total is None else total + term
                at = (s, slice(c0, c0 + tile), slice(l0, l0 + LANES))
                mixed[at] = (query[at] * (total + skip * gated[at])).astype(BF16)
    copies = [pltpu.make_async_copy(mixed, out_hbm.at[twin], out_sems.at[twin]) for twin in range(2)]
    for copy in copies:
        copy.start()
    for copy in copies:
        copy.wait()


def project_kernel(index_ref, mixed_ref, w_hbm, other_ref, out_ref, own, sems):
    chunks, rows, width = out_ref.shape
    copies = []
    for i in range(chunks):
        start = pl.multiple_of((2 * i + index_ref[1]) * width, width)
        copies.append(
            pltpu.make_async_copy(w_hbm.at[:, pl.ds(start, width)], own.at[:, i * width : (i + 1) * width], sems.at[i])
        )
        copies[i].start()
    mine = index_ref[0]
    first = mixed_ref[mine].reshape(width, rows).T
    second = mixed_ref[1 - mine].reshape(width, rows).T
    for i in range(chunks):
        columns = slice(i * width, (i + 1) * width)
        total = dot(second, other_ref[:, columns])
        copies[i].wait()
        out_ref[i] = (total + dot(first, own[:, columns])).astype(BF16)


def local(projected, short_taps, long_filter, skip_gain, w_out):
    ctx, tp, dp = lax.axis_size("ctx"), lax.axis_size("tp"), lax.axis_size("dp")
    rows, width = projected.shape[1:]
    group = width // ctx
    me_ctx, me_tp, me_dp = lax.axis_index("ctx"), lax.axis_index("tp"), lax.axis_index("dp")

    def partner(z, d):
        first = d + (z - d) % tp // 2 * 2
        return (first + (1 - (z - d) % tp % 2)) % tp

    pair_route = [(z * dp + d, partner(z, d) * dp + d) for z in range(tp) for d in range(dp)]
    pair_groups = [
        [(c * tp + (first + d + b) % tp) * dp + d for b in range(2) for c in range(ctx)]
        for d in range(dp)
        for first in range(0, tp, 2)
    ]
    parity_groups = [list(range(odd, tp, 2)) for odd in range(2)]
    chunks = tp // 2
    parity = (me_tp % 2).astype(jnp.int32)
    place = ((me_tp - me_dp) % tp % 2).astype(jnp.int32)

    vmem = pl.BlockSpec(memory_space=pltpu.VMEM)
    smem = pl.BlockSpec(memory_space=pltpu.SMEM)
    hbm = pl.BlockSpec(memory_space=pl.ANY)
    params = pltpu.CompilerParams(vmem_limit_bytes=60 * MIB)

    send, w_send = pl.pallas_call(
        prep_kernel,
        in_specs=[smem, hbm, hbm, hbm],
        out_specs=[hbm, hbm],
        out_shape=[
            jax.ShapeDtypeStruct((ctx, 4 * group, rows), BF16),
            jax.ShapeDtypeStruct((width, chunks * width), BF16),
        ],
        scratch_shapes=[
            pltpu.VMEM((3, rows, width), BF16),
            pltpu.VMEM((rows, width), F32),
            pltpu.VMEM((ctx, 4 * group, rows), BF16),
            pltpu.VMEM((width, chunks * width), BF16),
            pltpu.SemaphoreType.DMA((8,)),
            pltpu.SemaphoreType.DMA((2 * chunks,)),
        ],
        compiler_params=params,
        name="prep",
    )(parity[None], projected, long_filter, w_out)
    recv = lax.all_to_all(send, "ctx", 0, 0, tiled=True)
    w_other = lax.ppermute(w_send, ("tp", "dp"), pair_route)

    taps = jnp.concatenate([short_taps.reshape(3 * TAPS, width), skip_gain[None, :]], axis=0)
    taps = lax.dynamic_slice_in_dim(taps, me_ctx * group, group, axis=1).T
    tables = lane_tables(rows)
    mixed = pl.pallas_call(
        conv_kernel,
        in_specs=[vmem, vmem, vmem, hbm],
        out_specs=hbm,
        out_shape=jax.ShapeDtypeStruct((2, ctx, group, rows), BF16),
        scratch_shapes=[
            pltpu.VMEM((ctx, group, rows), F32),
            pltpu.VMEM((ctx, group, rows), F32),
            pltpu.VMEM((ctx * group, 2 * rows), BF16),
            pltpu.VMEM((ctx * group, 2 * rows), BF16),
            pltpu.VMEM((ctx * group, 2 * rows), F32),
            pltpu.VMEM((ctx * group, 2 * rows), F32),
            pltpu.VMEM((ctx, group, rows), BF16),
            pltpu.VMEM(tables.shape, BF16),
            pltpu.SemaphoreType.DMA((1,)),
            pltpu.SemaphoreType.DMA((2,)),
        ],
        compiler_params=pltpu.CompilerParams(vmem_limit_bytes=52 * MIB),
        name="conv",
    )(recv, taps, jnp.asarray(twiddles(ctx, rows)), jnp.asarray(tables))
    mixed = lax.all_to_all(
        mixed.reshape(2 * ctx, group, rows), ("ctx", "tp", "dp"), 0, 0, tiled=True, axis_index_groups=pair_groups
    ).reshape(2, ctx, group, rows)

    partial = pl.pallas_call(
        project_kernel,
        in_specs=[smem, vmem, hbm, vmem],
        out_specs=vmem,
        out_shape=jax.ShapeDtypeStruct((chunks, rows, width), BF16),
        scratch_shapes=[
            pltpu.VMEM((width, chunks * width), BF16),
            pltpu.SemaphoreType.DMA((chunks,)),
        ],
        compiler_params=pltpu.CompilerParams(vmem_limit_bytes=48 * MIB),
        name="project",
    )(jnp.stack([place, parity]), mixed, w_out, w_other)
    gathered = lax.all_to_all(partial, "tp", 0, 0, tiled=True, axis_index_groups=parity_groups)
    return jnp.sum(gathered.astype(F32), axis=0).astype(BF16)


def solution(mesh):
    in_specs = (
        P(None, ("dp", "ctx"), "tp"),
        P(None, None, "tp"),
        P("ctx", "tp"),
        P("tp"),
        P("tp", None),
    )
    out_specs = P(("dp", "ctx"), "tp")
    return jax.shard_map(local, mesh=mesh, in_specs=in_specs, out_specs=out_specs, check_vma=False)
```

```python
import math

import jax
import jax.numpy as jnp
import numpy as np
from jax import lax
from jax.experimental import pallas as pl
from jax.experimental.pallas import tpu as pltpu
from jax.sharding import PartitionSpec as P

TAPS = 7
LANES = 128
BF16 = jnp.bfloat16
F32 = jnp.float32
MIB = 1024 * 1024


def split_table(table):
    high = table.astype(np.float32).astype(jnp.bfloat16)
    low = (table - high.astype(np.float64)).astype(np.float32).astype(jnp.bfloat16)
    return np.stack([high, low])


def lane_tables(width):
    angle = 2.0 * np.pi * (np.outer(np.arange(width), np.arange(width)) % width) / width
    cos, sin = np.cos(angle), np.sin(angle)
    forward = np.block([[cos, -sin], [sin, cos]])
    return np.concatenate([split_table(table).reshape(-1, 2 * width) for table in (forward, forward.T)])


def twiddles(blocks, width):
    angle = 2.0 * np.pi * np.outer(np.arange(blocks) + 0.5, np.arange(width)) / (2 * blocks * width)
    return np.stack([np.cos(angle), -np.sin(angle)]).astype(np.float32)[:, :, None, :]


def block_angle(s, k, blocks):
    return math.pi * ((s * (2 * k + 1)) % (4 * blocks)) / (2 * blocks)


def split_bf16(values):
    high = values.astype(BF16)
    return high, (values - high.astype(F32)).astype(BF16)


def dot(a, b):
    return jnp.dot(a, b, preferred_element_type=F32)


def column_start(first, i, w_hbm):
    width = w_hbm.shape[0]
    return pl.multiple_of(lax.rem(first + i, w_hbm.shape[1] // width) * width, width)


def prep_kernel(
    index_ref, projected_hbm, filter_hbm, w_hbm, out_hbm, w_send, inputs, taps_in, turned, held, sems, w_sems
):
    blocks, quad, rows = turned.shape
    group = quad // 4
    width = w_hbm.shape[0]
    chunks = w_send.shape[1] // width
    arrive = [pltpu.make_async_copy(projected_hbm.at[part], inputs.at[part], sems.at[part]) for part in range(3)]
    arrive.append(pltpu.make_async_copy(filter_hbm, taps_in, sems.at[3]))
    for copy in arrive:
        copy.start()
    w_in, w_out = [], []
    for i in range(chunks):
        start = column_start(index_ref[2], i, w_hbm)
        columns = slice(i * width, (i + 1) * width)
        w_in.append(pltpu.make_async_copy(w_hbm.at[:, pl.ds(start, width)], held.at[:, columns], w_sems.at[i]))
        w_out.append(pltpu.make_async_copy(held.at[:, columns], w_send.at[:, columns], w_sems.at[chunks + i]))
        w_in[i].start()
    leave = []
    for part in range(4):
        arrive[part].wait()
        source = inputs[part] if part < 3 else taps_in[...].astype(BF16)
        lines = slice(part * group, (part + 1) * group)
        turned[:, lines, :] = source.T.reshape(blocks, group, rows)
        leave.append(pltpu.make_async_copy(turned.at[:, lines], out_hbm.at[:, lines], sems.at[4 + part]))
        leave[part].start()
    for i in range(chunks):
        w_in[i].wait()
        w_out[i].start()
    for copy in leave + w_out:
        copy.wait()


def featurize(recv_ref, taps_ref, query, gated):
    blocks, quad, width = recv_ref.shape
    group = quad // 4
    tile = 16
    batch = blocks
    lane = lax.broadcasted_iota(jnp.int32, (tile, LANES), 1)
    for c0 in range(0, group, tile):
        lines = slice(c0, c0 + tile)
        for part in (1, 2, 0):
            t = [
                jnp.broadcast_to(taps_ref[lines, part * TAPS + j : part * TAPS + j + 1], (tile, LANES))
                for j in range(TAPS)
            ]
            last = [jnp.zeros((tile, LANES), F32)] * 4
            first_row = part * group + c0
            for s0 in range(0, blocks, batch):
                places = [(s, lines, slice(l0, l0 + LANES)) for s in range(s0, s0 + batch) for l0 in range(0, width, LANES)]
                now = [recv_ref[s, first_row : first_row + tile, cols].astype(F32) for s, _, cols in places]
                gates = [gated[at] for at in places] if part == 2 else None

                def shifted(values, amount, which):
                    turns = [pltpu.roll(value, amount, 1) for value in values]
                    moved = [jnp.where(lane < amount, b, a) for b, a in zip([last[which]] + turns[:-1], turns)]
                    last[which] = turns[-1]
                    return moved

                one = shifted(now, 1, 0)
                two = shifted([t[2] * x + t[3] * y for x, y in zip(now, one)], 2, 1)
                four = shifted([t[4] * x + t[5] * y for x, y in zip(now, one)], 4, 2)
                six = shifted([t[6] * x for x in now], 6, 3)
                totals = [t[0] * x + t[1] * y + a + b + c for x, y, a, b, c in zip(now, one, two, four, six)]
                if part == 2:
                    totals = [g * total for g, total in zip(gates, totals)]
                for at, total in zip(places, totals):
                    (query if part == 0 else gated)[at] = total


def over_blocks(values, k, blocks):
    even_c = even_s = odd_c = odd_s = None
    for s, value in enumerate(values):
        c, t = math.cos(block_angle(s, k, blocks)), math.sin(block_angle(s, k, blocks))
        if s == 0:
            even_c = value
            continue
        term_c, term_s = value * c, value * t
        if s % 2 == 0:
            even_c = even_c + term_c
            even_s = term_s if even_s is None else even_s + term_s
        else:
            odd_c = term_c if odd_c is None else odd_c + term_c
            odd_s = term_s if odd_s is None else odd_s + term_s
    return (even_c + odd_c, -(even_s + odd_s)), (even_c - odd_c, even_s - odd_s)


def conv_kernel(
    recv_ref, taps_ref, tw_ref, tables_hbm, out_hbm, query, gated, high, low, spec_h, spec_u, mixed, tables, sems, out_sems
):
    blocks, quad, width = recv_ref.shape
    group = quad // 4
    tile = 16
    load = pltpu.make_async_copy(tables_hbm, tables, sems.at[0])
    load.start()
    featurize(recv_ref, taps_ref, query, gated)

    def table(which, term):
        start = (2 * which + term) * 2 * width
        return tables[start : start + 2 * width, :]

    def store_split(rows, cols, value):
        high[rows, cols], low[rows, cols] = split_bf16(value)

    def lanes(which):
        return dot(high[...], table(which, 0)) + dot(low[...], table(which, 0)) + dot(high[...], table(which, 1))

    def to_odd(block):
        for c0 in range(0, group, tile):
            for l0 in range(0, width, LANES):
                values = [block(s, c0, slice(l0, l0 + LANES)) for s in range(blocks)]
                for k in range(blocks // 2):
                    for kk, (re, im) in zip((k, blocks - 1 - k), over_blocks(values, k, blocks)):
                        tr = tw_ref[0, kk, :, l0 : l0 + LANES]
                        ti = tw_ref[1, kk, :, l0 : l0 + LANES]
                        rows = slice(kk * group + c0, kk * group + c0 + tile)
                        store_split(rows, slice(l0, l0 + LANES), re * tr - im * ti)
                        store_split(rows, slice(width + l0, width + l0 + LANES), re * ti + im * tr)

    to_odd(lambda s, c, p: recv_ref[s, 3 * group + c : 3 * group + c + tile, p].astype(F32))
    load.wait()
    spec_h[...] = lanes(0)
    to_odd(lambda s, c, p: gated[s, c : c + tile, p])
    spec_u[...] = lanes(0)

    hr, hi = spec_h[:, :width], spec_h[:, width:]
    ur, ui = spec_u[:, :width], spec_u[:, width:]
    store_split(slice(None), slice(0, width), hr * ur - hi * ui)
    store_split(slice(None), slice(width, 2 * width), hr * ui + hi * ur)
    spec_h[...] = lanes(1)

    scale = 1.0 / (blocks * width)
    half = blocks // 2
    for c0 in range(0, group, tile):
        skip = taps_ref[c0 : c0 + tile, 3 * TAPS : 3 * TAPS + 1]
        for l0 in range(0, width, LANES):
            reals, imags = [], []
            for k in range(blocks):
                rows = slice(k * group + c0, k * group + c0 + tile)
                tr = tw_ref[0, k, :, l0 : l0 + LANES] * scale
                ti = tw_ref[1, k, :, l0 : l0 + LANES] * scale
                re = spec_h[rows, l0 : l0 + LANES]
                im = spec_h[rows, width + l0 : width + l0 + LANES]
                reals.append(re * tr + im * ti)
                imags.append(im * tr - re * ti)
            sum_re = [reals[k] + reals[blocks - 1 - k] for k in range(half)]
            dif_re = [reals[k] - reals[blocks - 1 - k] for k in range(half)]
            sum_im = [imags[k] + imags[blocks - 1 - k] for k in range(half)]
            dif_im = [imags[k] - imags[blocks - 1 - k] for k in range(half)]
            for s in range(blocks):
                res, ims = (sum_re, dif_im) if s % 2 == 0 else (dif_re, sum_im)
                total = None
                for k in range(half):
                    angle = block_angle(s, k, blocks)
                    term = res[k] if s == 0 else res[k] * math.cos(angle) - ims[k] * math.sin(angle)
                    total = term if total is None else total + term
                at = (s, slice(c0, c0 + tile), slice(l0, l0 + LANES))
                mixed[at] = (query[at] * (total + skip * gated[at])).astype(BF16)
    copies = [pltpu.make_async_copy(mixed, out_hbm.at[twin], out_sems.at[twin]) for twin in range(2)]
    for copy in copies:
        copy.start()
    for copy in copies:
        copy.wait()


def project_kernel(index_ref, mixed_ref, w_hbm, other_ref, out_ref, own, sems):
    chunks, rows, width = out_ref.shape
    copies = []
    for i in range(chunks):
        start = column_start(index_ref[1], i, w_hbm)
        copies.append(
            pltpu.make_async_copy(w_hbm.at[:, pl.ds(start, width)], own.at[:, i * width : (i + 1) * width], sems.at[i])
        )
        copies[i].start()
    mine = index_ref[0]
    first = mixed_ref[mine].reshape(width, rows).T
    second = mixed_ref[1 - mine].reshape(width, rows).T
    for i in range(chunks):
        columns = slice(i * width, (i + 1) * width)
        total = dot(second, other_ref[:, columns])
        copies[i].wait()
        out_ref[i] = (total + dot(first, own[:, columns])).astype(BF16)


def local(projected, short_taps, long_filter, skip_gain, w_out):
    ctx, tp, dp = lax.axis_size("ctx"), lax.axis_size("tp"), lax.axis_size("dp")
    rows, width = projected.shape[1:]
    group = width // ctx
    me_ctx, me_tp, me_dp = lax.axis_index("ctx"), lax.axis_index("tp"), lax.axis_index("dp")

    half = tp // 2

    def plane(r, d):
        return (r + 2 * d) % tp

    pair_route = [(plane(r, d) * dp + d, plane(tp - 1 - r, d) * dp + d) for r in range(tp) for d in range(dp)]
    pair_groups = [
        [(c * tp + plane(r, d)) * dp + d for r in (first, tp - 1 - first) for c in range(ctx)]
        for d in range(dp)
        for first in range(half)
    ]
    quad_groups = [[plane(q * half + i, d) * dp + d for i in range(half)] for d in range(dp) for q in range(2)]
    chunks = half
    place = lax.rem(me_tp - 2 * me_dp + 2 * tp, tp) // half
    own_first = lax.rem(place * half + 2 * me_dp, tp)
    other_first = lax.rem((1 - place) * half + 2 * me_dp, tp)
    index = jnp.stack([place, own_first, other_first]).astype(jnp.int32)

    vmem = pl.BlockSpec(memory_space=pltpu.VMEM)
    smem = pl.BlockSpec(memory_space=pltpu.SMEM)
    hbm = pl.BlockSpec(memory_space=pl.ANY)
    params = pltpu.CompilerParams(vmem_limit_bytes=60 * MIB)

    send, w_send = pl.pallas_call(
        prep_kernel,
        in_specs=[smem, hbm, hbm, hbm],
        out_specs=[hbm, hbm],
        out_shape=[
            jax.ShapeDtypeStruct((ctx, 4 * group, rows), BF16),
            jax.ShapeDtypeStruct((width, chunks * width), BF16),
        ],
        scratch_shapes=[
            pltpu.VMEM((3, rows, width), BF16),
            pltpu.VMEM((rows, width), F32),
            pltpu.VMEM((ctx, 4 * group, rows), BF16),
            pltpu.VMEM((width, chunks * width), BF16),
            pltpu.SemaphoreType.DMA((8,)),
            pltpu.SemaphoreType.DMA((2 * chunks,)),
        ],
        compiler_params=params,
        name="prep",
    )(index, projected, long_filter, w_out)
    recv = lax.all_to_all(send, "ctx", 0, 0, tiled=True)
    w_other = lax.ppermute(w_send, ("tp", "dp"), pair_route)

    taps = jnp.concatenate([short_taps.reshape(3 * TAPS, width), skip_gain[None, :]], axis=0)
    taps = lax.dynamic_slice_in_dim(taps, me_ctx * group, group, axis=1).T
    tables = lane_tables(rows)
    mixed = pl.pallas_call(
        conv_kernel,
        in_specs=[vmem, vmem, vmem, hbm],
        out_specs=hbm,
        out_shape=jax.ShapeDtypeStruct((2, ctx, group, rows), BF16),
        scratch_shapes=[
            pltpu.VMEM((ctx, group, rows), F32),
            pltpu.VMEM((ctx, group, rows), F32),
            pltpu.VMEM((ctx * group, 2 * rows), BF16),
            pltpu.VMEM((ctx * group, 2 * rows), BF16),
            pltpu.VMEM((ctx * group, 2 * rows), F32),
            pltpu.VMEM((ctx * group, 2 * rows), F32),
            pltpu.VMEM((ctx, group, rows), BF16),
            pltpu.VMEM(tables.shape, BF16),
            pltpu.SemaphoreType.DMA((1,)),
            pltpu.SemaphoreType.DMA((2,)),
        ],
        compiler_params=pltpu.CompilerParams(vmem_limit_bytes=52 * MIB),
        name="conv",
    )(recv, taps, jnp.asarray(twiddles(ctx, rows)), jnp.asarray(tables))
    mixed = lax.all_to_all(
        mixed.reshape(2 * ctx, group, rows), ("ctx", "tp", "dp"), 0, 0, tiled=True, axis_index_groups=pair_groups
    ).reshape(2, ctx, group, rows)

    partial = pl.pallas_call(
        project_kernel,
        in_specs=[smem, vmem, hbm, vmem],
        out_specs=vmem,
        out_shape=jax.ShapeDtypeStruct((chunks, rows, width), BF16),
        scratch_shapes=[
            pltpu.VMEM((width, chunks * width), BF16),
            pltpu.SemaphoreType.DMA((chunks,)),
        ],
        compiler_params=pltpu.CompilerParams(vmem_limit_bytes=48 * MIB),
        name="project",
    )(index, mixed, w_out, w_other)
    gathered = lax.all_to_all(partial, ("tp", "dp"), 0, 0, tiled=True, axis_index_groups=quad_groups)
    return jnp.sum(gathered.astype(F32), axis=0).astype(BF16)


def solution(mesh):
    in_specs = (
        P(None, ("dp", "ctx"), "tp"),
        P(None, None, "tp"),
        P("ctx", "tp"),
        P("tp"),
        P("tp", None),
    )
    out_specs = P(("dp", "ctx"), "tp")
    return jax.shard_map(local, mesh=mesh, in_specs=in_specs, out_specs=out_specs, check_vma=False)
```

```python
import functools
import math

import jax
import jax.numpy as jnp
import numpy as np
from jax import lax
from jax.experimental import pallas as pl
from jax.experimental.pallas import tpu as pltpu
from jax.sharding import PartitionSpec as P

TAPS = 7
LANES = 128
BF16 = jnp.bfloat16
F32 = jnp.float32
MIB = 1024 * 1024


def split_table(table):
    high = table.astype(np.float32).astype(jnp.bfloat16)
    low = (table - high.astype(np.float64)).astype(np.float32).astype(jnp.bfloat16)
    return np.stack([high, low])


def lane_tables(width):
    angle = 2.0 * np.pi * (np.outer(np.arange(width), np.arange(width)) % width) / width
    cos, sin = np.cos(angle), np.sin(angle)
    forward = np.block([[cos, -sin], [sin, cos]])
    return np.concatenate([split_table(table).reshape(-1, 2 * width) for table in (forward, forward.T)])


def twiddles(blocks, width):
    angle = 2.0 * np.pi * np.outer(np.arange(blocks) + 0.5, np.arange(width)) / (2 * blocks * width)
    return np.stack([np.cos(angle), -np.sin(angle)]).astype(np.float32)[:, :, None, :]


def block_angle(s, k, blocks):
    return math.pi * ((s * (2 * k + 1)) % (4 * blocks)) / (2 * blocks)


def split_bf16(values):
    high = values.astype(BF16)
    return high, (values - high.astype(F32)).astype(BF16)


def dot(a, b):
    return jnp.dot(a, b, preferred_element_type=F32)


def column_start(place_ref, i, w_hbm, other=False):
    width = w_hbm.shape[0]
    chunks = w_hbm.shape[1] // width
    core, ring = lax.rem(place_ref[0], 2), place_ref[0] // 2
    mine = ring // 2
    side = (lax.rem(ring, 2) + (2 * mine >= chunks // 2).astype(jnp.int32) + int(other)) % 2
    upper = (2 * jnp.asarray(i, jnp.int32) >= chunks // 2).astype(jnp.int32)
    return pl.multiple_of(lax.rem(2 * i + lax.rem(side + upper, 2) + core, chunks) * width, width)


def prep_kernel(
    place_ref, projected_hbm, filter_hbm, w_hbm, out_hbm, w_send, inputs, taps_in, turned, held, sems, w_sems
):
    blocks, quad, rows = turned.shape
    group = quad // 4
    width = w_hbm.shape[0]
    chunks = w_send.shape[1] // width
    arrive = [pltpu.make_async_copy(projected_hbm.at[part], inputs.at[part], sems.at[part]) for part in range(3)]
    arrive.append(pltpu.make_async_copy(filter_hbm, taps_in, sems.at[3]))
    for copy in arrive:
        copy.start()
    w_in, w_out = [], []
    for i in range(chunks):
        start = column_start(place_ref, i, w_hbm, other=True)
        columns = slice(i * width, (i + 1) * width)
        w_in.append(pltpu.make_async_copy(w_hbm.at[:, pl.ds(start, width)], held.at[:, columns], w_sems.at[i]))
        w_out.append(pltpu.make_async_copy(held.at[:, columns], w_send.at[:, columns], w_sems.at[chunks + i]))
        w_in[i].start()
    leave = []
    for part in range(4):
        arrive[part].wait()
        source = inputs[part] if part < 3 else taps_in[...].astype(BF16)
        lines = slice(part * group, (part + 1) * group)
        turned[:, lines, :] = source.T.reshape(blocks, group, rows)
        leave.append(pltpu.make_async_copy(turned.at[:, lines], out_hbm.at[:, lines], sems.at[4 + part]))
        leave[part].start()
    for i in range(chunks):
        w_in[i].wait()
        w_out[i].start()
    for copy in leave + w_out:
        copy.wait()


def featurize(recv_ref, taps_ref, query, gated):
    blocks, quad, width = recv_ref.shape
    group = quad // 4
    tile = 16
    batch = blocks
    lane = lax.broadcasted_iota(jnp.int32, (tile, LANES), 1)
    for c0 in range(0, group, tile):
        lines = slice(c0, c0 + tile)
        for part in (1, 2, 0):
            t = [
                jnp.broadcast_to(taps_ref[lines, part * TAPS + j : part * TAPS + j + 1], (tile, LANES))
                for j in range(TAPS)
            ]
            last = [jnp.zeros((tile, LANES), F32)] * 4
            first_row = part * group + c0
            for s0 in range(0, blocks, batch):
                places = [(s, lines, slice(l0, l0 + LANES)) for s in range(s0, s0 + batch) for l0 in range(0, width, LANES)]
                now = [recv_ref[s, first_row : first_row + tile, cols].astype(F32) for s, _, cols in places]
                gates = [gated[at] for at in places] if part == 2 else None

                def shifted(values, amount, which):
                    turns = [pltpu.roll(value, amount, 1) for value in values]
                    moved = [jnp.where(lane < amount, b, a) for b, a in zip([last[which]] + turns[:-1], turns)]
                    last[which] = turns[-1]
                    return moved

                one = shifted(now, 1, 0)
                two = shifted([t[2] * x + t[3] * y for x, y in zip(now, one)], 2, 1)
                four = shifted([t[4] * x + t[5] * y for x, y in zip(now, one)], 4, 2)
                six = shifted([t[6] * x for x in now], 6, 3)
                totals = [t[0] * x + t[1] * y + a + b + c for x, y, a, b, c in zip(now, one, two, four, six)]
                if part == 2:
                    totals = [g * total for g, total in zip(gates, totals)]
                for at, total in zip(places, totals):
                    (query if part == 0 else gated)[at] = total


def over_blocks(values, k, blocks):
    even_c = even_s = odd_c = odd_s = None
    for s, value in enumerate(values):
        c, t = math.cos(block_angle(s, k, blocks)), math.sin(block_angle(s, k, blocks))
        if s == 0:
            even_c = value
            continue
        term_c, term_s = value * c, value * t
        if s % 2 == 0:
            even_c = even_c + term_c
            even_s = term_s if even_s is None else even_s + term_s
        else:
            odd_c = term_c if odd_c is None else odd_c + term_c
            odd_s = term_s if odd_s is None else odd_s + term_s
    return (even_c + odd_c, -(even_s + odd_s)), (even_c - odd_c, even_s - odd_s)


def conv_kernel(
    recv_ref, taps_ref, tw_ref, tables_hbm, out_hbm, query, gated, high, low, spec_h, spec_u, mixed, tables, sems, out_sems
):
    blocks, quad, width = recv_ref.shape
    group = quad // 4
    tile = 16
    load = pltpu.make_async_copy(tables_hbm, tables, sems.at[0])
    load.start()
    featurize(recv_ref, taps_ref, query, gated)

    def table(which, term):
        start = (2 * which + term) * 2 * width
        return tables[start : start + 2 * width, :]

    def store_split(rows, cols, value):
        high[rows, cols], low[rows, cols] = split_bf16(value)

    def lanes(which):
        return dot(high[...], table(which, 0)) + dot(low[...], table(which, 0)) + dot(high[...], table(which, 1))

    def to_odd(block):
        for c0 in range(0, group, tile):
            for l0 in range(0, width, LANES):
                values = [block(s, c0, slice(l0, l0 + LANES)) for s in range(blocks)]
                for k in range(blocks // 2):
                    for kk, (re, im) in zip((k, blocks - 1 - k), over_blocks(values, k, blocks)):
                        tr = tw_ref[0, kk, :, l0 : l0 + LANES]
                        ti = tw_ref[1, kk, :, l0 : l0 + LANES]
                        rows = slice(kk * group + c0, kk * group + c0 + tile)
                        store_split(rows, slice(l0, l0 + LANES), re * tr - im * ti)
                        store_split(rows, slice(width + l0, width + l0 + LANES), re * ti + im * tr)

    to_odd(lambda s, c, p: recv_ref[s, 3 * group + c : 3 * group + c + tile, p].astype(F32))
    load.wait()
    spec_h[...] = lanes(0)
    to_odd(lambda s, c, p: gated[s, c : c + tile, p])
    spec_u[...] = lanes(0)

    hr, hi = spec_h[:, :width], spec_h[:, width:]
    ur, ui = spec_u[:, :width], spec_u[:, width:]
    store_split(slice(None), slice(0, width), hr * ur - hi * ui)
    store_split(slice(None), slice(width, 2 * width), hr * ui + hi * ur)
    spec_h[...] = lanes(1)

    scale = 1.0 / (blocks * width)
    half = blocks // 2
    for c0 in range(0, group, tile):
        skip = taps_ref[c0 : c0 + tile, 3 * TAPS : 3 * TAPS + 1]
        for l0 in range(0, width, LANES):
            reals, imags = [], []
            for k in range(blocks):
                rows = slice(k * group + c0, k * group + c0 + tile)
                tr = tw_ref[0, k, :, l0 : l0 + LANES] * scale
                ti = tw_ref[1, k, :, l0 : l0 + LANES] * scale
                re = spec_h[rows, l0 : l0 + LANES]
                im = spec_h[rows, width + l0 : width + l0 + LANES]
                reals.append(re * tr + im * ti)
                imags.append(im * tr - re * ti)
            sum_re = [reals[k] + reals[blocks - 1 - k] for k in range(half)]
            dif_re = [reals[k] - reals[blocks - 1 - k] for k in range(half)]
            sum_im = [imags[k] + imags[blocks - 1 - k] for k in range(half)]
            dif_im = [imags[k] - imags[blocks - 1 - k] for k in range(half)]
            for s in range(blocks):
                res, ims = (sum_re, dif_im) if s % 2 == 0 else (dif_re, sum_im)
                total = None
                for k in range(half):
                    angle = block_angle(s, k, blocks)
                    term = res[k] if s == 0 else res[k] * math.cos(angle) - ims[k] * math.sin(angle)
                    total = term if total is None else total + term
                at = (s, slice(c0, c0 + tile), slice(l0, l0 + LANES))
                mixed[at] = (query[at] * (total + skip * gated[at])).astype(BF16)
    copies = [pltpu.make_async_copy(mixed, out_hbm.at[twin], out_sems.at[twin]) for twin in range(2)]
    for copy in copies:
        copy.start()
    for copy in copies:
        copy.wait()


def project_kernel(steps, first, place_ref, mixed_ref, w_hbm, other_ref, *refs):
    outs, (own, sems) = refs[:-2], refs[-2:]
    width = w_hbm.shape[0]
    index = place_ref[0] // 4
    copies = []
    for n, step in enumerate(steps):
        start = column_start(place_ref, index ^ step, w_hbm)
        copies.append(pltpu.make_async_copy(w_hbm.at[:, pl.ds(start, width)], own.at[n], sems.at[n]))
        copies[n].start()
    if first:
        turned = outs[-1]
        rows = turned.shape[1]
        mine = lax.rem(place_ref[0] // 2, 2)
        turned[0] = mixed_ref[mine].reshape(width, rows).T
        turned[1] = mixed_ref[1 - mine].reshape(width, rows).T
    else:
        turned = mixed_ref
    for n, step in enumerate(steps):
        start = pl.multiple_of((index ^ step) * width, width)
        total = dot(turned[1], other_ref[:, pl.ds(start, width)])
        copies[n].wait()
        outs[n][...] = (total + dot(turned[0], own[n])).astype(outs[n].dtype)


def sum_kernel(own_ref, *refs):
    total = own_ref[...]
    for ref in refs[:-1]:
        total = total + ref[...].astype(F32)
    refs[-1][...] = total.astype(BF16)


def local(projected, short_taps, long_filter, skip_gain, w_out):
    ctx, tp, dp = lax.axis_size("ctx"), lax.axis_size("tp"), lax.axis_size("dp")
    rows, width = projected.shape[1:]
    group = width // ctx
    me_ctx, me_tp, me_dp = lax.axis_index("ctx"), lax.axis_index("tp"), lax.axis_index("dp")

    chunks = tp // 2

    def quad_place(q, i):
        return 2 * i + (q + (2 * i >= tp // 2)) % 2

    def device(r, d):
        return (r + d) % tp * dp + d

    pair_route = [(device(r, d), device(r ^ 1, d)) for r in range(tp) for d in range(dp)]
    pair_groups = [[c * tp * dp + device(r, d) for r in (2 * i, 2 * i + 1) for c in range(ctx)] for d in range(dp) for i in range(chunks)]
    quads = [[device(quad_place(q, i), d) for i in range(chunks)] for d in range(dp) for q in range(2)]
    place = (lax.rem(me_tp - me_dp + tp, tp) * 2 + me_dp).astype(jnp.int32)[None]

    vmem = pl.BlockSpec(memory_space=pltpu.VMEM)
    smem = pl.BlockSpec(memory_space=pltpu.SMEM)
    hbm = pl.BlockSpec(memory_space=pl.ANY)
    params = pltpu.CompilerParams(vmem_limit_bytes=60 * MIB)

    send, w_send = pl.pallas_call(
        prep_kernel,
        in_specs=[smem, hbm, hbm, hbm],
        out_specs=[hbm, hbm],
        out_shape=[
            jax.ShapeDtypeStruct((ctx, 4 * group, rows), BF16),
            jax.ShapeDtypeStruct((width, chunks * width), BF16),
        ],
        scratch_shapes=[
            pltpu.VMEM((3, rows, width), BF16),
            pltpu.VMEM((rows, width), F32),
            pltpu.VMEM((ctx, 4 * group, rows), BF16),
            pltpu.VMEM((width, chunks * width), BF16),
            pltpu.SemaphoreType.DMA((8,)),
            pltpu.SemaphoreType.DMA((2 * chunks,)),
        ],
        compiler_params=params,
        name="prep",
    )(place, projected, long_filter, w_out)
    recv = lax.all_to_all(send, "ctx", 0, 0, tiled=True)
    w_other = lax.ppermute(w_send, ("tp", "dp"), pair_route)

    taps = jnp.concatenate([short_taps.reshape(3 * TAPS, width), skip_gain[None, :]], axis=0)
    taps = lax.dynamic_slice_in_dim(taps, me_ctx * group, group, axis=1).T
    tables = lane_tables(rows)
    mixed = pl.pallas_call(
        conv_kernel,
        in_specs=[vmem, vmem, vmem, hbm],
        out_specs=hbm,
        out_shape=jax.ShapeDtypeStruct((2, ctx, group, rows), BF16),
        scratch_shapes=[
            pltpu.VMEM((ctx, group, rows), F32),
            pltpu.VMEM((ctx, group, rows), F32),
            pltpu.VMEM((ctx * group, 2 * rows), BF16),
            pltpu.VMEM((ctx * group, 2 * rows), BF16),
            pltpu.VMEM((ctx * group, 2 * rows), F32),
            pltpu.VMEM((ctx * group, 2 * rows), F32),
            pltpu.VMEM((ctx, group, rows), BF16),
            pltpu.VMEM(tables.shape, BF16),
            pltpu.SemaphoreType.DMA((1,)),
            pltpu.SemaphoreType.DMA((2,)),
        ],
        compiler_params=pltpu.CompilerParams(vmem_limit_bytes=52 * MIB),
        name="conv",
    )(recv, taps, jnp.asarray(twiddles(ctx, rows)), jnp.asarray(tables))
    mixed = lax.all_to_all(
        mixed.reshape(2 * ctx, group, rows), ("ctx", "tp", "dp"), 0, 0, tiled=True, axis_index_groups=pair_groups
    ).reshape(2, ctx, group, rows)

    def project(steps, operand, kind):
        first = operand is mixed
        block = jax.ShapeDtypeStruct((rows, width), kind)
        extra = [jax.ShapeDtypeStruct((2, rows, width), BF16)] if first else []
        return pl.pallas_call(
            functools.partial(project_kernel, steps, first),
            in_specs=[smem, vmem, hbm, vmem],
            out_specs=[vmem for _ in steps] + [vmem] * len(extra),
            out_shape=[block] * len(steps) + extra,
            scratch_shapes=[pltpu.VMEM((len(steps), width, width), BF16), pltpu.SemaphoreType.DMA((len(steps),))],
            compiler_params=pltpu.CompilerParams(vmem_limit_bytes=48 * MIB),
            name="project",
        )(place, operand, w_out, w_other)

    def passed(block, step):
        return lax.ppermute(block, ("tp", "dp"), [(quad[i], quad[i ^ step]) for quad in quads for i in range(chunks)])

    far, turned = project((3,), mixed, BF16)
    parts = [passed(far, 3)]
    near = project((1, 2), turned, BF16)
    parts += [passed(block, step) for block, step in zip(near, (1, 2))]
    (own,) = project((0,), turned, F32)
    return pl.pallas_call(
        sum_kernel,
        in_specs=[vmem] * 4,
        out_shape=jax.ShapeDtypeStruct((rows, width), BF16),
        compiler_params=pltpu.CompilerParams(vmem_limit_bytes=48 * MIB),
        name="sum",
    )(own, *parts)


def solution(mesh):
    in_specs = (
        P(None, ("dp", "ctx"), "tp"),
        P(None, None, "tp"),
        P("ctx", "tp"),
        P("tp"),
        P("tp", None),
    )
    out_specs = P(("dp", "ctx"), "tp")
    return jax.shard_map(local, mesh=mesh, in_specs=in_specs, out_specs=out_specs, check_vma=False)
```

```python
import functools
import math

import jax
import jax.numpy as jnp
import numpy as np
from jax import lax
from jax.experimental import pallas as pl
from jax.experimental.pallas import tpu as pltpu
from jax.sharding import PartitionSpec as P

TAPS = 7
LANES = 128
HALO = 16
BF16 = jnp.bfloat16
F32 = jnp.float32
MIB = 1024 * 1024


def split_table(table):
    high = table.astype(np.float32).astype(jnp.bfloat16)
    low = (table - high.astype(np.float64)).astype(np.float32).astype(jnp.bfloat16)
    return np.stack([high, low])


def lane_tables(width):
    angle = 2.0 * np.pi * (np.outer(np.arange(width), np.arange(width)) % width) / width
    cos, sin = np.cos(angle), np.sin(angle)
    forward = np.block([[cos, -sin], [sin, cos]])
    return np.concatenate([split_table(table).reshape(-1, 2 * width) for table in (forward, forward.T)])


def twiddles(blocks, width):
    angle = 2.0 * np.pi * np.outer(np.arange(blocks) + 0.5, np.arange(width)) / (2 * blocks * width)
    return np.stack([np.cos(angle), -np.sin(angle)]).astype(np.float32)[:, :, None, :]


def block_angle(s, k, blocks):
    return math.pi * ((s * (2 * k + 1)) % (4 * blocks)) / (2 * blocks)


def split_bf16(values):
    high = values.astype(BF16)
    return high, (values - high.astype(F32)).astype(BF16)


def dot(a, b):
    return jnp.dot(a, b, preferred_element_type=F32)


def column_start(place_ref, i, w_hbm, other=False):
    width = w_hbm.shape[0]
    chunks = w_hbm.shape[1] // width
    core, ring = lax.rem(place_ref[0], 2), place_ref[0] // 2
    mine = ring // 2
    side = (lax.rem(ring, 2) + (2 * mine >= chunks // 2).astype(jnp.int32) + int(other)) % 2
    upper = (2 * jnp.asarray(i, jnp.int32) >= chunks // 2).astype(jnp.int32)
    return pl.multiple_of(lax.rem(2 * i + lax.rem(side + upper, 2) + core, chunks) * width, width)


def prep_kernel(place_ref, projected_hbm, filter_hbm, w_hbm, out_hbm, w_send, inputs, taps_in, turned, held, sems, w_sems):
    blocks, lines, rows = turned.shape
    group = lines // 3
    width = w_hbm.shape[0]
    chunks = w_send.shape[1] // width
    arrive = [pltpu.make_async_copy(projected_hbm.at[1 + part], inputs.at[part], sems.at[part]) for part in range(2)]
    arrive.append(pltpu.make_async_copy(filter_hbm, taps_in, sems.at[2]))
    for copy in arrive:
        copy.start()
    w_in, w_out = [], []
    for i in range(chunks):
        start = column_start(place_ref, i, w_hbm, other=True)
        columns = slice(i * width, (i + 1) * width)
        w_in.append(pltpu.make_async_copy(w_hbm.at[:, pl.ds(start, width)], held.at[:, columns], w_sems.at[i]))
        w_out.append(pltpu.make_async_copy(held.at[:, columns], w_send.at[:, columns], w_sems.at[chunks + i]))
        w_in[i].start()
    leave = []
    for part in range(3):
        arrive[part].wait()
        source = inputs[part] if part < 2 else taps_in[...].astype(BF16)
        at = slice(part * group, (part + 1) * group)
        turned[:, at, :] = source.T.reshape(blocks, group, rows)
        leave.append(pltpu.make_async_copy(turned.at[:, at], out_hbm.at[:, at], sems.at[3 + part]))
        leave[part].start()
    for i in range(chunks):
        w_in[i].wait()
        w_out[i].start()
    for copy in leave + w_out:
        copy.wait()


def query_kernel(now_ref, before_ref, taps_ref, out_ref, whole):
    rows = out_ref.shape[0]
    halo = before_ref.shape[0]
    whole[:halo] = before_ref[...].astype(F32)
    whole[halo:] = now_ref[...].astype(F32)
    total = taps_ref[0, 0:1, :] * whole[halo:]
    for j in range(1, TAPS):
        total = total + taps_ref[0, j : j + 1, :] * whole[pl.ds(halo - j, rows), :]
    out_ref[...] = total


def featurize(recv_ref, taps_ref, gated):
    blocks, lines_all, width = recv_ref.shape
    group = lines_all // 3
    tile = 16
    batch = blocks
    lane = lax.broadcasted_iota(jnp.int32, (tile, LANES), 1)
    for c0 in range(0, group, tile):
        lines = slice(c0, c0 + tile)
        for part in (1, 2):
            t = [
                jnp.broadcast_to(taps_ref[lines, part * TAPS + j : part * TAPS + j + 1], (tile, LANES))
                for j in range(TAPS)
            ]
            last = [jnp.zeros((tile, LANES), F32)] * 4
            first_row = (part - 1) * group + c0
            for s0 in range(0, blocks, batch):
                places = [(s, lines, slice(l0, l0 + LANES)) for s in range(s0, s0 + batch) for l0 in range(0, width, LANES)]
                now = [recv_ref[s, first_row : first_row + tile, cols].astype(F32) for s, _, cols in places]
                gates = [gated[at] for at in places] if part == 2 else None

                def shifted(values, amount, which):
                    turns = [pltpu.roll(value, amount, 1) for value in values]
                    moved = [jnp.where(lane < amount, b, a) for b, a in zip([last[which]] + turns[:-1], turns)]
                    last[which] = turns[-1]
                    return moved

                one = shifted(now, 1, 0)
                two = shifted([t[2] * x + t[3] * y for x, y in zip(now, one)], 2, 1)
                four = shifted([t[4] * x + t[5] * y for x, y in zip(now, one)], 4, 2)
                six = shifted([t[6] * x for x in now], 6, 3)
                totals = [t[0] * x + t[1] * y + a + b + c for x, y, a, b, c in zip(now, one, two, four, six)]
                if part == 2:
                    totals = [g * total for g, total in zip(gates, totals)]
                for at, total in zip(places, totals):
                    gated[at] = total


def over_blocks(values, k, blocks):
    even_c = even_s = odd_c = odd_s = None
    for s, value in enumerate(values):
        c, t = math.cos(block_angle(s, k, blocks)), math.sin(block_angle(s, k, blocks))
        if s == 0:
            even_c = value
            continue
        term_c, term_s = value * c, value * t
        if s % 2 == 0:
            even_c = even_c + term_c
            even_s = term_s if even_s is None else even_s + term_s
        else:
            odd_c = term_c if odd_c is None else odd_c + term_c
            odd_s = term_s if odd_s is None else odd_s + term_s
    return (even_c + odd_c, -(even_s + odd_s)), (even_c - odd_c, even_s - odd_s)


def conv_kernel(
    recv_ref, taps_ref, tw_ref, tables_hbm, out_ref, gated, high, low, spec_h, spec_u, tables, sems
):
    blocks, lines_all, width = recv_ref.shape
    group = lines_all // 3
    tile = 16
    load = pltpu.make_async_copy(tables_hbm, tables, sems.at[0])
    load.start()
    featurize(recv_ref, taps_ref, gated)

    def table(which, term):
        start = (2 * which + term) * 2 * width
        return tables[start : start + 2 * width, :]

    def store_split(rows, cols, value):
        high[rows, cols], low[rows, cols] = split_bf16(value)

    def lanes(which):
        return dot(high[...], table(which, 0)) + dot(low[...], table(which, 0)) + dot(high[...], table(which, 1))

    def to_odd(block):
        for c0 in range(0, group, tile):
            for l0 in range(0, width, LANES):
                values = [block(s, c0, slice(l0, l0 + LANES)) for s in range(blocks)]
                for k in range(blocks // 2):
                    for kk, (re, im) in zip((k, blocks - 1 - k), over_blocks(values, k, blocks)):
                        tr = tw_ref[0, kk, :, l0 : l0 + LANES]
                        ti = tw_ref[1, kk, :, l0 : l0 + LANES]
                        rows = slice(kk * group + c0, kk * group + c0 + tile)
                        store_split(rows, slice(l0, l0 + LANES), re * tr - im * ti)
                        store_split(rows, slice(width + l0, width + l0 + LANES), re * ti + im * tr)

    to_odd(lambda s, c, p: recv_ref[s, 2 * group + c : 2 * group + c + tile, p].astype(F32))
    load.wait()
    spec_h[...] = lanes(0)
    to_odd(lambda s, c, p: gated[s, c : c + tile, p])
    spec_u[...] = lanes(0)

    hr, hi = spec_h[:, :width], spec_h[:, width:]
    ur, ui = spec_u[:, :width], spec_u[:, width:]
    store_split(slice(None), slice(0, width), hr * ur - hi * ui)
    store_split(slice(None), slice(width, 2 * width), hr * ui + hi * ur)
    spec_h[...] = lanes(1)

    scale = 1.0 / (blocks * width)
    half = blocks // 2
    for c0 in range(0, group, tile):
        skip = taps_ref[c0 : c0 + tile, 3 * TAPS : 3 * TAPS + 1]
        for l0 in range(0, width, LANES):
            reals, imags = [], []
            for k in range(blocks):
                rows = slice(k * group + c0, k * group + c0 + tile)
                tr = tw_ref[0, k, :, l0 : l0 + LANES] * scale
                ti = tw_ref[1, k, :, l0 : l0 + LANES] * scale
                re = spec_h[rows, l0 : l0 + LANES]
                im = spec_h[rows, width + l0 : width + l0 + LANES]
                reals.append(re * tr + im * ti)
                imags.append(im * tr - re * ti)
            sum_re = [reals[k] + reals[blocks - 1 - k] for k in range(half)]
            dif_re = [reals[k] - reals[blocks - 1 - k] for k in range(half)]
            sum_im = [imags[k] + imags[blocks - 1 - k] for k in range(half)]
            dif_im = [imags[k] - imags[blocks - 1 - k] for k in range(half)]
            for s in range(blocks):
                res, ims = (sum_re, dif_im) if s % 2 == 0 else (dif_re, sum_im)
                total = None
                for k in range(half):
                    angle = block_angle(s, k, blocks)
                    term = res[k] if s == 0 else res[k] * math.cos(angle) - ims[k] * math.sin(angle)
                    total = term if total is None else total + term
                at = (s, slice(c0, c0 + tile), slice(l0, l0 + LANES))
                out_ref[at] = (total + skip * gated[at]).astype(BF16)


def mix_kernel(conv_ref, query_ref, out_ref):
    rows, width = query_ref.shape
    turned = conv_ref[...].reshape(width, rows).T
    out_ref[...] = (query_ref[...] * turned.astype(F32)).astype(BF16)


def own_kernel(place_ref, mixed_ref, w_hbm, out_ref, own, sems):
    width = w_hbm.shape[0]
    index = place_ref[0] // 4
    copies = []
    for step in range(own.shape[0]):
        start = column_start(place_ref, index ^ step, w_hbm)
        copies.append(pltpu.make_async_copy(w_hbm.at[:, pl.ds(start, width)], own.at[step], sems.at[step]))
        copies[step].start()
    for step in reversed(range(own.shape[0])):
        copies[step].wait()
        out_ref[step] = dot(mixed_ref[...], own[step])


def other_kernel(steps, place_ref, mixed_ref, own_ref, other_ref, *outs):
    width = other_ref.shape[0]
    index = place_ref[0] // 4
    for step, out in zip(steps, outs):
        start = pl.multiple_of((index ^ step) * width, width)
        out[...] = (own_ref[step] + dot(mixed_ref[...], other_ref[:, pl.ds(start, width)])).astype(out.dtype)


def sum_kernel(own_ref, *refs):
    total = own_ref[...]
    for ref in refs[:-1]:
        total = total + ref[...].astype(F32)
    refs[-1][...] = total.astype(BF16)


def local(projected, short_taps, long_filter, skip_gain, w_out):
    ctx, tp, dp = lax.axis_size("ctx"), lax.axis_size("tp"), lax.axis_size("dp")
    rows, width = projected.shape[1:]
    group = width // ctx
    me_ctx, me_tp, me_dp = lax.axis_index("ctx"), lax.axis_index("tp"), lax.axis_index("dp")

    chunks = tp // 2

    def quad_place(q, i):
        return 2 * i + (q + (2 * i >= tp // 2)) % 2

    def device(r, d):
        return (r + d) % tp * dp + d

    pair_route = [(device(r, d), device(r ^ 1, d)) for r in range(tp) for d in range(dp)]
    quads = [[device(quad_place(q, i), d) for i in range(chunks)] for d in range(dp) for q in range(2)]
    place = (lax.rem(me_tp - me_dp + tp, tp) * 2 + me_dp).astype(jnp.int32)[None]

    vmem = pl.BlockSpec(memory_space=pltpu.VMEM)
    smem = pl.BlockSpec(memory_space=pltpu.SMEM)
    hbm = pl.BlockSpec(memory_space=pl.ANY)
    params = pltpu.CompilerParams(vmem_limit_bytes=60 * MIB)

    send, w_send = pl.pallas_call(
        prep_kernel,
        in_specs=[smem, hbm, hbm, hbm],
        out_specs=[hbm, hbm],
        out_shape=[
            jax.ShapeDtypeStruct((ctx, 3 * group, rows), BF16),
            jax.ShapeDtypeStruct((width, chunks * width), BF16),
        ],
        scratch_shapes=[
            pltpu.VMEM((2, rows, width), BF16),
            pltpu.VMEM((rows, width), F32),
            pltpu.VMEM((ctx, 3 * group, rows), BF16),
            pltpu.VMEM((width, chunks * width), BF16),
            pltpu.SemaphoreType.DMA((6,)),
            pltpu.SemaphoreType.DMA((2 * chunks,)),
        ],
        compiler_params=params,
        name="prep",
    )(place, projected, long_filter, w_out)
    recv = lax.all_to_all(send, "ctx", 0, 0, tiled=True)
    w_other = lax.ppermute(w_send, ("tp", "dp"), pair_route)

    before = lax.ppermute(projected[0, rows - HALO :], "ctx", [(i, i + 1) for i in range(ctx - 1)])
    query = pl.pallas_call(
        query_kernel,
        in_specs=[vmem] * 3,
        out_specs=vmem,
        out_shape=jax.ShapeDtypeStruct((rows, width), F32),
        scratch_shapes=[pltpu.VMEM((HALO + rows, width), F32)],
        compiler_params=pltpu.CompilerParams(vmem_limit_bytes=48 * MIB),
        name="query",
    )(projected[0], before, short_taps)

    taps = jnp.concatenate([short_taps.reshape(3 * TAPS, width), skip_gain[None, :]], axis=0)
    taps = lax.dynamic_slice_in_dim(taps, me_ctx * group, group, axis=1).T
    taps, query = lax.optimization_barrier((taps, query))
    tables = lane_tables(rows)
    conv = pl.pallas_call(
        conv_kernel,
        in_specs=[vmem, vmem, vmem, hbm],
        out_specs=vmem,
        out_shape=jax.ShapeDtypeStruct((ctx, group, rows), BF16),
        scratch_shapes=[
            pltpu.VMEM((ctx, group, rows), F32),
            pltpu.VMEM((ctx * group, 2 * rows), BF16),
            pltpu.VMEM((ctx * group, 2 * rows), BF16),
            pltpu.VMEM((ctx * group, 2 * rows), F32),
            pltpu.VMEM((ctx * group, 2 * rows), F32),
            pltpu.VMEM(tables.shape, BF16),
            pltpu.SemaphoreType.DMA((1,)),
        ],
        compiler_params=pltpu.CompilerParams(vmem_limit_bytes=52 * MIB),
        name="conv",
    )(recv, taps, jnp.asarray(twiddles(ctx, rows)), jnp.asarray(tables))
    conv = lax.all_to_all(conv, "ctx", 0, 0, tiled=True)

    small = pltpu.CompilerParams(vmem_limit_bytes=48 * MIB)
    block = jax.ShapeDtypeStruct((rows, width), BF16)
    mixed = pl.pallas_call(
        mix_kernel, in_specs=[vmem, vmem], out_specs=vmem, out_shape=block, compiler_params=small, name="mix"
    )(conv, query)
    mixed_other = lax.ppermute(mixed, ("tp", "dp"), pair_route)
    own_sums = pl.pallas_call(
        own_kernel,
        in_specs=[smem, vmem, hbm],
        out_specs=vmem,
        out_shape=jax.ShapeDtypeStruct((chunks, rows, width), F32),
        scratch_shapes=[pltpu.VMEM((chunks, width, width), BF16), pltpu.SemaphoreType.DMA((chunks,))],
        compiler_params=small,
        name="own",
    )(place, mixed, w_out)

    def project(steps, kind):
        return pl.pallas_call(
            functools.partial(other_kernel, steps),
            in_specs=[smem, vmem, vmem, vmem],
            out_specs=[vmem] * len(steps),
            out_shape=[jax.ShapeDtypeStruct((rows, width), kind)] * len(steps),
            compiler_params=small,
            name="other",
        )(place, mixed_other, own_sums, w_other)

    def passed(block, step):
        return lax.ppermute(block, ("tp", "dp"), [(quad[i], quad[i ^ step]) for quad in quads for i in range(chunks)])

    parts = [passed(block, step) for step, block in zip((3,), project((3,), BF16))]
    parts += [passed(block, step) for step, block in zip((1, 2), project((1, 2), BF16))]
    (own,) = project((0,), F32)
    return pl.pallas_call(
        sum_kernel,
        in_specs=[vmem] * 4,
        out_shape=jax.ShapeDtypeStruct((rows, width), BF16),
        compiler_params=pltpu.CompilerParams(vmem_limit_bytes=48 * MIB),
        name="sum",
    )(own, *parts)


def solution(mesh):
    in_specs = (
        P(None, ("dp", "ctx"), "tp"),
        P(None, None, "tp"),
        P("ctx", "tp"),
        P("tp"),
        P("tp", None),
    )
    out_specs = P(("dp", "ctx"), "tp")
    return jax.shard_map(local, mesh=mesh, in_specs=in_specs, out_specs=out_specs, check_vma=False)
```

```python
import functools
import math

import jax
import jax.numpy as jnp
import numpy as np
from jax import lax
from jax.experimental import pallas as pl
from jax.experimental.pallas import tpu as pltpu
from jax.sharding import PartitionSpec as P

TAPS = 7
LANES = 128
HALO = 16
BF16 = jnp.bfloat16
F32 = jnp.float32
MIB = 1024 * 1024


def split_table(table):
    high = table.astype(np.float32).astype(jnp.bfloat16)
    low = (table - high.astype(np.float64)).astype(np.float32).astype(jnp.bfloat16)
    return np.stack([high, low])


def lane_tables(width):
    angle = 2.0 * np.pi * (np.outer(np.arange(width), np.arange(width)) % width) / width
    cos, sin = np.cos(angle), np.sin(angle)
    forward = np.block([[cos, -sin], [sin, cos]])
    return np.concatenate([split_table(table).reshape(-1, 2 * width) for table in (forward, forward.T)])


def twiddles(blocks, width):
    angle = 2.0 * np.pi * np.outer(np.arange(blocks) + 0.5, np.arange(width)) / (2 * blocks * width)
    return np.stack([np.cos(angle), -np.sin(angle)]).astype(np.float32)[:, :, None, :]


def block_angle(s, k, blocks):
    return math.pi * ((s * (2 * k + 1)) % (4 * blocks)) / (2 * blocks)


def split_bf16(values):
    high = values.astype(BF16)
    return high, (values - high.astype(F32)).astype(BF16)


def dot(a, b):
    return jnp.dot(a, b, preferred_element_type=F32)


def column_start(place_ref, i, w_hbm, other=False):
    width = w_hbm.shape[0]
    chunks = w_hbm.shape[1] // width
    core, ring = lax.rem(place_ref[0], 2), place_ref[0] // 2
    mine = ring // 2
    side = (lax.rem(ring, 2) + (2 * mine >= chunks // 2).astype(jnp.int32) + int(other)) % 2
    upper = (2 * jnp.asarray(i, jnp.int32) >= chunks // 2).astype(jnp.int32)
    return pl.multiple_of(lax.rem(2 * i + lax.rem(side + upper, 2) + core, chunks) * width, width)


def prep_kernel(
    place_ref, projected_hbm, filter_hbm, w_hbm, out_hbm, w_send, tail_ref, inputs, taps_in, turned, held, sems, w_sems
):
    blocks, lines, rows = turned.shape
    group = lines // 3
    width = w_hbm.shape[0]
    chunks = w_send.shape[1] // width
    arrive = [pltpu.make_async_copy(projected_hbm.at[1 + part], inputs.at[part], sems.at[part]) for part in range(2)]
    arrive.append(pltpu.make_async_copy(filter_hbm, taps_in, sems.at[2]))
    tail = pltpu.make_async_copy(projected_hbm.at[0, rows - HALO :], tail_ref, sems.at[6])
    for copy in [*arrive, tail]:
        copy.start()
    w_in, w_out = [], []
    for i in range(chunks):
        start = column_start(place_ref, i, w_hbm, other=True)
        columns = slice(i * width, (i + 1) * width)
        w_in.append(pltpu.make_async_copy(w_hbm.at[:, pl.ds(start, width)], held.at[:, columns], w_sems.at[i]))
        w_out.append(pltpu.make_async_copy(held.at[:, columns], w_send.at[:, columns], w_sems.at[chunks + i]))
        w_in[i].start()
    leave = []
    for part in range(3):
        arrive[part].wait()
        source = inputs[part] if part < 2 else taps_in[...].astype(BF16)
        at = slice(part * group, (part + 1) * group)
        turned[:, at, :] = source.T.reshape(blocks, group, rows)
        leave.append(pltpu.make_async_copy(turned.at[:, at], out_hbm.at[:, at], sems.at[3 + part]))
        leave[part].start()
    for i in range(chunks):
        w_in[i].wait()
        w_out[i].start()
    for copy in [*leave, *w_out, tail]:
        copy.wait()


def query_kernel(projected_hbm, before_ref, taps_ref, out_ref, now_ref, whole, sem):
    rows = out_ref.shape[0]
    halo = before_ref.shape[0]
    copy = pltpu.make_async_copy(projected_hbm.at[0], now_ref, sem.at[0])
    copy.start()
    whole[:halo] = before_ref[...].astype(F32)
    copy.wait()
    whole[halo:] = now_ref[...].astype(F32)
    total = taps_ref[0, 0:1, :] * whole[halo:]
    for j in range(1, TAPS):
        total = total + taps_ref[0, j : j + 1, :] * whole[pl.ds(halo - j, rows), :]
    out_ref[...] = total


def featurize(recv_ref, taps_ref, gated):
    blocks, lines_all, width = recv_ref.shape
    group = lines_all // 3
    tile = 16
    batch = blocks
    lane = lax.broadcasted_iota(jnp.int32, (tile, LANES), 1)
    for c0 in range(0, group, tile):
        lines = slice(c0, c0 + tile)
        for part in (1, 2):
            t = [
                jnp.broadcast_to(taps_ref[lines, part * TAPS + j : part * TAPS + j + 1], (tile, LANES))
                for j in range(TAPS)
            ]
            last = [jnp.zeros((tile, LANES), F32)] * 4
            first_row = (part - 1) * group + c0
            for s0 in range(0, blocks, batch):
                places = [(s, lines, slice(l0, l0 + LANES)) for s in range(s0, s0 + batch) for l0 in range(0, width, LANES)]
                now = [recv_ref[s, first_row : first_row + tile, cols].astype(F32) for s, _, cols in places]
                gates = [gated[at] for at in places] if part == 2 else None

                def shifted(values, amount, which):
                    turns = [pltpu.roll(value, amount, 1) for value in values]
                    moved = [jnp.where(lane < amount, b, a) for b, a in zip([last[which]] + turns[:-1], turns)]
                    last[which] = turns[-1]
                    return moved

                one = shifted(now, 1, 0)
                two = shifted([t[2] * x + t[3] * y for x, y in zip(now, one)], 2, 1)
                four = shifted([t[4] * x + t[5] * y for x, y in zip(now, one)], 4, 2)
                six = shifted([t[6] * x for x in now], 6, 3)
                totals = [t[0] * x + t[1] * y + a + b + c for x, y, a, b, c in zip(now, one, two, four, six)]
                if part == 2:
                    totals = [g * total for g, total in zip(gates, totals)]
                for at, total in zip(places, totals):
                    gated[at] = total


def over_blocks(values, k, blocks):
    even_c = even_s = odd_c = odd_s = None
    for s, value in enumerate(values):
        c, t = math.cos(block_angle(s, k, blocks)), math.sin(block_angle(s, k, blocks))
        if s == 0:
            even_c = value
            continue
        term_c, term_s = value * c, value * t
        if s % 2 == 0:
            even_c = even_c + term_c
            even_s = term_s if even_s is None else even_s + term_s
        else:
            odd_c = term_c if odd_c is None else odd_c + term_c
            odd_s = term_s if odd_s is None else odd_s + term_s
    return (even_c + odd_c, -(even_s + odd_s)), (even_c - odd_c, even_s - odd_s)


def conv_kernel(
    recv_ref, taps_ref, tw_ref, tables_hbm, out_ref, gated, high, low, spec_h, spec_u, tables, sems
):
    blocks, lines_all, width = recv_ref.shape
    group = lines_all // 3
    tile = 16
    load = pltpu.make_async_copy(tables_hbm, tables, sems.at[0])
    load.start()
    featurize(recv_ref, taps_ref, gated)

    def table(which, term):
        start = (2 * which + term) * 2 * width
        return tables[start : start + 2 * width, :]

    def store_split(rows, cols, value):
        high[rows, cols], low[rows, cols] = split_bf16(value)

    def lanes(which):
        return dot(high[...], table(which, 0)) + dot(low[...], table(which, 0)) + dot(high[...], table(which, 1))

    def to_odd(block):
        for c0 in range(0, group, tile):
            for l0 in range(0, width, LANES):
                values = [block(s, c0, slice(l0, l0 + LANES)) for s in range(blocks)]
                for k in range(blocks // 2):
                    for kk, (re, im) in zip((k, blocks - 1 - k), over_blocks(values, k, blocks)):
                        tr = tw_ref[0, kk, :, l0 : l0 + LANES]
                        ti = tw_ref[1, kk, :, l0 : l0 + LANES]
                        rows = slice(kk * group + c0, kk * group + c0 + tile)
                        store_split(rows, slice(l0, l0 + LANES), re * tr - im * ti)
                        store_split(rows, slice(width + l0, width + l0 + LANES), re * ti + im * tr)

    to_odd(lambda s, c, p: recv_ref[s, 2 * group + c : 2 * group + c + tile, p].astype(F32))
    load.wait()
    spec_h[...] = lanes(0)
    to_odd(lambda s, c, p: gated[s, c : c + tile, p])
    spec_u[...] = lanes(0)

    hr, hi = spec_h[:, :width], spec_h[:, width:]
    ur, ui = spec_u[:, :width], spec_u[:, width:]
    store_split(slice(None), slice(0, width), hr * ur - hi * ui)
    store_split(slice(None), slice(width, 2 * width), hr * ui + hi * ur)
    spec_h[...] = lanes(1)

    scale = 1.0 / (blocks * width)
    half = blocks // 2
    for c0 in range(0, group, tile):
        skip = taps_ref[c0 : c0 + tile, 3 * TAPS : 3 * TAPS + 1]
        for l0 in range(0, width, LANES):
            reals, imags = [], []
            for k in range(blocks):
                rows = slice(k * group + c0, k * group + c0 + tile)
                tr = tw_ref[0, k, :, l0 : l0 + LANES] * scale
                ti = tw_ref[1, k, :, l0 : l0 + LANES] * scale
                re = spec_h[rows, l0 : l0 + LANES]
                im = spec_h[rows, width + l0 : width + l0 + LANES]
                reals.append(re * tr + im * ti)
                imags.append(im * tr - re * ti)
            sum_re = [reals[k] + reals[blocks - 1 - k] for k in range(half)]
            dif_re = [reals[k] - reals[blocks - 1 - k] for k in range(half)]
            sum_im = [imags[k] + imags[blocks - 1 - k] for k in range(half)]
            dif_im = [imags[k] - imags[blocks - 1 - k] for k in range(half)]
            for s in range(blocks):
                res, ims = (sum_re, dif_im) if s % 2 == 0 else (dif_re, sum_im)
                total = None
                for k in range(half):
                    angle = block_angle(s, k, blocks)
                    term = res[k] if s == 0 else res[k] * math.cos(angle) - ims[k] * math.sin(angle)
                    total = term if total is None else total + term
                at = (s, slice(c0, c0 + tile), slice(l0, l0 + LANES))
                out_ref[at] = (total + skip * gated[at]).astype(BF16)


def mix_kernel(conv_ref, query_ref, out_ref):
    rows, width = query_ref.shape
    turned = conv_ref[...].reshape(width, rows).T
    out_ref[...] = (query_ref[...] * turned.astype(F32)).astype(BF16)


def own_kernel(place_ref, mixed_ref, w_hbm, out_ref, own, sems):
    width = w_hbm.shape[0]
    index = place_ref[0] // 4
    copies = []
    for step in range(own.shape[0]):
        start = column_start(place_ref, index ^ step, w_hbm)
        copies.append(pltpu.make_async_copy(w_hbm.at[:, pl.ds(start, width)], own.at[step], sems.at[step]))
        copies[step].start()
    for step in reversed(range(own.shape[0])):
        copies[step].wait()
        out_ref[step] = dot(mixed_ref[...], own[step])


def other_kernel(steps, place_ref, mixed_ref, own_ref, other_ref, *outs):
    width = other_ref.shape[0]
    index = place_ref[0] // 4
    for step, out in zip(steps, outs):
        start = pl.multiple_of((index ^ step) * width, width)
        out[...] = (own_ref[step] + dot(mixed_ref[...], other_ref[:, pl.ds(start, width)])).astype(out.dtype)


def sum_kernel(own_ref, *refs):
    total = own_ref[...]
    for ref in refs[:-1]:
        total = total + ref[...].astype(F32)
    refs[-1][...] = total.astype(BF16)


def local(projected, short_taps, long_filter, skip_gain, w_out):
    ctx, tp, dp = lax.axis_size("ctx"), lax.axis_size("tp"), lax.axis_size("dp")
    rows, width = projected.shape[1:]
    group = width // ctx
    me_ctx, me_tp, me_dp = lax.axis_index("ctx"), lax.axis_index("tp"), lax.axis_index("dp")

    chunks = tp // 2

    def quad_place(q, i):
        return 2 * i + (q + (2 * i >= tp // 2)) % 2

    def device(r, d):
        return (r + d) % tp * dp + d

    pair_route = [(device(r, d), device(r ^ 1, d)) for r in range(tp) for d in range(dp)]
    quads = [[device(quad_place(q, i), d) for i in range(chunks)] for d in range(dp) for q in range(2)]
    place = (lax.rem(me_tp - me_dp + tp, tp) * 2 + me_dp).astype(jnp.int32)[None]

    vmem = pl.BlockSpec(memory_space=pltpu.VMEM)
    smem = pl.BlockSpec(memory_space=pltpu.SMEM)
    hbm = pl.BlockSpec(memory_space=pl.ANY)
    params = pltpu.CompilerParams(vmem_limit_bytes=60 * MIB)

    send, w_send, tail = pl.pallas_call(
        prep_kernel,
        in_specs=[smem, hbm, hbm, hbm],
        out_specs=[hbm, hbm, vmem],
        out_shape=[
            jax.ShapeDtypeStruct((ctx, 3 * group, rows), BF16),
            jax.ShapeDtypeStruct((width, chunks * width), BF16),
            jax.ShapeDtypeStruct((HALO, width), BF16),
        ],
        scratch_shapes=[
            pltpu.VMEM((2, rows, width), BF16),
            pltpu.VMEM((rows, width), F32),
            pltpu.VMEM((ctx, 3 * group, rows), BF16),
            pltpu.VMEM((width, chunks * width), BF16),
            pltpu.SemaphoreType.DMA((7,)),
            pltpu.SemaphoreType.DMA((2 * chunks,)),
        ],
        compiler_params=params,
        name="prep",
    )(place, projected, long_filter, w_out)
    recv = lax.all_to_all(send, "ctx", 0, 0, tiled=True)
    w_other = lax.ppermute(w_send, ("tp", "dp"), pair_route)

    taps = jnp.concatenate([short_taps.reshape(3 * TAPS, width), skip_gain[None, :]], axis=0)
    taps = lax.dynamic_slice_in_dim(taps, me_ctx * group, group, axis=1).T
    before = lax.ppermute(tail, "ctx", [(i, i + 1) for i in range(ctx - 1)])
    taps, before = lax.optimization_barrier((taps, before))
    query = pl.pallas_call(
        query_kernel,
        in_specs=[hbm, vmem, vmem],
        out_specs=vmem,
        out_shape=jax.ShapeDtypeStruct((rows, width), F32),
        scratch_shapes=[
            pltpu.VMEM((rows, width), BF16),
            pltpu.VMEM((HALO + rows, width), F32),
            pltpu.SemaphoreType.DMA((1,)),
        ],
        compiler_params=pltpu.CompilerParams(vmem_limit_bytes=50 * MIB),
        name="query",
    )(projected, before, short_taps)

    tables = lane_tables(rows)
    conv = pl.pallas_call(
        conv_kernel,
        in_specs=[vmem, vmem, vmem, hbm],
        out_specs=vmem,
        out_shape=jax.ShapeDtypeStruct((ctx, group, rows), BF16),
        scratch_shapes=[
            pltpu.VMEM((ctx, group, rows), F32),
            pltpu.VMEM((ctx * group, 2 * rows), BF16),
            pltpu.VMEM((ctx * group, 2 * rows), BF16),
            pltpu.VMEM((ctx * group, 2 * rows), F32),
            pltpu.VMEM((ctx * group, 2 * rows), F32),
            pltpu.VMEM(tables.shape, BF16),
            pltpu.SemaphoreType.DMA((1,)),
        ],
        compiler_params=pltpu.CompilerParams(vmem_limit_bytes=52 * MIB),
        name="conv",
    )(recv, taps, jnp.asarray(twiddles(ctx, rows)), jnp.asarray(tables))
    conv = lax.all_to_all(conv, "ctx", 0, 0, tiled=True)

    small = pltpu.CompilerParams(vmem_limit_bytes=48 * MIB)
    block = jax.ShapeDtypeStruct((rows, width), BF16)
    mixed = pl.pallas_call(
        mix_kernel, in_specs=[vmem, vmem], out_specs=vmem, out_shape=block, compiler_params=small, name="mix"
    )(conv, query)
    mixed_other = lax.ppermute(mixed, ("tp", "dp"), pair_route)
    own_sums = pl.pallas_call(
        own_kernel,
        in_specs=[smem, vmem, hbm],
        out_specs=vmem,
        out_shape=jax.ShapeDtypeStruct((chunks, rows, width), F32),
        scratch_shapes=[pltpu.VMEM((chunks, width, width), BF16), pltpu.SemaphoreType.DMA((chunks,))],
        compiler_params=small,
        name="own",
    )(place, mixed, w_out)

    def project(steps, kind):
        return pl.pallas_call(
            functools.partial(other_kernel, steps),
            in_specs=[smem, vmem, vmem, vmem],
            out_specs=[vmem] * len(steps),
            out_shape=[jax.ShapeDtypeStruct((rows, width), kind)] * len(steps),
            compiler_params=small,
            name="other",
        )(place, mixed_other, own_sums, w_other)

    def passed(block, step):
        return lax.ppermute(block, ("tp", "dp"), [(quad[i], quad[i ^ step]) for quad in quads for i in range(chunks)])

    parts = [passed(block, step) for step, block in zip((3,), project((3,), BF16))]
    parts += [passed(block, step) for step, block in zip((1, 2), project((1, 2), BF16))]
    (own,) = project((0,), F32)
    return pl.pallas_call(
        sum_kernel,
        in_specs=[vmem] * 4,
        out_shape=jax.ShapeDtypeStruct((rows, width), BF16),
        compiler_params=pltpu.CompilerParams(vmem_limit_bytes=48 * MIB),
        name="sum",
    )(own, *parts)


def solution(mesh):
    in_specs = (
        P(None, ("dp", "ctx"), "tp"),
        P(None, None, "tp"),
        P("ctx", "tp"),
        P("tp"),
        P("tp", None),
    )
    out_specs = P(("dp", "ctx"), "tp")
    return jax.shard_map(local, mesh=mesh, in_specs=in_specs, out_specs=out_specs, check_vma=False)
```

```python
import functools
import math

import jax
import jax.numpy as jnp
import numpy as np
from jax import lax
from jax.experimental import pallas as pl
from jax.experimental.pallas import tpu as pltpu
from jax.sharding import PartitionSpec as P

TAPS = 7
LANES = 128
HALO = 16
EDGE_LANES = 64
BF16 = jnp.bfloat16
F32 = jnp.float32
MIB = 1024 * 1024


def split_table(table):
    high = table.astype(np.float32).astype(jnp.bfloat16)
    low = (table - high.astype(np.float64)).astype(np.float32).astype(jnp.bfloat16)
    return np.stack([high, low])


def lane_tables(width):
    angle = 2.0 * np.pi * (np.outer(np.arange(width), np.arange(width)) % width) / width
    cos, sin = np.cos(angle), np.sin(angle)
    forward = np.block([[cos, -sin], [sin, cos]])
    return np.concatenate([split_table(table).reshape(-1, 2 * width) for table in (forward, forward.T)])


def twiddles(blocks, width):
    angle = 2.0 * np.pi * np.outer(np.arange(blocks) + 0.5, np.arange(width)) / (2 * blocks * width)
    return np.stack([np.cos(angle), -np.sin(angle)]).astype(np.float32)[:, :, None, :]


def block_angle(s, k, blocks):
    return math.pi * ((s * (2 * k + 1)) % (4 * blocks)) / (2 * blocks)


def split_bf16(values):
    high = values.astype(BF16)
    return high, (values - high.astype(F32)).astype(BF16)


def dot(a, b):
    return jnp.dot(a, b, preferred_element_type=F32)


def column_start(place_ref, i, w_hbm, other=False):
    width = w_hbm.shape[0]
    chunks = w_hbm.shape[1] // width
    core, ring = lax.rem(place_ref[0], 2), place_ref[0] // 2
    mine = ring // 2
    side = (lax.rem(ring, 2) + (2 * mine >= chunks // 2).astype(jnp.int32) + int(other)) % 2
    upper = (2 * jnp.asarray(i, jnp.int32) >= chunks // 2).astype(jnp.int32)
    return pl.multiple_of(lax.rem(2 * i + lax.rem(side + upper, 2) + core, chunks) * width, width)


def prep_kernel(
    place_ref, projected_hbm, filter_hbm, taps_hbm, w_hbm, out_hbm, w_send,
    inputs, filter_in, taps, whole, edges, turned, held, sems, w_sems,
):
    blocks, group, _ = turned.shape
    rows, width = inputs.shape[1:]
    halo = TAPS - 1
    chunks = w_send.shape[1] // width
    arrive = [
        pltpu.make_async_copy(filter_hbm, filter_in, sems.at[0]),
        pltpu.make_async_copy(taps_hbm, taps, sems.at[1]),
        pltpu.make_async_copy(projected_hbm.at[1], inputs.at[0], sems.at[2]),
        pltpu.make_async_copy(projected_hbm.at[2], inputs.at[1], sems.at[3]),
    ]
    for copy in arrive:
        copy.start()
    w_in, w_out = [], []
    for i in range(chunks):
        start = column_start(place_ref, i, w_hbm, other=True)
        columns = slice(i * width, (i + 1) * width)
        w_in.append(pltpu.make_async_copy(w_hbm.at[:, pl.ds(start, width)], held.at[:, columns], w_sems.at[i]))
        w_out.append(pltpu.make_async_copy(held.at[:, columns], w_send.at[:, columns], w_sems.at[chunks + i]))
        w_in[i].start()
    leave = []

    def store(values, lanes):
        turned[:, :, lanes] = values.astype(BF16).T.reshape(blocks, group, -1)
        leave.append(pltpu.make_async_copy(turned.at[:, :, lanes], out_hbm.at[:, :, lanes], sems.at[4 + len(leave)]))
        leave[-1].start()

    arrive[0].wait()
    store(filter_in[...], slice(rows, 2 * rows))
    arrive[1].wait()
    edges[...] = jnp.zeros_like(edges)
    gated = None
    for part in range(2):
        arrive[2 + part].wait()
        now = whole.at[part]
        now[:8] = jnp.zeros((8, width), F32)
        now[8:] = inputs[part].astype(F32)
        first = part * EDGE_LANES
        edges[first : first + halo] = now[rows + 8 - halo : rows + 8]
        edges[first + halo : first + 2 * halo] = now[8 : 8 + halo]
        total = taps[1 + part, 0:1, :] * now[8:]
        for j in range(1, TAPS):
            total = total + taps[1 + part, j : j + 1, :] * now[8 - j : 8 - j + rows]
        gated = total if gated is None else gated * total
    store(edges[...], slice(2 * rows, 2 * rows + LANES))
    store(gated, slice(0, rows))
    for i in range(chunks):
        w_in[i].wait()
        w_out[i].start()
    for copy in leave + w_out:
        copy.wait()


def query_kernel(now_ref, before_ref, taps_ref, out_ref, whole):
    rows = out_ref.shape[0]
    halo = before_ref.shape[0]
    whole[:halo] = before_ref[...].astype(F32)
    whole[halo:] = now_ref[...].astype(F32)
    total = taps_ref[0, 0:1, :] * whole[halo:]
    for j in range(1, TAPS):
        total = total + taps_ref[0, j : j + 1, :] * whole[pl.ds(halo - j, rows), :]
    out_ref[...] = total


def complete(recv_ref, taps_ref, gated):
    blocks, group, lanes_all = recv_ref.shape
    width = (lanes_all - LANES) // 2
    halo = TAPS - 1
    tile = 16
    lane = lax.broadcasted_iota(jnp.int32, (tile, LANES), 1)
    value_side = lane >= EDGE_LANES
    tail = (lane < halo) | (value_side & (lane < EDGE_LANES + halo))
    for c0 in range(0, group, tile):
        lines = slice(c0, c0 + tile)
        t = []
        for j in range(TAPS):
            key, value = (taps_ref[lines, part * TAPS + j : part * TAPS + j + 1] for part in (1, 2))
            t.append(jnp.where(value_side, jnp.broadcast_to(value, lane.shape), jnp.broadcast_to(key, lane.shape)))
        packs = [recv_ref[s, lines, 2 * width :].astype(F32) for s in range(blocks)]
        starts = [recv_ref[s, lines, :LANES].astype(F32) for s in range(blocks)]
        rests = [recv_ref[s, lines, LANES:width].astype(F32) for s in range(blocks)]
        spans = [jnp.where(tail, b, a) for b, a in zip([jnp.zeros_like(packs[0])] + packs[:-1], packs)]
        totals = [t[0] * span for span in spans]
        for j in range(1, TAPS):
            totals = [total + t[j] * pltpu.roll(span, j, 1) for total, span in zip(totals, spans)]
        firsts = [total * pltpu.roll(total, EDGE_LANES, 1) for total in totals]
        firsts = [pltpu.roll(first, LANES - halo, 1) for first in firsts]
        starts = [jnp.where(lane < halo, first, start) for first, start in zip(firsts, starts)]
        for s in range(blocks):
            gated[s, lines, :LANES] = starts[s]
            gated[s, lines, LANES:width] = rests[s]


def over_blocks(values, k, blocks):
    even_c = even_s = odd_c = odd_s = None
    for s, value in enumerate(values):
        c, t = math.cos(block_angle(s, k, blocks)), math.sin(block_angle(s, k, blocks))
        if s == 0:
            even_c = value
            continue
        term_c, term_s = value * c, value * t
        if s % 2 == 0:
            even_c = even_c + term_c
            even_s = term_s if even_s is None else even_s + term_s
        else:
            odd_c = term_c if odd_c is None else odd_c + term_c
            odd_s = term_s if odd_s is None else odd_s + term_s
    return (even_c + odd_c, -(even_s + odd_s)), (even_c - odd_c, even_s - odd_s)


def conv_kernel(
    recv_ref, taps_ref, tw_ref, tables_hbm, out_ref, gated, high, low, spec_h, spec_u, tables, sems
):
    blocks, group, lanes_all = recv_ref.shape
    width = (lanes_all - LANES) // 2
    tile = 16
    load = pltpu.make_async_copy(tables_hbm, tables, sems.at[0])
    load.start()
    complete(recv_ref, taps_ref, gated)

    def table(which, term):
        start = (2 * which + term) * 2 * width
        return tables[start : start + 2 * width, :]

    def store_split(rows, cols, value):
        high[rows, cols], low[rows, cols] = split_bf16(value)

    def lanes(which):
        return dot(high[...], table(which, 0)) + dot(low[...], table(which, 0)) + dot(high[...], table(which, 1))

    def to_odd(block):
        for c0 in range(0, group, tile):
            for l0 in range(0, width, LANES):
                values = [block(s, c0, slice(l0, l0 + LANES)) for s in range(blocks)]
                for k in range(blocks // 2):
                    for kk, (re, im) in zip((k, blocks - 1 - k), over_blocks(values, k, blocks)):
                        tr = tw_ref[0, kk, :, l0 : l0 + LANES]
                        ti = tw_ref[1, kk, :, l0 : l0 + LANES]
                        rows = slice(kk * group + c0, kk * group + c0 + tile)
                        store_split(rows, slice(l0, l0 + LANES), re * tr - im * ti)
                        store_split(rows, slice(width + l0, width + l0 + LANES), re * ti + im * tr)

    to_odd(lambda s, c, p: recv_ref[s, c : c + tile, width + p.start : width + p.stop].astype(F32))
    load.wait()
    spec_h[...] = lanes(0)
    to_odd(lambda s, c, p: gated[s, c : c + tile, p])
    spec_u[...] = lanes(0)

    hr, hi = spec_h[:, :width], spec_h[:, width:]
    ur, ui = spec_u[:, :width], spec_u[:, width:]
    store_split(slice(None), slice(0, width), hr * ur - hi * ui)
    store_split(slice(None), slice(width, 2 * width), hr * ui + hi * ur)
    spec_h[...] = lanes(1)

    scale = 1.0 / (blocks * width)
    half = blocks // 2
    for c0 in range(0, group, tile):
        skip = taps_ref[c0 : c0 + tile, 3 * TAPS : 3 * TAPS + 1]
        for l0 in range(0, width, LANES):
            reals, imags = [], []
            for k in range(blocks):
                rows = slice(k * group + c0, k * group + c0 + tile)
                tr = tw_ref[0, k, :, l0 : l0 + LANES] * scale
                ti = tw_ref[1, k, :, l0 : l0 + LANES] * scale
                re = spec_h[rows, l0 : l0 + LANES]
                im = spec_h[rows, width + l0 : width + l0 + LANES]
                reals.append(re * tr + im * ti)
                imags.append(im * tr - re * ti)
            sum_re = [reals[k] + reals[blocks - 1 - k] for k in range(half)]
            dif_re = [reals[k] - reals[blocks - 1 - k] for k in range(half)]
            sum_im = [imags[k] + imags[blocks - 1 - k] for k in range(half)]
            dif_im = [imags[k] - imags[blocks - 1 - k] for k in range(half)]
            for s in range(blocks):
                res, ims = (sum_re, dif_im) if s % 2 == 0 else (dif_re, sum_im)
                total = None
                for k in range(half):
                    angle = block_angle(s, k, blocks)
                    term = res[k] if s == 0 else res[k] * math.cos(angle) - ims[k] * math.sin(angle)
                    total = term if total is None else total + term
                at = (s, slice(c0, c0 + tile), slice(l0, l0 + LANES))
                out_ref[at] = (total + skip * gated[at]).astype(BF16)


def mix_kernel(conv_ref, query_ref, out_ref):
    rows, width = query_ref.shape
    turned = conv_ref[...].reshape(width, rows).T
    out_ref[...] = (query_ref[...] * turned.astype(F32)).astype(BF16)


def own_kernel(place_ref, mixed_ref, w_hbm, out_ref, own, sems):
    width = w_hbm.shape[0]
    index = place_ref[0] // 4
    copies = []
    for step in range(own.shape[0]):
        start = column_start(place_ref, index ^ step, w_hbm)
        copies.append(pltpu.make_async_copy(w_hbm.at[:, pl.ds(start, width)], own.at[step], sems.at[step]))
        copies[step].start()
    for step in reversed(range(own.shape[0])):
        copies[step].wait()
        out_ref[step] = dot(mixed_ref[...], own[step])


def other_kernel(steps, place_ref, mixed_ref, own_ref, other_ref, *outs):
    width = other_ref.shape[0]
    index = place_ref[0] // 4
    for step, out in zip(steps, outs):
        start = pl.multiple_of((index ^ step) * width, width)
        out[...] = (own_ref[step] + dot(mixed_ref[...], other_ref[:, pl.ds(start, width)])).astype(out.dtype)


def sum_kernel(own_ref, *refs):
    total = own_ref[...]
    for ref in refs[:-1]:
        total = total + ref[...].astype(F32)
    refs[-1][...] = total.astype(BF16)


def local(projected, short_taps, long_filter, skip_gain, w_out):
    ctx, tp, dp = lax.axis_size("ctx"), lax.axis_size("tp"), lax.axis_size("dp")
    rows, width = projected.shape[1:]
    group = width // ctx
    me_ctx, me_tp, me_dp = lax.axis_index("ctx"), lax.axis_index("tp"), lax.axis_index("dp")

    chunks = tp // 2

    def quad_place(q, i):
        return 2 * i + (q + (2 * i >= tp // 2)) % 2

    def device(r, d):
        return (r + d) % tp * dp + d

    pair_route = [(device(r, d), device(r ^ 1, d)) for r in range(tp) for d in range(dp)]
    quads = [[device(quad_place(q, i), d) for i in range(chunks)] for d in range(dp) for q in range(2)]
    place = (lax.rem(me_tp - me_dp + tp, tp) * 2 + me_dp).astype(jnp.int32)[None]

    vmem = pl.BlockSpec(memory_space=pltpu.VMEM)
    smem = pl.BlockSpec(memory_space=pltpu.SMEM)
    hbm = pl.BlockSpec(memory_space=pl.ANY)
    params = pltpu.CompilerParams(vmem_limit_bytes=60 * MIB)

    send, w_send = pl.pallas_call(
        prep_kernel,
        in_specs=[smem, hbm, hbm, hbm, hbm],
        out_specs=[hbm, hbm],
        out_shape=[
            jax.ShapeDtypeStruct((ctx, group, 2 * rows + LANES), BF16),
            jax.ShapeDtypeStruct((width, chunks * width), BF16),
        ],
        scratch_shapes=[
            pltpu.VMEM((2, rows, width), BF16),
            pltpu.VMEM((rows, width), F32),
            pltpu.VMEM(short_taps.shape, F32),
            pltpu.VMEM((2, 8 + rows, width), F32),
            pltpu.VMEM((LANES, width), F32),
            pltpu.VMEM((ctx, group, 2 * rows + LANES), BF16),
            pltpu.VMEM((width, chunks * width), BF16),
            pltpu.SemaphoreType.DMA((7,)),
            pltpu.SemaphoreType.DMA((2 * chunks,)),
        ],
        compiler_params=params,
        name="prep",
    )(place, projected, long_filter, short_taps, w_out)
    recv = lax.all_to_all(send, "ctx", 0, 0, tiled=True)
    w_other = lax.ppermute(w_send, ("tp", "dp"), pair_route)

    before = lax.ppermute(projected[0, rows - HALO :], "ctx", [(i, i + 1) for i in range(ctx - 1)])
    query = pl.pallas_call(
        query_kernel,
        in_specs=[vmem] * 3,
        out_specs=vmem,
        out_shape=jax.ShapeDtypeStruct((rows, width), F32),
        scratch_shapes=[pltpu.VMEM((HALO + rows, width), F32)],
        compiler_params=pltpu.CompilerParams(vmem_limit_bytes=48 * MIB),
        name="query",
    )(projected[0], before, short_taps)

    taps = jnp.concatenate([short_taps.reshape(3 * TAPS, width), skip_gain[None, :]], axis=0)
    taps = lax.dynamic_slice_in_dim(taps, me_ctx * group, group, axis=1).T
    taps, query = lax.optimization_barrier((taps, query))
    tables = lane_tables(rows)
    conv = pl.pallas_call(
        conv_kernel,
        in_specs=[vmem, vmem, vmem, hbm],
        out_specs=vmem,
        out_shape=jax.ShapeDtypeStruct((ctx, group, rows), BF16),
        scratch_shapes=[
            pltpu.VMEM((ctx, group, rows), F32),
            pltpu.VMEM((ctx * group, 2 * rows), BF16),
            pltpu.VMEM((ctx * group, 2 * rows), BF16),
            pltpu.VMEM((ctx * group, 2 * rows), F32),
            pltpu.VMEM((ctx * group, 2 * rows), F32),
            pltpu.VMEM(tables.shape, BF16),
            pltpu.SemaphoreType.DMA((1,)),
        ],
        compiler_params=pltpu.CompilerParams(vmem_limit_bytes=52 * MIB),
        name="conv",
    )(recv, taps, jnp.asarray(twiddles(ctx, rows)), jnp.asarray(tables))
    conv = lax.all_to_all(conv, "ctx", 0, 0, tiled=True)

    small = pltpu.CompilerParams(vmem_limit_bytes=48 * MIB)
    block = jax.ShapeDtypeStruct((rows, width), BF16)
    mixed = pl.pallas_call(
        mix_kernel, in_specs=[vmem, vmem], out_specs=vmem, out_shape=block, compiler_params=small, name="mix"
    )(conv, query)
    mixed_other = lax.ppermute(mixed, ("tp", "dp"), pair_route)
    own_sums = pl.pallas_call(
        own_kernel,
        in_specs=[smem, vmem, hbm],
        out_specs=vmem,
        out_shape=jax.ShapeDtypeStruct((chunks, rows, width), F32),
        scratch_shapes=[pltpu.VMEM((chunks, width, width), BF16), pltpu.SemaphoreType.DMA((chunks,))],
        compiler_params=small,
        name="own",
    )(place, mixed, w_out)

    def project(steps, kind):
        return pl.pallas_call(
            functools.partial(other_kernel, steps),
            in_specs=[smem, vmem, vmem, vmem],
            out_specs=[vmem] * len(steps),
            out_shape=[jax.ShapeDtypeStruct((rows, width), kind)] * len(steps),
            compiler_params=small,
            name="other",
        )(place, mixed_other, own_sums, w_other)

    def passed(block, step):
        return lax.ppermute(block, ("tp", "dp"), [(quad[i], quad[i ^ step]) for quad in quads for i in range(chunks)])

    parts = [passed(block, step) for step, block in zip((2,), project((2,), BF16))]
    parts += [passed(block, step) for step, block in zip((3, 1), project((3, 1), BF16))]
    (own,) = project((0,), F32)
    return pl.pallas_call(
        sum_kernel,
        in_specs=[vmem] * 4,
        out_shape=jax.ShapeDtypeStruct((rows, width), BF16),
        compiler_params=pltpu.CompilerParams(vmem_limit_bytes=48 * MIB),
        name="sum",
    )(own, *parts)


def solution(mesh):
    in_specs = (
        P(None, ("dp", "ctx"), "tp"),
        P(None, None, "tp"),
        P("ctx", "tp"),
        P("tp"),
        P("tp", None),
    )
    out_specs = P(("dp", "ctx"), "tp")
    return jax.shard_map(local, mesh=mesh, in_specs=in_specs, out_specs=out_specs, check_vma=False)
```

```python
import functools
import math

import jax
import jax.numpy as jnp
import numpy as np
from jax import lax
from jax.experimental import pallas as pl
from jax.experimental.pallas import tpu as pltpu
from jax.sharding import PartitionSpec as P

TAPS = 7
LANES = 128
HALO = 16
EDGE_LANES = 64
BF16 = jnp.bfloat16
F32 = jnp.float32
MIB = 1024 * 1024


def split_table(table):
    high = table.astype(np.float32).astype(jnp.bfloat16)
    low = (table - high.astype(np.float64)).astype(np.float32).astype(jnp.bfloat16)
    return np.stack([high, low])


def lane_tables(width):
    angle = 2.0 * np.pi * (np.outer(np.arange(width), np.arange(width)) % width) / width
    cos, sin = np.cos(angle), np.sin(angle)
    forward = np.block([[cos, -sin], [sin, cos]])
    return np.concatenate([split_table(table).reshape(-1, 2 * width) for table in (forward, forward.T)])


def twiddles(blocks, width):
    angle = 2.0 * np.pi * np.outer(np.arange(blocks) + 0.5, np.arange(width)) / (2 * blocks * width)
    return np.stack([np.cos(angle), -np.sin(angle)]).astype(np.float32)[:, :, None, :]


def block_angle(s, k, blocks):
    return math.pi * ((s * (2 * k + 1)) % (4 * blocks)) / (2 * blocks)


def split_bf16(values):
    high = values.astype(BF16)
    return high, (values - high.astype(F32)).astype(BF16)


def dot(a, b):
    return jnp.dot(a, b, preferred_element_type=F32)


def column_start(place_ref, i, w_hbm, other=False):
    width = w_hbm.shape[0]
    chunks = w_hbm.shape[1] // width
    core, ring = lax.rem(place_ref[0], 2), place_ref[0] // 2
    mine = ring // 2
    side = (lax.rem(ring, 2) + (2 * mine >= chunks // 2).astype(jnp.int32) + int(other)) % 2
    upper = (2 * jnp.asarray(i, jnp.int32) >= chunks // 2).astype(jnp.int32)
    return pl.multiple_of(lax.rem(2 * i + lax.rem(side + upper, 2) + core, chunks) * width, width)


def prep_kernel(
    place_ref, projected_hbm, filter_hbm, taps_hbm, w_hbm, out_hbm, w_send,
    inputs, filter_in, taps, whole, edges, turned, held, sems, w_sems,
):
    blocks, group, _ = turned.shape
    rows, width = inputs.shape[1:]
    halo = TAPS - 1
    chunks = w_send.shape[1] // width
    arrive = [
        pltpu.make_async_copy(filter_hbm, filter_in, sems.at[0]),
        pltpu.make_async_copy(taps_hbm, taps, sems.at[1]),
        pltpu.make_async_copy(projected_hbm.at[1], inputs.at[0], sems.at[2]),
        pltpu.make_async_copy(projected_hbm.at[2], inputs.at[1], sems.at[3]),
    ]
    for copy in arrive:
        copy.start()
    w_in, w_out = [], []
    for i in range(chunks):
        start = column_start(place_ref, i, w_hbm, other=True)
        columns = slice(i * width, (i + 1) * width)
        w_in.append(pltpu.make_async_copy(w_hbm.at[:, pl.ds(start, width)], held.at[:, columns], w_sems.at[i]))
        w_out.append(pltpu.make_async_copy(held.at[:, columns], w_send.at[:, columns], w_sems.at[chunks + i]))
        w_in[i].start()
    leave = []

    def store(values, lanes):
        turned[:, :, lanes] = values.astype(BF16).T.reshape(blocks, group, -1)
        leave.append(pltpu.make_async_copy(turned.at[:, :, lanes], out_hbm.at[:, :, lanes], sems.at[4 + len(leave)]))
        leave[-1].start()

    arrive[0].wait()
    store(filter_in[...], slice(rows, 2 * rows))
    arrive[1].wait()
    edges[...] = jnp.zeros_like(edges)
    gated = None
    for part in range(2):
        arrive[2 + part].wait()
        now = whole.at[part]
        now[:8] = jnp.zeros((8, width), F32)
        now[8:] = inputs[part].astype(F32)
        first = part * EDGE_LANES
        edges[first : first + halo] = now[rows + 8 - halo : rows + 8]
        edges[first + halo : first + 2 * halo] = now[8 : 8 + halo]
        total = taps[1 + part, 0:1, :] * now[8:]
        for j in range(1, TAPS):
            total = total + taps[1 + part, j : j + 1, :] * now[8 - j : 8 - j + rows]
        gated = total if gated is None else gated * total
    store(edges[...], slice(2 * rows, 2 * rows + LANES))
    store(gated, slice(0, rows))
    for i in range(chunks):
        w_in[i].wait()
        w_out[i].start()
    for copy in leave + w_out:
        copy.wait()


def query_kernel(projected_hbm, before_ref, taps_ref, out_ref, now_ref, whole, sem):
    rows = out_ref.shape[0]
    halo = before_ref.shape[0]
    copy = pltpu.make_async_copy(projected_hbm.at[0], now_ref, sem.at[0])
    copy.start()
    whole[:halo] = before_ref[...].astype(F32)
    copy.wait()
    whole[halo:] = now_ref[...].astype(F32)
    total = taps_ref[0, 0:1, :] * whole[halo:]
    for j in range(1, TAPS):
        total = total + taps_ref[0, j : j + 1, :] * whole[pl.ds(halo - j, rows), :]
    out_ref[...] = total


def complete(recv_ref, taps_ref, gated):
    blocks, group, lanes_all = recv_ref.shape
    width = (lanes_all - LANES) // 2
    halo = TAPS - 1
    tile = 16
    lane = lax.broadcasted_iota(jnp.int32, (tile, LANES), 1)
    value_side = lane >= EDGE_LANES
    tail = (lane < halo) | (value_side & (lane < EDGE_LANES + halo))
    for c0 in range(0, group, tile):
        lines = slice(c0, c0 + tile)
        t = []
        for j in range(TAPS):
            key, value = (taps_ref[lines, part * TAPS + j : part * TAPS + j + 1] for part in (1, 2))
            t.append(jnp.where(value_side, jnp.broadcast_to(value, lane.shape), jnp.broadcast_to(key, lane.shape)))
        packs = [recv_ref[s, lines, 2 * width :].astype(F32) for s in range(blocks)]
        starts = [recv_ref[s, lines, :LANES].astype(F32) for s in range(blocks)]
        rests = [recv_ref[s, lines, LANES:width].astype(F32) for s in range(blocks)]
        spans = [jnp.where(tail, b, a) for b, a in zip([jnp.zeros_like(packs[0])] + packs[:-1], packs)]
        totals = [t[0] * span for span in spans]
        for j in range(1, TAPS):
            totals = [total + t[j] * pltpu.roll(span, j, 1) for total, span in zip(totals, spans)]
        firsts = [total * pltpu.roll(total, EDGE_LANES, 1) for total in totals]
        firsts = [pltpu.roll(first, LANES - halo, 1) for first in firsts]
        starts = [jnp.where(lane < halo, first, start) for first, start in zip(firsts, starts)]
        for s in range(blocks):
            gated[s, lines, :LANES] = starts[s]
            gated[s, lines, LANES:width] = rests[s]


def over_blocks(values, k, blocks):
    even_c = even_s = odd_c = odd_s = None
    for s, value in enumerate(values):
        c, t = math.cos(block_angle(s, k, blocks)), math.sin(block_angle(s, k, blocks))
        if s == 0:
            even_c = value
            continue
        term_c, term_s = value * c, value * t
        if s % 2 == 0:
            even_c = even_c + term_c
            even_s = term_s if even_s is None else even_s + term_s
        else:
            odd_c = term_c if odd_c is None else odd_c + term_c
            odd_s = term_s if odd_s is None else odd_s + term_s
    return (even_c + odd_c, -(even_s + odd_s)), (even_c - odd_c, even_s - odd_s)


def conv_kernel(
    recv_ref, taps_ref, tw_ref, tables_hbm, out_ref, gated, high, low, spec_h, spec_u, tables, sems
):
    blocks, group, lanes_all = recv_ref.shape
    width = (lanes_all - LANES) // 2
    tile = 16
    load = pltpu.make_async_copy(tables_hbm, tables, sems.at[0])
    load.start()
    complete(recv_ref, taps_ref, gated)

    def table(which, term):
        start = (2 * which + term) * 2 * width
        return tables[start : start + 2 * width, :]

    def store_split(rows, cols, value):
        high[rows, cols], low[rows, cols] = split_bf16(value)

    def lanes(which):
        return dot(high[...], table(which, 0)) + dot(low[...], table(which, 0)) + dot(high[...], table(which, 1))

    def to_odd(block):
        for c0 in range(0, group, tile):
            for l0 in range(0, width, LANES):
                values = [block(s, c0, slice(l0, l0 + LANES)) for s in range(blocks)]
                for k in range(blocks // 2):
                    for kk, (re, im) in zip((k, blocks - 1 - k), over_blocks(values, k, blocks)):
                        tr = tw_ref[0, kk, :, l0 : l0 + LANES]
                        ti = tw_ref[1, kk, :, l0 : l0 + LANES]
                        rows = slice(kk * group + c0, kk * group + c0 + tile)
                        store_split(rows, slice(l0, l0 + LANES), re * tr - im * ti)
                        store_split(rows, slice(width + l0, width + l0 + LANES), re * ti + im * tr)

    to_odd(lambda s, c, p: recv_ref[s, c : c + tile, width + p.start : width + p.stop].astype(F32))
    load.wait()
    spec_h[...] = lanes(0)
    to_odd(lambda s, c, p: gated[s, c : c + tile, p])
    spec_u[...] = lanes(0)

    hr, hi = spec_h[:, :width], spec_h[:, width:]
    ur, ui = spec_u[:, :width], spec_u[:, width:]
    store_split(slice(None), slice(0, width), hr * ur - hi * ui)
    store_split(slice(None), slice(width, 2 * width), hr * ui + hi * ur)
    spec_h[...] = lanes(1)

    scale = 1.0 / (blocks * width)
    half = blocks // 2
    for c0 in range(0, group, tile):
        skip = taps_ref[c0 : c0 + tile, 3 * TAPS : 3 * TAPS + 1]
        for l0 in range(0, width, LANES):
            reals, imags = [], []
            for k in range(blocks):
                rows = slice(k * group + c0, k * group + c0 + tile)
                tr = tw_ref[0, k, :, l0 : l0 + LANES] * scale
                ti = tw_ref[1, k, :, l0 : l0 + LANES] * scale
                re = spec_h[rows, l0 : l0 + LANES]
                im = spec_h[rows, width + l0 : width + l0 + LANES]
                reals.append(re * tr + im * ti)
                imags.append(im * tr - re * ti)
            sum_re = [reals[k] + reals[blocks - 1 - k] for k in range(half)]
            dif_re = [reals[k] - reals[blocks - 1 - k] for k in range(half)]
            sum_im = [imags[k] + imags[blocks - 1 - k] for k in range(half)]
            dif_im = [imags[k] - imags[blocks - 1 - k] for k in range(half)]
            for s in range(blocks):
                res, ims = (sum_re, dif_im) if s % 2 == 0 else (dif_re, sum_im)
                total = None
                for k in range(half):
                    angle = block_angle(s, k, blocks)
                    term = res[k] if s == 0 else res[k] * math.cos(angle) - ims[k] * math.sin(angle)
                    total = term if total is None else total + term
                at = (s, slice(c0, c0 + tile), slice(l0, l0 + LANES))
                out_ref[at] = (total + skip * gated[at]).astype(BF16)


def mix_kernel(conv_ref, query_ref, out_ref):
    rows, width = query_ref.shape
    turned = conv_ref[...].reshape(width, rows).T
    out_ref[...] = (query_ref[...] * turned.astype(F32)).astype(BF16)


def own_kernel(place_ref, mixed_ref, w_hbm, out_ref, own, sems):
    width = w_hbm.shape[0]
    index = place_ref[0] // 4
    copies = []
    for step in range(own.shape[0]):
        start = column_start(place_ref, index ^ step, w_hbm)
        copies.append(pltpu.make_async_copy(w_hbm.at[:, pl.ds(start, width)], own.at[step], sems.at[step]))
        copies[step].start()
    for step in reversed(range(own.shape[0])):
        copies[step].wait()
        out_ref[step] = dot(mixed_ref[...], own[step])


def other_kernel(steps, place_ref, mixed_ref, own_ref, other_ref, *outs):
    width = other_ref.shape[0]
    index = place_ref[0] // 4
    for step, out in zip(steps, outs):
        start = pl.multiple_of((index ^ step) * width, width)
        out[...] = (own_ref[step] + dot(mixed_ref[...], other_ref[:, pl.ds(start, width)])).astype(out.dtype)


def sum_kernel(own_ref, *refs):
    total = own_ref[...]
    for ref in refs[:-1]:
        total = total + ref[...].astype(F32)
    refs[-1][...] = total.astype(BF16)


def local(projected, short_taps, long_filter, skip_gain, w_out):
    ctx, tp, dp = lax.axis_size("ctx"), lax.axis_size("tp"), lax.axis_size("dp")
    rows, width = projected.shape[1:]
    group = width // ctx
    me_ctx, me_tp, me_dp = lax.axis_index("ctx"), lax.axis_index("tp"), lax.axis_index("dp")

    chunks = tp // 2

    def quad_place(q, i):
        return 2 * i + (q + (2 * i >= tp // 2)) % 2

    def device(r, d):
        return (r + d) % tp * dp + d

    pair_route = [(device(r, d), device(r ^ 1, d)) for r in range(tp) for d in range(dp)]
    quads = [[device(quad_place(q, i), d) for i in range(chunks)] for d in range(dp) for q in range(2)]
    place = (lax.rem(me_tp - me_dp + tp, tp) * 2 + me_dp).astype(jnp.int32)[None]

    vmem = pl.BlockSpec(memory_space=pltpu.VMEM)
    smem = pl.BlockSpec(memory_space=pltpu.SMEM)
    hbm = pl.BlockSpec(memory_space=pl.ANY)
    params = pltpu.CompilerParams(vmem_limit_bytes=60 * MIB)

    send, w_send = pl.pallas_call(
        prep_kernel,
        in_specs=[smem, hbm, hbm, hbm, hbm],
        out_specs=[hbm, hbm],
        out_shape=[
            jax.ShapeDtypeStruct((ctx, group, 2 * rows + LANES), BF16),
            jax.ShapeDtypeStruct((width, chunks * width), BF16),
        ],
        scratch_shapes=[
            pltpu.VMEM((2, rows, width), BF16),
            pltpu.VMEM((rows, width), F32),
            pltpu.VMEM(short_taps.shape, F32),
            pltpu.VMEM((2, 8 + rows, width), F32),
            pltpu.VMEM((LANES, width), F32),
            pltpu.VMEM((ctx, group, 2 * rows + LANES), BF16),
            pltpu.VMEM((width, chunks * width), BF16),
            pltpu.SemaphoreType.DMA((7,)),
            pltpu.SemaphoreType.DMA((2 * chunks,)),
        ],
        compiler_params=params,
        name="prep",
    )(place, projected, long_filter, short_taps, w_out)
    recv = lax.all_to_all(send, "ctx", 0, 0, tiled=True)
    w_other = lax.ppermute(w_send, ("tp", "dp"), pair_route)

    taps = jnp.concatenate([short_taps.reshape(3 * TAPS, width), skip_gain[None, :]], axis=0)
    taps = lax.dynamic_slice_in_dim(taps, me_ctx * group, group, axis=1).T
    before = lax.ppermute(projected[0, rows - HALO :], "ctx", [(i, i + 1) for i in range(ctx - 1)])
    taps, before = lax.optimization_barrier((taps, before))
    query = pl.pallas_call(
        query_kernel,
        in_specs=[hbm, vmem, vmem],
        out_specs=vmem,
        out_shape=jax.ShapeDtypeStruct((rows, width), F32),
        scratch_shapes=[
            pltpu.VMEM((rows, width), BF16),
            pltpu.VMEM((HALO + rows, width), F32),
            pltpu.SemaphoreType.DMA((1,)),
        ],
        compiler_params=pltpu.CompilerParams(vmem_limit_bytes=58 * MIB),
        name="query",
    )(projected, before, short_taps)

    tables = lane_tables(rows)
    conv = pl.pallas_call(
        conv_kernel,
        in_specs=[vmem, vmem, vmem, hbm],
        out_specs=vmem,
        out_shape=jax.ShapeDtypeStruct((ctx, group, rows), BF16),
        scratch_shapes=[
            pltpu.VMEM((ctx, group, rows), F32),
            pltpu.VMEM((ctx * group, 2 * rows), BF16),
            pltpu.VMEM((ctx * group, 2 * rows), BF16),
            pltpu.VMEM((ctx * group, 2 * rows), F32),
            pltpu.VMEM((ctx * group, 2 * rows), F32),
            pltpu.VMEM(tables.shape, BF16),
            pltpu.SemaphoreType.DMA((1,)),
        ],
        compiler_params=pltpu.CompilerParams(vmem_limit_bytes=52 * MIB),
        name="conv",
    )(recv, taps, jnp.asarray(twiddles(ctx, rows)), jnp.asarray(tables))
    conv = lax.all_to_all(conv, "ctx", 0, 0, tiled=True)

    small = pltpu.CompilerParams(vmem_limit_bytes=48 * MIB)
    block = jax.ShapeDtypeStruct((rows, width), BF16)
    mixed = pl.pallas_call(
        mix_kernel, in_specs=[vmem, vmem], out_specs=vmem, out_shape=block, compiler_params=small, name="mix"
    )(conv, query)
    mixed_other = lax.ppermute(mixed, ("tp", "dp"), pair_route)
    own_sums = pl.pallas_call(
        own_kernel,
        in_specs=[smem, vmem, hbm],
        out_specs=vmem,
        out_shape=jax.ShapeDtypeStruct((chunks, rows, width), F32),
        scratch_shapes=[pltpu.VMEM((chunks, width, width), BF16), pltpu.SemaphoreType.DMA((chunks,))],
        compiler_params=small,
        name="own",
    )(place, mixed, w_out)

    def project(steps, kind):
        return pl.pallas_call(
            functools.partial(other_kernel, steps),
            in_specs=[smem, vmem, vmem, vmem],
            out_specs=[vmem] * len(steps),
            out_shape=[jax.ShapeDtypeStruct((rows, width), kind)] * len(steps),
            compiler_params=small,
            name="other",
        )(place, mixed_other, own_sums, w_other)

    def passed(block, step):
        return lax.ppermute(block, ("tp", "dp"), [(quad[i], quad[i ^ step]) for quad in quads for i in range(chunks)])

    parts = [passed(block, step) for step, block in zip((3,), project((3,), BF16))]
    parts += [passed(block, step) for step, block in zip((1, 2), project((1, 2), BF16))]
    (own,) = project((0,), F32)
    return pl.pallas_call(
        sum_kernel,
        in_specs=[vmem] * 4,
        out_shape=jax.ShapeDtypeStruct((rows, width), BF16),
        compiler_params=pltpu.CompilerParams(vmem_limit_bytes=48 * MIB),
        name="sum",
    )(own, *parts)


def solution(mesh):
    in_specs = (
        P(None, ("dp", "ctx"), "tp"),
        P(None, None, "tp"),
        P("ctx", "tp"),
        P("tp"),
        P("tp", None),
    )
    out_specs = P(("dp", "ctx"), "tp")
    return jax.shard_map(local, mesh=mesh, in_specs=in_specs, out_specs=out_specs, check_vma=False)
```

```python
import functools
import math

import jax
import jax.numpy as jnp
import numpy as np
from jax import lax
from jax.experimental import pallas as pl
from jax.experimental.pallas import tpu as pltpu
from jax.sharding import PartitionSpec as P

TAPS = 7
LANES = 128
HALO = 16
BF16 = jnp.bfloat16
F32 = jnp.float32
MIB = 1024 * 1024


def split_table(table):
    high = table.astype(np.float32).astype(jnp.bfloat16)
    low = (table - high.astype(np.float64)).astype(np.float32).astype(jnp.bfloat16)
    return np.stack([high, low])


def lane_tables(width):
    angle = 2.0 * np.pi * (np.outer(np.arange(width), np.arange(width)) % width) / width
    cos, sin = np.cos(angle), np.sin(angle)
    forward = np.block([[cos, -sin], [sin, cos]])
    return np.concatenate([split_table(table).reshape(-1, 2 * width) for table in (forward, forward.T)])


def twiddles(blocks, width):
    angle = 2.0 * np.pi * np.outer(np.arange(blocks) + 0.5, np.arange(width)) / (2 * blocks * width)
    return np.stack([np.cos(angle), -np.sin(angle)]).astype(np.float32)[:, :, None, :]


def block_angle(s, k, blocks):
    return math.pi * ((s * (2 * k + 1)) % (4 * blocks)) / (2 * blocks)


def split_bf16(values):
    high = values.astype(BF16)
    return high, (values - high.astype(F32)).astype(BF16)


def dot(a, b):
    return jnp.dot(a, b, preferred_element_type=F32)


def column_start(place_ref, i, w_hbm, other=False):
    width = w_hbm.shape[0]
    chunks = w_hbm.shape[1] // width
    core, ring = lax.rem(place_ref[0], 2), place_ref[0] // 2
    mine = ring // 2
    side = (lax.rem(ring, 2) + (2 * mine >= chunks // 2).astype(jnp.int32) + int(other)) % 2
    upper = (2 * jnp.asarray(i, jnp.int32) >= chunks // 2).astype(jnp.int32)
    return pl.multiple_of(lax.rem(2 * i + lax.rem(side + upper, 2) + core, chunks) * width, width)


def prep_kernel(place_ref, projected_hbm, filter_hbm, w_hbm, out_hbm, w_send, inputs, taps_in, turned, held, sems, w_sems):
    blocks, lines, rows = turned.shape
    group = lines // 3
    width = w_hbm.shape[0]
    chunks = w_send.shape[1] // width
    arrive = [pltpu.make_async_copy(projected_hbm.at[1 + part], inputs.at[part], sems.at[part]) for part in range(2)]
    arrive.append(pltpu.make_async_copy(filter_hbm, taps_in, sems.at[2]))
    for copy in arrive:
        copy.start()
    w_in, w_out = [], []
    for i in range(chunks):
        start = column_start(place_ref, i, w_hbm, other=True)
        columns = slice(i * width, (i + 1) * width)
        w_in.append(pltpu.make_async_copy(w_hbm.at[:, pl.ds(start, width)], held.at[:, columns], w_sems.at[i]))
        w_out.append(pltpu.make_async_copy(held.at[:, columns], w_send.at[:, columns], w_sems.at[chunks + i]))
        w_in[i].start()
    leave = []
    for part in range(3):
        arrive[part].wait()
        source = inputs[part] if part < 2 else taps_in[...].astype(BF16)
        at = slice(part * group, (part + 1) * group)
        turned[:, at, :] = source.T.reshape(blocks, group, rows)
        leave.append(pltpu.make_async_copy(turned.at[:, at], out_hbm.at[:, at], sems.at[3 + part]))
        leave[part].start()
    for i in range(chunks):
        w_in[i].wait()
        w_out[i].start()
    for copy in leave + w_out:
        copy.wait()


def query_kernel(now_ref, before_ref, taps_ref, out_ref, whole):
    rows = out_ref.shape[0]
    halo = before_ref.shape[0]
    whole[:halo] = before_ref[...].astype(F32)
    whole[halo:] = now_ref[...].astype(F32)
    total = taps_ref[0, 0:1, :] * whole[halo:]
    for j in range(1, TAPS):
        total = total + taps_ref[0, j : j + 1, :] * whole[pl.ds(halo - j, rows), :]
    out_ref[...] = total


def featurize(recv_ref, taps_ref, gated):
    blocks, lines_all, width = recv_ref.shape
    group = lines_all // 3
    tile = 16
    batch = blocks
    lane = lax.broadcasted_iota(jnp.int32, (tile, LANES), 1)
    for c0 in range(0, group, tile):
        lines = slice(c0, c0 + tile)
        for part in (1, 2):
            t = [
                jnp.broadcast_to(taps_ref[lines, part * TAPS + j : part * TAPS + j + 1], (tile, LANES))
                for j in range(TAPS)
            ]
            last = [jnp.zeros((tile, LANES), F32)] * 4
            first_row = (part - 1) * group + c0
            for s0 in range(0, blocks, batch):
                places = [(s, lines, slice(l0, l0 + LANES)) for s in range(s0, s0 + batch) for l0 in range(0, width, LANES)]
                now = [recv_ref[s, first_row : first_row + tile, cols].astype(F32) for s, _, cols in places]
                gates = [gated[at] for at in places] if part == 2 else None

                def shifted(values, amount, which):
                    turns = [pltpu.roll(value, amount, 1) for value in values]
                    moved = [jnp.where(lane < amount, b, a) for b, a in zip([last[which]] + turns[:-1], turns)]
                    last[which] = turns[-1]
                    return moved

                one = shifted(now, 1, 0)
                two = shifted([t[2] * x + t[3] * y for x, y in zip(now, one)], 2, 1)
                four = shifted([t[4] * x + t[5] * y for x, y in zip(now, one)], 4, 2)
                six = shifted([t[6] * x for x in now], 6, 3)
                totals = [t[0] * x + t[1] * y + a + b + c for x, y, a, b, c in zip(now, one, two, four, six)]
                if part == 2:
                    totals = [g * total for g, total in zip(gates, totals)]
                for at, total in zip(places, totals):
                    gated[at] = total


def over_blocks(values, k, blocks):
    even_c = even_s = odd_c = odd_s = None
    for s, value in enumerate(values):
        c, t = math.cos(block_angle(s, k, blocks)), math.sin(block_angle(s, k, blocks))
        if s == 0:
            even_c = value
            continue
        term_c, term_s = value * c, value * t
        if s % 2 == 0:
            even_c = even_c + term_c
            even_s = term_s if even_s is None else even_s + term_s
        else:
            odd_c = term_c if odd_c is None else odd_c + term_c
            odd_s = term_s if odd_s is None else odd_s + term_s
    return (even_c + odd_c, -(even_s + odd_s)), (even_c - odd_c, even_s - odd_s)


def conv_kernel(
    recv_ref, taps_ref, tw_ref, tables_hbm, out_ref, gated, high, low, spec_h, spec_u, tables, sems
):
    blocks, lines_all, width = recv_ref.shape
    group = lines_all // 3
    tile = 16
    load = pltpu.make_async_copy(tables_hbm, tables, sems.at[0])
    load.start()
    featurize(recv_ref, taps_ref, gated)

    def table(which, term):
        start = (2 * which + term) * 2 * width
        return tables[start : start + 2 * width, :]

    def store_split(rows, cols, value):
        high[rows, cols], low[rows, cols] = split_bf16(value)

    def lanes(which):
        return dot(high[...], table(which, 0)) + dot(low[...], table(which, 0)) + dot(high[...], table(which, 1))

    def to_odd(block):
        for c0 in range(0, group, tile):
            for l0 in range(0, width, LANES):
                values = [block(s, c0, slice(l0, l0 + LANES)) for s in range(blocks)]
                for k in range(blocks // 2):
                    for kk, (re, im) in zip((k, blocks - 1 - k), over_blocks(values, k, blocks)):
                        tr = tw_ref[0, kk, :, l0 : l0 + LANES]
                        ti = tw_ref[1, kk, :, l0 : l0 + LANES]
                        rows = slice(kk * group + c0, kk * group + c0 + tile)
                        store_split(rows, slice(l0, l0 + LANES), re * tr - im * ti)
                        store_split(rows, slice(width + l0, width + l0 + LANES), re * ti + im * tr)

    to_odd(lambda s, c, p: recv_ref[s, 2 * group + c : 2 * group + c + tile, p].astype(F32))
    load.wait()
    spec_h[...] = lanes(0)
    to_odd(lambda s, c, p: gated[s, c : c + tile, p])
    spec_u[...] = lanes(0)

    hr, hi = spec_h[:, :width], spec_h[:, width:]
    ur, ui = spec_u[:, :width], spec_u[:, width:]
    store_split(slice(None), slice(0, width), hr * ur - hi * ui)
    store_split(slice(None), slice(width, 2 * width), hr * ui + hi * ur)
    spec_h[...] = lanes(1)

    scale = 1.0 / (blocks * width)
    half = blocks // 2
    for c0 in range(0, group, tile):
        skip = taps_ref[c0 : c0 + tile, 3 * TAPS : 3 * TAPS + 1]
        for l0 in range(0, width, LANES):
            reals, imags = [], []
            for k in range(blocks):
                rows = slice(k * group + c0, k * group + c0 + tile)
                tr = tw_ref[0, k, :, l0 : l0 + LANES] * scale
                ti = tw_ref[1, k, :, l0 : l0 + LANES] * scale
                re = spec_h[rows, l0 : l0 + LANES]
                im = spec_h[rows, width + l0 : width + l0 + LANES]
                reals.append(re * tr + im * ti)
                imags.append(im * tr - re * ti)
            sum_re = [reals[k] + reals[blocks - 1 - k] for k in range(half)]
            dif_re = [reals[k] - reals[blocks - 1 - k] for k in range(half)]
            sum_im = [imags[k] + imags[blocks - 1 - k] for k in range(half)]
            dif_im = [imags[k] - imags[blocks - 1 - k] for k in range(half)]
            for s in range(blocks):
                res, ims = (sum_re, dif_im) if s % 2 == 0 else (dif_re, sum_im)
                total = None
                for k in range(half):
                    angle = block_angle(s, k, blocks)
                    term = res[k] if s == 0 else res[k] * math.cos(angle) - ims[k] * math.sin(angle)
                    total = term if total is None else total + term
                at = (s, slice(c0, c0 + tile), slice(l0, l0 + LANES))
                out_ref[at] = (total + skip * gated[at]).astype(BF16)


def mix_kernel(conv_ref, query_ref, out_ref):
    rows, width = query_ref.shape
    turned = conv_ref[...].reshape(width, rows).T
    out_ref[...] = (query_ref[...] * turned.astype(F32)).astype(BF16)


def own_kernel(place_ref, mixed_ref, w_hbm, out_ref, own, sems):
    width = w_hbm.shape[0]
    index = place_ref[0] // 4
    order = list(reversed(range(own.shape[0])))
    copies = {}
    for step in order:
        start = column_start(place_ref, index ^ step, w_hbm)
        copies[step] = pltpu.make_async_copy(w_hbm.at[:, pl.ds(start, width)], own.at[step], sems.at[step])
        copies[step].start()
    for step in order:
        copies[step].wait()
        out_ref[step] = dot(mixed_ref[...], own[step])


def other_kernel(steps, place_ref, mixed_ref, own_ref, other_ref, *outs):
    width = other_ref.shape[0]
    index = place_ref[0] // 4
    for step, out in zip(steps, outs):
        start = pl.multiple_of((index ^ step) * width, width)
        out[...] = (own_ref[step] + dot(mixed_ref[...], other_ref[:, pl.ds(start, width)])).astype(out.dtype)


def sum_kernel(own_ref, *refs):
    total = own_ref[...]
    for ref in refs[:-1]:
        total = total + ref[...].astype(F32)
    refs[-1][...] = total.astype(BF16)


def local(projected, short_taps, long_filter, skip_gain, w_out):
    ctx, tp, dp = lax.axis_size("ctx"), lax.axis_size("tp"), lax.axis_size("dp")
    rows, width = projected.shape[1:]
    group = width // ctx
    me_ctx, me_tp, me_dp = lax.axis_index("ctx"), lax.axis_index("tp"), lax.axis_index("dp")

    chunks = tp // 2

    def quad_place(q, i):
        return 2 * i + (q + (2 * i >= tp // 2)) % 2

    def device(r, d):
        return (r + d) % tp * dp + d

    pair_route = [(device(r, d), device(r ^ 1, d)) for r in range(tp) for d in range(dp)]
    quads = [[device(quad_place(q, i), d) for i in range(chunks)] for d in range(dp) for q in range(2)]
    place = (lax.rem(me_tp - me_dp + tp, tp) * 2 + me_dp).astype(jnp.int32)[None]

    vmem = pl.BlockSpec(memory_space=pltpu.VMEM)
    smem = pl.BlockSpec(memory_space=pltpu.SMEM)
    hbm = pl.BlockSpec(memory_space=pl.ANY)
    params = pltpu.CompilerParams(vmem_limit_bytes=60 * MIB)

    send, w_send = pl.pallas_call(
        prep_kernel,
        in_specs=[smem, hbm, hbm, hbm],
        out_specs=[hbm, hbm],
        out_shape=[
            jax.ShapeDtypeStruct((ctx, 3 * group, rows), BF16),
            jax.ShapeDtypeStruct((width, chunks * width), BF16),
        ],
        scratch_shapes=[
            pltpu.VMEM((2, rows, width), BF16),
            pltpu.VMEM((rows, width), F32),
            pltpu.VMEM((ctx, 3 * group, rows), BF16),
            pltpu.VMEM((width, chunks * width), BF16),
            pltpu.SemaphoreType.DMA((6,)),
            pltpu.SemaphoreType.DMA((2 * chunks,)),
        ],
        compiler_params=params,
        name="prep",
    )(place, projected, long_filter, w_out)
    recv = lax.all_to_all(send, "ctx", 0, 0, tiled=True)
    w_other = lax.ppermute(w_send, ("tp", "dp"), pair_route)

    before = lax.ppermute(projected[0, rows - HALO :], "ctx", [(i, i + 1) for i in range(ctx - 1)])
    query = pl.pallas_call(
        query_kernel,
        in_specs=[vmem] * 3,
        out_specs=vmem,
        out_shape=jax.ShapeDtypeStruct((rows, width), F32),
        scratch_shapes=[pltpu.VMEM((HALO + rows, width), F32)],
        compiler_params=pltpu.CompilerParams(vmem_limit_bytes=48 * MIB),
        name="query",
    )(projected[0], before, short_taps)

    taps = jnp.concatenate([short_taps.reshape(3 * TAPS, width), skip_gain[None, :]], axis=0)
    taps = lax.dynamic_slice_in_dim(taps, me_ctx * group, group, axis=1).T
    taps, query = lax.optimization_barrier((taps, query))
    tables = lane_tables(rows)
    conv = pl.pallas_call(
        conv_kernel,
        in_specs=[vmem, vmem, vmem, hbm],
        out_specs=vmem,
        out_shape=jax.ShapeDtypeStruct((ctx, group, rows), BF16),
        scratch_shapes=[
            pltpu.VMEM((ctx, group, rows), F32),
            pltpu.VMEM((ctx * group, 2 * rows), BF16),
            pltpu.VMEM((ctx * group, 2 * rows), BF16),
            pltpu.VMEM((ctx * group, 2 * rows), F32),
            pltpu.VMEM((ctx * group, 2 * rows), F32),
            pltpu.VMEM(tables.shape, BF16),
            pltpu.SemaphoreType.DMA((1,)),
        ],
        compiler_params=pltpu.CompilerParams(vmem_limit_bytes=52 * MIB),
        name="conv",
    )(recv, taps, jnp.asarray(twiddles(ctx, rows)), jnp.asarray(tables))
    conv = lax.all_to_all(conv, "ctx", 0, 0, tiled=True)

    small = pltpu.CompilerParams(vmem_limit_bytes=48 * MIB)
    block = jax.ShapeDtypeStruct((rows, width), BF16)
    mixed = pl.pallas_call(
        mix_kernel, in_specs=[vmem, vmem], out_specs=vmem, out_shape=block, compiler_params=small, name="mix"
    )(conv, query)
    mixed_other = lax.ppermute(mixed, ("tp", "dp"), pair_route)
    own_sums = pl.pallas_call(
        own_kernel,
        in_specs=[smem, vmem, hbm],
        out_specs=vmem,
        out_shape=jax.ShapeDtypeStruct((chunks, rows, width), F32),
        scratch_shapes=[pltpu.VMEM((chunks, width, width), BF16), pltpu.SemaphoreType.DMA((chunks,))],
        compiler_params=small,
        name="own",
    )(place, mixed, w_out)

    def project(steps, kind):
        return pl.pallas_call(
            functools.partial(other_kernel, steps),
            in_specs=[smem, vmem, vmem, vmem],
            out_specs=[vmem] * len(steps),
            out_shape=[jax.ShapeDtypeStruct((rows, width), kind)] * len(steps),
            compiler_params=small,
            name="other",
        )(place, mixed_other, own_sums, w_other)

    def passed(block, step):
        return lax.ppermute(block, ("tp", "dp"), [(quad[i], quad[i ^ step]) for quad in quads for i in range(chunks)])

    parts = [passed(block, step) for step, block in zip((3,), project((3,), BF16))]
    parts += [passed(block, step) for step, block in zip((1, 2), project((1, 2), BF16))]
    (own,) = project((0,), F32)
    return pl.pallas_call(
        sum_kernel,
        in_specs=[vmem] * 4,
        out_shape=jax.ShapeDtypeStruct((rows, width), BF16),
        compiler_params=pltpu.CompilerParams(vmem_limit_bytes=48 * MIB),
        name="sum",
    )(own, *parts)


def solution(mesh):
    in_specs = (
        P(None, ("dp", "ctx"), "tp"),
        P(None, None, "tp"),
        P("ctx", "tp"),
        P("tp"),
        P("tp", None),
    )
    out_specs = P(("dp", "ctx"), "tp")
    return jax.shard_map(local, mesh=mesh, in_specs=in_specs, out_specs=out_specs, check_vma=False)
```

```python
import functools
import math

import jax
import jax.numpy as jnp
import numpy as np
from jax import lax
from jax.experimental import pallas as pl
from jax.experimental.pallas import tpu as pltpu
from jax.sharding import PartitionSpec as P

TAPS = 7
LANES = 128
HALO = 16
BF16 = jnp.bfloat16
F32 = jnp.float32
MIB = 1024 * 1024


def split_table(table):
    high = table.astype(np.float32).astype(jnp.bfloat16)
    low = (table - high.astype(np.float64)).astype(np.float32).astype(jnp.bfloat16)
    return np.stack([high, low])


def lane_tables(width):
    angle = 2.0 * np.pi * (np.outer(np.arange(width), np.arange(width)) % width) / width
    cos, sin = np.cos(angle), np.sin(angle)
    forward = np.block([[cos, -sin], [sin, cos]])
    return np.concatenate([split_table(table).reshape(-1, 2 * width) for table in (forward, forward.T)])


def twiddles(blocks, width):
    angle = 2.0 * np.pi * np.outer(np.arange(blocks) + 0.5, np.arange(width)) / (2 * blocks * width)
    return np.stack([np.cos(angle), -np.sin(angle)]).astype(np.float32)[:, :, None, :]


def block_angle(s, k, blocks):
    return math.pi * ((s * (2 * k + 1)) % (4 * blocks)) / (2 * blocks)


def split_bf16(values):
    high = values.astype(BF16)
    return high, (values - high.astype(F32)).astype(BF16)


def dot(a, b):
    return jnp.dot(a, b, preferred_element_type=F32)


def column_start(place_ref, i, w_hbm, other=False):
    width = w_hbm.shape[0]
    chunks = w_hbm.shape[1] // width
    core, ring = lax.rem(place_ref[0], 2), place_ref[0] // 2
    mine = ring // 2
    side = (lax.rem(ring, 2) + (2 * mine >= chunks // 2).astype(jnp.int32) + int(other)) % 2
    upper = (2 * jnp.asarray(i, jnp.int32) >= chunks // 2).astype(jnp.int32)
    return pl.multiple_of(lax.rem(2 * i + lax.rem(side + upper, 2) + core, chunks) * width, width)


def prep_kernel(place_ref, projected_hbm, filter_hbm, w_hbm, out_hbm, w_send, inputs, taps_in, turned, held, sems, w_sems):
    blocks, lines, rows = turned.shape
    group = lines // 3
    width = w_hbm.shape[0]
    chunks = w_send.shape[1] // width
    arrive = [pltpu.make_async_copy(projected_hbm.at[1 + part], inputs.at[part], sems.at[part]) for part in range(2)]
    arrive.append(pltpu.make_async_copy(filter_hbm, taps_in, sems.at[2]))
    for copy in arrive:
        copy.start()
    w_in, w_out = [], []
    for i in range(chunks):
        start = column_start(place_ref, i, w_hbm, other=True)
        columns = slice(i * width, (i + 1) * width)
        w_in.append(pltpu.make_async_copy(w_hbm.at[:, pl.ds(start, width)], held.at[:, columns], w_sems.at[i]))
        w_out.append(pltpu.make_async_copy(held.at[:, columns], w_send.at[:, columns], w_sems.at[chunks + i]))
        w_in[i].start()
    leave = []
    for part in range(3):
        arrive[part].wait()
        source = inputs[part] if part < 2 else taps_in[...].astype(BF16)
        at = slice(part * group, (part + 1) * group)
        turned[:, at, :] = source.T.reshape(blocks, group, rows)
        leave.append(pltpu.make_async_copy(turned.at[:, at], out_hbm.at[:, at], sems.at[3 + part]))
        leave[part].start()
    for i in range(chunks):
        w_in[i].wait()
        w_out[i].start()
    for copy in leave + w_out:
        copy.wait()


def query_kernel(now_ref, before_ref, taps_ref, out_ref, whole):
    rows = out_ref.shape[0]
    halo = before_ref.shape[0]
    whole[:halo] = before_ref[...].astype(F32)
    whole[halo:] = now_ref[...].astype(F32)
    total = taps_ref[0, 0:1, :] * whole[halo:]
    for j in range(1, TAPS):
        total = total + taps_ref[0, j : j + 1, :] * whole[pl.ds(halo - j, rows), :]
    out_ref[...] = total


def featurize(recv_ref, taps_ref, gated):
    blocks, lines_all, width = recv_ref.shape
    group = lines_all // 3
    tile = 16
    batch = blocks
    lane = lax.broadcasted_iota(jnp.int32, (tile, LANES), 1)
    for c0 in range(0, group, tile):
        lines = slice(c0, c0 + tile)
        for part in (1, 2):
            t = [
                jnp.broadcast_to(taps_ref[lines, part * TAPS + j : part * TAPS + j + 1], (tile, LANES))
                for j in range(TAPS)
            ]
            last = [jnp.zeros((tile, LANES), F32)] * 4
            first_row = (part - 1) * group + c0
            for s0 in range(0, blocks, batch):
                places = [(s, lines, slice(l0, l0 + LANES)) for s in range(s0, s0 + batch) for l0 in range(0, width, LANES)]
                now = [recv_ref[s, first_row : first_row + tile, cols].astype(F32) for s, _, cols in places]
                gates = [gated[at] for at in places] if part == 2 else None

                def shifted(values, amount, which):
                    turns = [pltpu.roll(value, amount, 1) for value in values]
                    moved = [jnp.where(lane < amount, b, a) for b, a in zip([last[which]] + turns[:-1], turns)]
                    last[which] = turns[-1]
                    return moved

                one = shifted(now, 1, 0)
                two = shifted([t[2] * x + t[3] * y for x, y in zip(now, one)], 2, 1)
                four = shifted([t[4] * x + t[5] * y for x, y in zip(now, one)], 4, 2)
                six = shifted([t[6] * x for x in now], 6, 3)
                totals = [t[0] * x + t[1] * y + a + b + c for x, y, a, b, c in zip(now, one, two, four, six)]
                if part == 2:
                    totals = [g * total for g, total in zip(gates, totals)]
                for at, total in zip(places, totals):
                    gated[at] = total


def over_blocks(values, k, blocks):
    even_c = even_s = odd_c = odd_s = None
    for s, value in enumerate(values):
        c, t = math.cos(block_angle(s, k, blocks)), math.sin(block_angle(s, k, blocks))
        if s == 0:
            even_c = value
            continue
        term_c, term_s = value * c, value * t
        if s % 2 == 0:
            even_c = even_c + term_c
            even_s = term_s if even_s is None else even_s + term_s
        else:
            odd_c = term_c if odd_c is None else odd_c + term_c
            odd_s = term_s if odd_s is None else odd_s + term_s
    return (even_c + odd_c, -(even_s + odd_s)), (even_c - odd_c, even_s - odd_s)


def conv_kernel(
    recv_ref, taps_ref, tw_ref, tables_hbm, out_ref, gated, high, low, spec_h, spec_u, tables, sems
):
    blocks, lines_all, width = recv_ref.shape
    group = lines_all // 3
    tile = 16
    load = pltpu.make_async_copy(tables_hbm, tables, sems.at[0])
    load.start()
    featurize(recv_ref, taps_ref, gated)

    def table(which, term):
        start = (2 * which + term) * 2 * width
        return tables[start : start + 2 * width, :]

    def store_split(rows, cols, value):
        high[rows, cols], low[rows, cols] = split_bf16(value)

    def lanes(which):
        return dot(high[...], table(which, 0)) + dot(low[...], table(which, 0)) + dot(high[...], table(which, 1))

    def to_odd(block):
        for c0 in range(0, group, tile):
            for l0 in range(0, width, LANES):
                values = [block(s, c0, slice(l0, l0 + LANES)) for s in range(blocks)]
                for k in range(blocks // 2):
                    for kk, (re, im) in zip((k, blocks - 1 - k), over_blocks(values, k, blocks)):
                        tr = tw_ref[0, kk, :, l0 : l0 + LANES]
                        ti = tw_ref[1, kk, :, l0 : l0 + LANES]
                        rows = slice(kk * group + c0, kk * group + c0 + tile)
                        store_split(rows, slice(l0, l0 + LANES), re * tr - im * ti)
                        store_split(rows, slice(width + l0, width + l0 + LANES), re * ti + im * tr)

    to_odd(lambda s, c, p: recv_ref[s, 2 * group + c : 2 * group + c + tile, p].astype(F32))
    load.wait()
    spec_h[...] = lanes(0)
    to_odd(lambda s, c, p: gated[s, c : c + tile, p])
    spec_u[...] = lanes(0)

    hr, hi = spec_h[:, :width], spec_h[:, width:]
    ur, ui = spec_u[:, :width], spec_u[:, width:]
    store_split(slice(None), slice(0, width), hr * ur - hi * ui)
    store_split(slice(None), slice(width, 2 * width), hr * ui + hi * ur)
    spec_h[...] = lanes(1)

    scale = 1.0 / (blocks * width)
    half = blocks // 2
    for c0 in range(0, group, tile):
        skip = taps_ref[c0 : c0 + tile, 3 * TAPS : 3 * TAPS + 1]
        for l0 in range(0, width, LANES):
            reals, imags = [], []
            for k in range(blocks):
                rows = slice(k * group + c0, k * group + c0 + tile)
                tr = tw_ref[0, k, :, l0 : l0 + LANES] * scale
                ti = tw_ref[1, k, :, l0 : l0 + LANES] * scale
                re = spec_h[rows, l0 : l0 + LANES]
                im = spec_h[rows, width + l0 : width + l0 + LANES]
                reals.append(re * tr + im * ti)
                imags.append(im * tr - re * ti)
            sum_re = [reals[k] + reals[blocks - 1 - k] for k in range(half)]
            dif_re = [reals[k] - reals[blocks - 1 - k] for k in range(half)]
            sum_im = [imags[k] + imags[blocks - 1 - k] for k in range(half)]
            dif_im = [imags[k] - imags[blocks - 1 - k] for k in range(half)]
            for s in range(blocks):
                res, ims = (sum_re, dif_im) if s % 2 == 0 else (dif_re, sum_im)
                total = None
                for k in range(half):
                    angle = block_angle(s, k, blocks)
                    term = res[k] if s == 0 else res[k] * math.cos(angle) - ims[k] * math.sin(angle)
                    total = term if total is None else total + term
                at = (s, slice(c0, c0 + tile), slice(l0, l0 + LANES))
                out_ref[at] = (total + skip * gated[at]).astype(BF16)


def mix_kernel(conv_ref, query_ref, out_ref):
    rows, width = query_ref.shape
    turned = conv_ref[...].reshape(width, rows).T
    out_ref[...] = (query_ref[...] * turned.astype(F32)).astype(BF16)


def own_kernel(place_ref, mixed_ref, w_hbm, out_ref, own, sems):
    width = w_hbm.shape[0]
    index = place_ref[0] // 4
    order = list(reversed(range(own.shape[0])))
    copies = {}
    for step in order:
        start = column_start(place_ref, index ^ step, w_hbm)
        copies[step] = pltpu.make_async_copy(w_hbm.at[:, pl.ds(start, width)], own.at[step], sems.at[step])
        copies[step].start()
    for step in order:
        copies[step].wait()
        out_ref[step] = dot(mixed_ref[...], own[step])


def other_kernel(steps, place_ref, mixed_ref, own_ref, other_ref, *outs):
    width = other_ref.shape[0]
    index = place_ref[0] // 4
    for step, out in zip(steps, outs):
        start = pl.multiple_of((index ^ step) * width, width)
        out[...] = (own_ref[step] + dot(mixed_ref[...], other_ref[:, pl.ds(start, width)])).astype(out.dtype)


def sum_kernel(own_ref, *refs):
    total = own_ref[...]
    for ref in refs[:-1]:
        total = total + ref[...].astype(F32)
    refs[-1][...] = total.astype(BF16)


def local(projected, short_taps, long_filter, skip_gain, w_out):
    ctx, tp, dp = lax.axis_size("ctx"), lax.axis_size("tp"), lax.axis_size("dp")
    rows, width = projected.shape[1:]
    group = width // ctx
    me_ctx, me_tp, me_dp = lax.axis_index("ctx"), lax.axis_index("tp"), lax.axis_index("dp")

    chunks = tp // 2

    def quad_place(q, i):
        return 2 * i + (q + (2 * i >= tp // 2)) % 2

    def device(r, d):
        return (r + d) % tp * dp + d

    pair_route = [(device(r, d), device(r ^ 1, d)) for r in range(tp) for d in range(dp)]
    quads = [[device(quad_place(q, i), d) for i in range(chunks)] for d in range(dp) for q in range(2)]
    place = (lax.rem(me_tp - me_dp + tp, tp) * 2 + me_dp).astype(jnp.int32)[None]

    vmem = pl.BlockSpec(memory_space=pltpu.VMEM)
    smem = pl.BlockSpec(memory_space=pltpu.SMEM)
    hbm = pl.BlockSpec(memory_space=pl.ANY)
    params = pltpu.CompilerParams(vmem_limit_bytes=60 * MIB)

    send, w_send = pl.pallas_call(
        prep_kernel,
        in_specs=[smem, hbm, hbm, hbm],
        out_specs=[hbm, hbm],
        out_shape=[
            jax.ShapeDtypeStruct((ctx, 3 * group, rows), BF16),
            jax.ShapeDtypeStruct((width, chunks * width), BF16),
        ],
        scratch_shapes=[
            pltpu.VMEM((2, rows, width), BF16),
            pltpu.VMEM((rows, width), F32),
            pltpu.VMEM((ctx, 3 * group, rows), BF16),
            pltpu.VMEM((width, chunks * width), BF16),
            pltpu.SemaphoreType.DMA((6,)),
            pltpu.SemaphoreType.DMA((2 * chunks,)),
        ],
        compiler_params=params,
        name="prep",
    )(place, projected, long_filter, w_out)
    recv = lax.all_to_all(send, "ctx", 0, 0, tiled=True)
    w_other = lax.ppermute(w_send, ("tp", "dp"), pair_route)

    before = lax.ppermute(projected[0, rows - HALO :], "ctx", [(i, i + 1) for i in range(ctx - 1)])
    query = pl.pallas_call(
        query_kernel,
        in_specs=[vmem] * 3,
        out_specs=vmem,
        out_shape=jax.ShapeDtypeStruct((rows, width), F32),
        scratch_shapes=[pltpu.VMEM((HALO + rows, width), F32)],
        compiler_params=pltpu.CompilerParams(vmem_limit_bytes=48 * MIB),
        name="query",
    )(projected[0], before, short_taps)

    taps = jnp.concatenate([short_taps.reshape(3 * TAPS, width), skip_gain[None, :]], axis=0)
    taps = lax.dynamic_slice_in_dim(taps, me_ctx * group, group, axis=1).T
    taps, query = lax.optimization_barrier((taps, query))
    tables = lane_tables(rows)
    conv = pl.pallas_call(
        conv_kernel,
        in_specs=[vmem, vmem, vmem, hbm],
        out_specs=vmem,
        out_shape=jax.ShapeDtypeStruct((ctx, group, rows), BF16),
        scratch_shapes=[
            pltpu.VMEM((ctx, group, rows), F32),
            pltpu.VMEM((ctx * group, 2 * rows), BF16),
            pltpu.VMEM((ctx * group, 2 * rows), BF16),
            pltpu.VMEM((ctx * group, 2 * rows), F32),
            pltpu.VMEM((ctx * group, 2 * rows), F32),
            pltpu.VMEM(tables.shape, BF16),
            pltpu.SemaphoreType.DMA((1,)),
        ],
        compiler_params=pltpu.CompilerParams(vmem_limit_bytes=52 * MIB),
        name="conv",
    )(recv, taps, jnp.asarray(twiddles(ctx, rows)), jnp.asarray(tables))
    conv = lax.all_to_all(conv, "ctx", 0, 0, tiled=True)

    small = pltpu.CompilerParams(vmem_limit_bytes=48 * MIB)
    block = jax.ShapeDtypeStruct((rows, width), BF16)
    mixed = pl.pallas_call(
        mix_kernel, in_specs=[vmem, vmem], out_specs=vmem, out_shape=block, compiler_params=small, name="mix"
    )(conv, query)
    mixed_other = lax.ppermute(mixed, ("tp", "dp"), pair_route)
    own_sums = pl.pallas_call(
        own_kernel,
        in_specs=[smem, vmem, hbm],
        out_specs=vmem,
        out_shape=jax.ShapeDtypeStruct((chunks, rows, width), F32),
        scratch_shapes=[pltpu.VMEM((chunks, width, width), BF16), pltpu.SemaphoreType.DMA((chunks,))],
        compiler_params=small,
        name="own",
    )(place, mixed, w_out)

    def project(steps, kind):
        return pl.pallas_call(
            functools.partial(other_kernel, steps),
            in_specs=[smem, vmem, vmem, vmem],
            out_specs=[vmem] * len(steps),
            out_shape=[jax.ShapeDtypeStruct((rows, width), kind)] * len(steps),
            compiler_params=small,
            name="other",
        )(place, mixed_other, own_sums, w_other)

    def passed(block, step):
        return lax.ppermute(block, ("tp", "dp"), [(quad[i], quad[i ^ step]) for quad in quads for i in range(chunks)])

    parts = [passed(block, step) for step, block in zip((3, 1, 2), project((3, 1, 2), BF16))]
    (own,) = project((0,), F32)
    return pl.pallas_call(
        sum_kernel,
        in_specs=[vmem] * 4,
        out_shape=jax.ShapeDtypeStruct((rows, width), BF16),
        compiler_params=pltpu.CompilerParams(vmem_limit_bytes=48 * MIB),
        name="sum",
    )(own, *parts)


def solution(mesh):
    in_specs = (
        P(None, ("dp", "ctx"), "tp"),
        P(None, None, "tp"),
        P("ctx", "tp"),
        P("tp"),
        P("tp", None),
    )
    out_specs = P(("dp", "ctx"), "tp")
    return jax.shard_map(local, mesh=mesh, in_specs=in_specs, out_specs=out_specs, check_vma=False)
```
